32 devices in a mesh: tm: 2 (over core), space: 16 (over z, y, x).
Axes of the slice: x: 2, y: 2, z: 4, core: 2. Of those that a mesh axis runs over, the one named last changes fastest.
Arguments:
- start_states: float32 [2, 3, 128, 4096], P('tm', None, 'space'), may hold values from -6 to 6
- coarse_gain: float32 [3, 128, 4096], P(None, 'space'), may hold values from 0.55 to 0.95
- depth_level: int32 [128, 4096], P('space'), may hold values from 0 to 63
- depth_table: float32 [64], replicated, may hold values from 0.2 to 1
- wet: int32 [128, 4096], P('space'), may hold values 0 or 1
- block_count: int32 [16], P('space'), may hold values from 1 to 8, 80 in all
- neighbour: int32 [128, 4], P('space'), may hold values from -1 to 7
- coriolis: float32 [128, 4096], P('space'), may hold values from -0.5 to 0.5
- tide: float32 [2, 128, 4096], P(None, 'space'), may hold values from -2 to 2
Outputs:
- new_states: float32 [2, 3, 128, 4096], P('tm', None, 'space')
The draws below stay inside these ranges and needn't reach their ends.
Inputs may be any that keep to these rules, and one draw needn't show every extreme that they name: `block_count`: each column's count is the number of its first slots that hold ocean blocks; some column holds 8. `neighbour`: entries 0 and 1 name slots of the same column, entries 2 and 3 slots of the next and the previous column along the periodic longitude; -1 is a closed face.
All inputs are finite; a program needn't handle non-finite values. No bound on the sum of `wet` on one device may be relied on, other than what follows from the above.
Results may differ from the reference program's by a relative error of at most 0.00007.
Values sent between devices are 32-bit elements; how exact they have to be, the bound alone decides.
No kernel may reach another device: no remote copies, remote signals or barrier semaphores. Data moves between devices by JAX's collectives and lax.ppermute only.
A program may use at most 64 MiB of HBM per device.

```python
import math
import jax
import jax.numpy as jnp
import numpy as np

BS = 64
CELLS = 4096
NB = 8
STEPS = 6
LEVELS = 64
SLICES = 2
SLOTS = 128
N_SPACE = 16


def with_ends(values, stream_key, least, top_value):
    shape = values.shape
    index_at = [jax.random.randint(jax.random.fold_in(stream_key, axis), (), 0, shape[axis]) for axis in range(len(shape))]
    values = values.at[tuple(index_at)].set(least)
    longest = shape.index(max(shape))
    index_at[longest] = (index_at[longest] + 1) % shape[longest]
    return values.at[tuple(index_at)].set(top_value)


def steps_of(rng, dims, cuts, least, high):
    gain = 1.0
    for position, shards_of in cuts:
        heights = jax.random.uniform(jax.random.fold_in(jax.random.fold_in(rng, 6), position), (shards_of,), jnp.float32, least / len(cuts), high / len(cuts))
        gain = gain * jnp.repeat(jnp.exp(heights), dims[position] // shards_of).reshape((-1,) + (1,) * (len(dims) - 1 - position))
    return gain


def length_profile(amount, total, limit, lean):
    loads = [(1 << 20) // math.isqrt(rank ** lean) + 1 for rank in range(2, amount + 1)]
    surplus, counts = total - limit - (amount - 1), [1] * (amount - 1)
    while surplus > 0:
        candidates = [i for i in range(amount - 1) if counts[i] < limit]
        whole, budget = sum([loads[i] for i in candidates]), surplus
        for i in candidates:
            extra = min(limit - counts[i], max(1, budget * loads[i] // whole), surplus)
            counts[i] = counts[i] + extra
            surplus = surplus - extra
    return np.array([limit] + counts)


def uneven_parts(key, count, total, limit, slope):
    if count == 2:
        one = jax.random.randint(key, (), max(1, total - limit), min(limit, total - 1) + 1)
        return jnp.stack([one, total - one])
    tallies = jnp.asarray(length_profile(count, total, limit, slope), jnp.int32)
    pairs = (count - 1) // 2
    source_of, taker = tallies[1:1 + 2 * pairs:2], tallies[2:2 + 2 * pairs:2]
    margin = jnp.minimum(source_of - 1, limit - taker)
    shifted = jax.random.randint(jax.random.fold_in(key, 1), (pairs,), 0, 1 << 20) % (margin + 1)
    tallies = tallies.at[1:1 + 2 * pairs:2].set(source_of - shifted).at[2:2 + 2 * pairs:2].set(taker + shifted)
    return tallies[jax.random.permutation(jax.random.fold_in(key, 2), count)]


def scatter_about(own_key, dims, spread, limit, shards=(), kind=jnp.bfloat16):
    values = jax.random.normal(own_key, dims, jnp.float32) * spread
    if len(shards) > 0:
        values = steps_of(own_key, dims, shards, -0.22, 0.18) * values
    return jnp.clip(values, min=-limit, max=limit).astype(kind)


def setup_inputs(seed: int = 0) -> dict:
    key_of = jax.random.split(jax.random.key(seed), 10)
    return {
        "start_states": scatter_about(key_of[0], (SLICES, 3, SLOTS, CELLS), 1.0, 6.0, ((0, 2), (2, 16)), jnp.float32),
        "coarse_gain": jnp.clip(jnp.exp(math.log(0.95) - 0.54654367 * jax.random.uniform(key_of[1], (3, SLOTS, CELLS), jnp.float32) ** steps_of(key_of[1], (3, SLOTS, CELLS), ((1, 16),), -0.2, 0.2)), 0.55, 0.95),
        "depth_level": with_ends(jax.random.randint(key_of[2], (SLOTS, CELLS), 0, LEVELS), jax.random.fold_in(key_of[2], 1), 0, LEVELS - 1).astype(jnp.int32),
        "depth_table": jnp.clip(jnp.exp(jax.random.uniform(key_of[3], (LEVELS,), jnp.float32, math.log(0.2), math.log(1.0))), 0.2, 1.0),
        "wet": with_ends((jax.random.randint(key_of[4], (SLOTS, CELLS), 0, 8) < 7).astype(jnp.int32), jax.random.fold_in(key_of[4], 1), 0, 1),
        "block_count": uneven_parts(key_of[5], N_SPACE, N_SPACE * NB * 5 // 8, NB, 1).astype(jnp.int32),
        "neighbour": with_ends(jax.random.randint(key_of[6], (SLOTS, 4), -1, NB), jax.random.fold_in(key_of[6], 1), -1, NB - 1).astype(jnp.int32),
        "coriolis": jnp.clip(jax.random.uniform(key_of[7], (SLOTS, CELLS), jnp.float32, -0.5, 0.5) * steps_of(key_of[7], (SLOTS, CELLS), ((0, 16),), -0.4, 0.0), -0.5, 0.5),
        "tide": scatter_about(key_of[8], (2, SLOTS, CELLS), 0.3, 2.0, ((1, 16),), jnp.float32),
    }


def take_edges(edges, index):
    valid = (index >= 0).astype(edges.dtype)
    return jnp.take(edges, jnp.maximum(index, 0).astype(jnp.int32), axis=0) * valid[:, None]


def across(field, west_ghost, east_ghost):
    column = jnp.arange(field.shape[-1]) % BS
    zero = jnp.zeros(field.shape[:-1] + (1,), field.dtype)
    east = jnp.where(column == BS - 1, jnp.repeat(east_ghost, BS, axis=-1), jnp.concatenate([field[:, 1:], zero], -1))
    west = jnp.where(column == 0, jnp.repeat(west_ghost, BS, axis=-1), jnp.concatenate([zero, field[:, :-1]], -1))
    return 0.5 * (east - west)


def along(field, north_ghost, south_ghost):
    north = jnp.concatenate([field[:, BS:], north_ghost], -1)
    south = jnp.concatenate([south_ghost, field[:, :-BS]], -1)
    return 0.5 * (north - south)


def reference(start_states, coarse_gain, depth_level, depth_table, wet, block_count, neighbour, coriolis, tide):
    slot = jnp.arange(SLOTS).astype(jnp.int32)
    column = slot // NB
    count = jnp.repeat(block_count, NB)
    live = wet.astype(jnp.float32) * ((slot % NB) < count).astype(jnp.float32)[:, None]
    depth = jnp.take(depth_table, depth_level)

    def global_id(entry, col):
        return jnp.where(entry >= 0, col * NB + entry, -1).astype(jnp.int32)

    north_id = global_id(neighbour[:, 0], column)
    south_id = global_id(neighbour[:, 1], column)
    east_id = global_id(neighbour[:, 2], (column + 1) % N_SPACE)
    west_id = global_id(neighbour[:, 3], (column + N_SPACE - 1) % N_SPACE)

    def grad_x(field):
        return across(field, take_edges(field[:, BS - 1::BS], west_id), take_edges(field[:, 0::BS], east_id))

    def grad_y(field):
        return along(field, take_edges(field[:, :BS], north_id), take_edges(field[:, -BS:], south_id))

    start = start_states * live
    omega = 2.0 * math.pi / (SLICES * STEPS)
    fine = []
    for index in range(SLICES):
        level, east_vel, north_vel = start[index, 0], start[index, 1], start[index, 2]
        for step in range(STEPS):
            angle = jnp.float32((index * STEPS + step) * omega)
            source = tide[0] * jnp.cos(angle) + tide[1] * jnp.sin(angle)
            div = grad_x(depth * east_vel) + grad_y(depth * north_vel)
            level = (level + 0.3 * (source - div)) * live
            new_east = (east_vel + 0.3 * (coriolis * north_vel - grad_x(level) - 0.05 * east_vel)) * live
            north_vel = (north_vel + 0.3 * (-coriolis * east_vel - grad_y(level) - 0.05 * north_vel)) * live
            east_vel = new_east
        fine.append(jnp.stack([level, east_vel, north_vel]))
    defect = jnp.stack(fine) - coarse_gain * start
    total = jnp.zeros_like(defect)
    for lag in range(1, SLICES + 1):
        total = total + coarse_gain ** (lag - 1) * jnp.roll(defect, lag, axis=0)
    return total / (1.0 - coarse_gain ** SLICES)
```

```python
import functools
import math

import jax
import jax.numpy as jnp
from jax import lax
from jax.experimental import pallas as pl
from jax.experimental.pallas import tpu as pltpu
from jax.sharding import PartitionSpec as P

BS = 64
STEPS = 6
HALF = 2 * STEPS
SENT = STEPS // 2
OUT = STEPS
LANES = 128
USED = 8 * OUT
F32 = jnp.float32
VMEM_LIMIT = 24 * 1024 * 1024


def roll(x, by):
    by = by % LANES
    return x if by == 0 else pltpu.roll(x, by, 1)


def take(x, index):
    return jnp.take_along_axis(x, index, axis=0)


def lane_ids():
    lane = lax.broadcasted_iota(jnp.int32, (8, LANES), 1)
    return lane, lane % BS


def spread(column):
    return jnp.broadcast_to(column, (8, LANES))


def ghost_index(entry):
    return jnp.maximum(entry, 0), (entry >= 0).astype(F32)


class Field:
    def __init__(self, ref, lead=()):
        self.ref, self.lead = ref, tuple(lead)

    def __getitem__(self, v):
        return self.ref[self.lead + (slice(None), pl.ds(v * LANES, LANES))]

    def __setitem__(self, v, value):
        self.ref[self.lead + (slice(None), pl.ds(v * LANES, LANES))] = value


def phase(count, step):
    omega = 2.0 * math.pi / (count * STEPS)
    here = lax.axis_index("tm")
    ca, sa = F32(0), F32(0)
    for n in range(count):
        for j in range(STEPS):
            hit = jnp.logical_and(here == n, step == j)
            angle = (n * STEPS + j) * omega
            ca = jnp.where(hit, F32(0.3 * math.cos(angle)), ca)
            sa = jnp.where(hit, F32(0.3 * math.sin(angle)), sa)
    return ca, sa


def along(tile, count, lower, north, south):
    first, last = roll(tile(0), BS), roll(tile(count - 1), BS)
    (north_at, north_on), (south_at, south_on) = north, south
    before, here = take(last, south_at) * south_on, first
    for v in range(count):
        if v == count - 1:
            after = take(first, north_at) * north_on
        elif v == count - 2:
            after = last
        else:
            after = roll(tile(v + 1), BS)
        yield jnp.where(lower, here, after) - jnp.where(lower, before, here)
        before, here = here, after


def across_open(x):
    return roll(x, -1) - roll(x, 1)


def level_half(s, count, ca, sa, update, lower, north, south, across):
    depth, level, east, northv = s["depth"], s["level"], s["east"], s["north"]
    slope = along(lambda v: depth[v] * northv[v], count, lower, north, south)
    for v, dy in enumerate(slope):
        div = across(depth[v] * east[v]) + dy
        old = level[v]
        new = (old + (s["tide0"][v] * ca + s["tide1"][v] * sa) - div) * s["live"][v]
        level[v] = jnp.where(update, new, old)


def velocity_half(s, count, update, lower, north, south, across):
    level = s["level"]
    slope = along(lambda v: level[v], count, lower, north, south)
    for v, dy in enumerate(slope):
        dx = across(level[v])
        u, w = s["east"][v], s["north"][v]
        cor, live = s["cor"](v), s["live"][v]
        new_u = (F32(0.985) * u + cor * w - F32(0.15) * dx) * live
        new_w = (F32(0.985) * w - cor * u - F32(0.15) * dy) * live
        s["east"][v] = jnp.where(update, new_u, u)
        s["north"][v] = jnp.where(update, new_w, w)


def own_ghosts(nb_ref):
    nb = nb_ref[...]
    return ghost_index(spread(nb[:, 0:1])), ghost_index(spread(nb[:, 1:2]))


def interior_steps(s, count, slices, steps, nb_ref):
    lane, cell = lane_ids()
    lower = lane < BS
    edge = jnp.minimum(cell, BS - 1 - cell) + 1
    north, south = own_ghosts(nb_ref)
    for step in steps:
        ca, sa = phase(slices, step)
        level_half(s, count, ca, sa, edge > 2 * step + 1, lower, north, south, across_open)
        velocity_half(s, count, edge > 2 * step + 2, lower, north, south, across_open)


def window(cell, f):
    return jnp.logical_and(cell >= OUT * f, cell < OUT * f + OUT)


def before_kernel(
    slices, start, level_id, table, wet, count_ref, nb_ref, cor, tide,
    state, depth_out, live_out, pe, pw,
):
    tiles = wet.shape[1] // LANES
    lane, cell = lane_ids()
    slot = lax.broadcasted_iota(jnp.int32, (8, LANES), 0)
    held = (slot < count_ref[0]).astype(F32)
    row = F32(0.15) * table[...].reshape(1, table.shape[0])
    row = jnp.broadcast_to(jnp.concatenate([row] * (LANES // row.shape[1]), axis=1), (8, LANES))
    depth, live = Field(depth_out), Field(live_out)
    fields = [Field(state, (i,)) for i in range(3)]
    ids, land = Field(level_id), Field(wet)
    for v in range(tiles):
        depth[v] = jnp.take_along_axis(row, ids[v], axis=1)
        live[v] = land[v].astype(F32) * held
        for i in range(3):
            fields[i][v] = Field(start, (0, i))[v] * live[v]
    cor_f = Field(cor)
    s = dict(
        depth=depth, live=live, level=fields[0], east=fields[1], north=fields[2],
        tide0=Field(tide, (0,)), tide1=Field(tide, (1,)), cor=lambda v: F32(0.3) * cor_f[v],
    )
    interior_steps(s, tiles, slices, range(SENT), nb_ref)

    nb = nb_ref[...].astype(F32)
    masks = [window(cell, f) for f in range(8)]

    def packed(v, going_east):
        items = [
            s["level"][v], s["east"][v], s["north"][v], depth[v], live[v],
            s["cor"](v), s["tide0"][v], s["tide1"][v],
        ]
        if going_east:
            shift, spare, far = -(BS - OUT), 0, -(BS - OUT - 1)
        else:
            shift, spare, far = BS, OUT - 1, BS - 1
        out = jnp.zeros((8, LANES), F32)
        for f, item in enumerate(items):
            out = jnp.where(masks[f], roll(item, OUT * f + shift), out)
        out = jnp.where(cell == 6 * OUT + spare, roll(items[0], 6 * OUT + far), out)
        if v < 2:
            at = 7 * OUT + spare + (0 if going_east else BS)
            for h in range(2):
                put = lane == (at + BS * h) % LANES
                out = jnp.where(put, spread(nb[:, 2 * v + h : 2 * v + h + 1]), out)
        return out

    full = tiles * 3 // 4
    for ref, going_east in ((pe, True), (pw, False)):
        for i in range(tiles - full):
            extra = packed(full + i, going_east)
            for q in range(3):
                own = packed(3 * i + q, going_east)
                ref[3 * i + q] = jnp.where(cell < USED, own, roll(extra, USED - 16 * q))


def strip_of(tile, cell):
    return jnp.where(cell < BS // 2, roll(tile, OUT), roll(tile, -OUT))


def during_kernel(slices, state, depth_in, live_in, nb_ref, cor, tide, last, strips):
    tiles = depth_in.shape[1] // LANES
    lane, cell = lane_ids()
    fields = [Field(last, (i,)) for i in range(3)]
    for v in range(tiles):
        for i in range(3):
            fields[i][v] = Field(state, (i,))[v]
    cor_f = Field(cor)
    s = dict(
        depth=Field(depth_in), live=Field(live_in), level=fields[0], east=fields[1],
        north=fields[2], tide0=Field(tide, (0,)), tide1=Field(tide, (1,)),
        cor=lambda v: F32(0.3) * cor_f[v],
    )
    interior_steps(s, tiles, slices, range(SENT, STEPS), nb_ref)
    for v in range(tiles):
        items = [
            s["level"][v], s["east"][v], s["north"][v], s["depth"][v], s["live"][v],
            s["cor"](v), s["tide0"][v], s["tide1"][v],
        ]
        for f, item in enumerate(items):
            Field(strips, (f,))[v] = strip_of(item, cell)


def after_kernel(slices, pe, pw, strips, nb_ref, last, start, live_in, gain, defect, work):
    tiles = live_in.shape[1] // LANES
    lane, cell = lane_ids()
    lower = lane < BS
    full = tiles * 3 // 4
    odd = (cell // OUT) % 2 == 1
    even = jnp.logical_and(jnp.logical_not(odd), cell < USED)
    odd = jnp.logical_and(odd, cell < USED)
    outer = jnp.logical_or(cell < OUT, cell >= BS - OUT)

    def opened(ref, v):
        if v < full:
            return ref[v]
        out = None
        for q in range(3):
            part = roll(ref[3 * (v - full) + q], 16 * q - USED)
            out = part if out is None else jnp.where(cell >= 16 * q, part, out)
        return out

    for v in range(tiles):
        west, east = opened(pe, v), roll(opened(pw, v), -OUT)
        pair = (jnp.where(even, west, east), jnp.where(odd, west, east))
        for f in range(8):
            Field(work, (f,))[v] = jnp.where(outer, roll(pair[f % 2], -OUT * f), Field(strips, (f,))[v])

    names = ("level", "east", "north", "depth", "live", "cor", "tide0", "tide1")
    s = {name: Field(work, (f,)) for f, name in enumerate(names)}
    cor_f = s["cor"]
    s["cor"] = lambda v: cor_f[v]

    nb = nb_ref[...]
    t1 = s["tide1"]
    sent = [t1[0], t1[1]]

    def entry(j):
        tile, base = sent[j // 2], BS * (j % 2)
        west = spread(tile[:, base : base + 1]).astype(jnp.int32)
        east = spread(tile[:, base + BS - 1 : base + BS]).astype(jnp.int32)
        return west, spread(nb[:, j : j + 1]), east

    west_side, east_side = cell < OUT, cell >= BS - OUT

    def row_ghost(j):
        west, own, east = entry(j)
        return ghost_index(jnp.where(west_side, west, jnp.where(east_side, east, own)))

    north, south = row_ghost(0), row_ghost(1)
    slot = lax.broadcasted_iota(jnp.int32, (8, LANES), 0)
    west_e, own_e, _ = entry(2)
    _, own_w, east_w = entry(3)
    join_e = jnp.where(cell == OUT - 1, west_e, jnp.where(cell == BS - OUT - 1, own_e, slot))
    join_w = jnp.where(cell == OUT, own_w, jnp.where(cell == BS - OUT, east_w, slot))
    (to_e, on_e), (to_w, on_w) = ghost_index(join_e), ghost_index(join_w)

    def across(x):
        return take(roll(x, -1), to_e) * on_e - take(roll(x, 1), to_w) * on_w

    depth_of = jnp.minimum(cell, BS - 1 - cell)

    def update(k):
        low = OUT - jnp.minimum(k, HALF - k)
        return jnp.logical_and(depth_of >= low, depth_of <= k + OUT - 1)

    far = s["tide0"]
    far_w, far_e = cell == 0, cell == BS - 1

    def step_of(step, carry):
        ca, sa = phase(slices, step)
        level_half(s, tiles, ca, sa, update(2 * step + 1), lower, north, south, across)
        level = s["level"]
        slope = along(lambda v: level[v], tiles, lower, north, south)
        now = update(2 * step + 2)
        for v, dy in enumerate(slope):
            x, beyond = level[v], far[v]
            e = jnp.where(far_e, beyond, roll(x, -1))
            w = jnp.where(far_w, beyond, roll(x, 1))
            dx = take(e, to_e) * on_e - take(w, to_w) * on_w
            u, n = s["east"][v], s["north"][v]
            cor, live = s["cor"](v), s["live"][v]
            new_u = (F32(0.985) * u + cor * n - F32(0.15) * dx) * live
            new_n = (F32(0.985) * n - cor * u - F32(0.15) * dy) * live
            s["east"][v] = jnp.where(now, new_u, u)
            s["north"][v] = jnp.where(now, new_n, n)
        return carry

    lax.fori_loop(0, STEPS, step_of, 0)

    head, tail = cell < HALF, cell >= BS - HALF
    for v in range(tiles):
        live = Field(live_in)[v]
        for i in range(3):
            x = Field(work, (i,))[v]
            fine = jnp.where(head, roll(x, -OUT), jnp.where(tail, roll(x, OUT), Field(last, (i,))[v]))
            Field(defect, (i,))[v] = fine - Field(gain, (i,))[v] * (Field(start, (0, i))[v] * live)


def call(kernel, out_shape, operands, smem=(), scratch=(), flops=0):
    vmem = pl.BlockSpec(memory_space=pltpu.VMEM)
    size = sum(4 * x.size for x in operands)
    return pl.pallas_call(
        kernel,
        out_shape=out_shape,
        in_specs=[
            pl.BlockSpec(memory_space=pltpu.SMEM) if i in smem else vmem
            for i in range(len(operands))
        ],
        out_specs=jax.tree.map(lambda _: vmem, out_shape),
        scratch_shapes=scratch,
        cost_estimate=pl.CostEstimate(flops=flops, bytes_accessed=2 * size, transcendentals=0),
        compiler_params=pltpu.CompilerParams(vmem_limit_bytes=VMEM_LIMIT),
    )(*operands)


def shape(*dims):
    return jax.ShapeDtypeStruct(dims, F32)


def passed_along(shard, axis, by):
    size = lax.axis_size(axis)
    return lax.ppermute(shard, axis, [(i, (i + by) % size) for i in range(size)])


def body(
    start_states, coarse_gain, depth_level, depth_table, wet, block_count, neighbour, coriolis, tide
):
    slots, cells = wet.shape
    tiles = cells // LANES
    slices = lax.axis_size("tm")
    state, depth, live, pe, pw = call(
        functools.partial(before_kernel, slices),
        [shape(3, slots, cells), shape(slots, cells), shape(slots, cells)]
        + [shape(tiles * 3 // 4, slots, LANES)] * 2,
        [start_states, depth_level, depth_table, wet, block_count, neighbour, coriolis, tide],
        smem=(4,),
    )
    from_west = passed_along(pe, "space", 1)
    from_east = passed_along(pw, "space", -1)
    last, strips = call(
        functools.partial(during_kernel, slices),
        [shape(3, slots, cells), shape(8, slots, cells)],
        [state, depth, live, neighbour, coriolis, tide],
    )
    defect = call(
        functools.partial(after_kernel, slices),
        shape(3, slots, cells),
        [from_west, from_east, strips, neighbour, last, start_states, live, coarse_gain],
        scratch=[pltpu.VMEM((8, slots, cells), F32)],
    )
    total, power = passed_along(defect, "tm", 1), coarse_gain
    for _ in range(slices - 2):
        total = passed_along(defect + coarse_gain * total, "tm", 1)
        power = power * coarse_gain
    total = total + power * defect
    return (total / (1.0 - power * coarse_gain))[None]


def solution(mesh):
    return jax.shard_map(
        body,
        mesh=mesh,
        in_specs=(
            P("tm", None, "space", None),
            P(None, "space", None),
            P("space", None),
            P(),
            P("space", None),
            P("space"),
            P("space", None),
            P("space", None),
            P(None, "space", None),
        ),
        out_specs=P("tm", None, "space", None),
        check_vma=False,
    )
```

```python
import functools
import math

import jax
import jax.numpy as jnp
from jax import lax
from jax.experimental import pallas as pl
from jax.experimental.pallas import tpu as pltpu
from jax.sharding import PartitionSpec as P

BS = 64
STEPS = 6
HALF = 2 * STEPS
SENT = STEPS // 2
OUT = STEPS
LANES = 128
USED = 8 * OUT
F32 = jnp.float32
VMEM_LIMIT = 24 * 1024 * 1024


def roll(x, by):
    by = by % LANES
    return x if by == 0 else pltpu.roll(x, by, 1)


def take(x, index):
    return jnp.take_along_axis(x, index, axis=0, mode="promise_in_bounds")


def lane_ids():
    lane = lax.broadcasted_iota(jnp.int32, (8, LANES), 1)
    return lane, lane % BS


def spread(column):
    return jnp.broadcast_to(column, (8, LANES))


def ghost_index(entry):
    return jnp.maximum(entry, 0), (entry >= 0).astype(F32)


class Field:
    def __init__(self, ref, lead=()):
        self.ref, self.lead = ref, tuple(lead)

    def __getitem__(self, v):
        return self.ref[self.lead + (slice(None), pl.ds(v * LANES, LANES))]

    def __setitem__(self, v, value):
        self.ref[self.lead + (slice(None), pl.ds(v * LANES, LANES))] = value


def phase(count, step):
    omega = 2.0 * math.pi / (count * STEPS)
    here = lax.axis_index("tm")
    ca, sa = F32(0), F32(0)
    for n in range(count):
        for j in range(STEPS):
            hit = jnp.logical_and(here == n, step == j)
            angle = (n * STEPS + j) * omega
            ca = jnp.where(hit, F32(0.3 * math.cos(angle)), ca)
            sa = jnp.where(hit, F32(0.3 * math.sin(angle)), sa)
    return ca, sa


def along(tile, count, lower, north, south):
    first, last = roll(tile(0), BS), roll(tile(count - 1), BS)
    (north_at, north_on), (south_at, south_on) = north, south
    before, here = take(last, south_at) * south_on, first
    for v in range(count):
        if v == count - 1:
            after = take(first, north_at) * north_on
        elif v == count - 2:
            after = last
        else:
            after = roll(tile(v + 1), BS)
        yield jnp.where(lower, here, after) - jnp.where(lower, before, here)
        before, here = here, after


def across_open(x):
    return roll(x, -1) - roll(x, 1)


def level_half(s, count, ca, sa, update, lower, north, south, across):
    depth, level, east, northv = s["depth"], s["level"], s["east"], s["north"]
    slope = along(lambda v: depth[v] * northv[v], count, lower, north, south)
    for v, dy in enumerate(slope):
        div = across(depth[v] * east[v]) + dy
        old = level[v]
        new = (old + (s["tide0"][v] * ca + s["tide1"][v] * sa) - div) * s["live"][v]
        level[v] = jnp.where(update, new, old)


def velocity_half(s, count, update, lower, north, south, across):
    level = s["level"]
    slope = along(lambda v: level[v], count, lower, north, south)
    for v, dy in enumerate(slope):
        dx = across(level[v])
        u, w = s["east"][v], s["north"][v]
        cor, live = s["cor"](v), s["live"][v]
        new_u = (F32(0.985) * u + cor * w - F32(0.15) * dx) * live
        new_w = (F32(0.985) * w - cor * u - F32(0.15) * dy) * live
        s["east"][v] = jnp.where(update, new_u, u)
        s["north"][v] = jnp.where(update, new_w, w)


def own_ghosts(face):
    return ghost_index(face[0]), ghost_index(face[1])


def interior_steps(s, count, slices, steps, face):
    lane, cell = lane_ids()
    lower = lane < BS
    edge = jnp.minimum(cell, BS - 1 - cell) + 1
    north, south = own_ghosts(face)
    for step in steps:
        ca, sa = phase(slices, step)
        level_half(s, count, ca, sa, edge > 2 * step + 1, lower, north, south, across_open)
        velocity_half(s, count, edge > 2 * step + 2, lower, north, south, across_open)


def window(cell, f):
    return jnp.logical_and(cell >= OUT * f, cell < OUT * f + OUT)


def before_kernel(
    slices, count_ref, level_h, table_h, wet_h, nb_h, start_h, tide_h, cor_h,
    state, depth_out, live_out, face, pe, pw,
    level_id, table, wet, nb_ref, start, tide, cor, sems,
):
    loads = [
        pltpu.make_async_copy(src, dst, sems.at[i])
        for i, (src, dst) in enumerate(
            [
                (level_h, level_id), (table_h, table), (wet_h, wet), (nb_h, nb_ref),
                (start_h, start), (tide_h, tide), (cor_h, cor),
            ]
        )
    ]
    for load in loads:
        load.start()
    tiles = wet.shape[1] // LANES
    lane, cell = lane_ids()
    slot = lax.broadcasted_iota(jnp.int32, (8, LANES), 0)
    held = (slot < count_ref[0]).astype(F32)
    for load in loads[:5]:
        load.wait()
    for j in range(4):
        entry = jnp.broadcast_to(nb_ref[j : j + 1, :], (8, 8))
        here = lax.broadcasted_iota(jnp.int32, (8, 8), 0) == lax.broadcasted_iota(jnp.int32, (8, 8), 1)
        face[j] = spread(jnp.sum(jnp.where(here, entry, 0), axis=1, keepdims=True))
    row = F32(0.15) * table[...].reshape(1, table.shape[0])
    row = jnp.broadcast_to(jnp.concatenate([row] * (LANES // row.shape[1]), axis=1), (8, LANES))
    depth, live = Field(depth_out), Field(live_out)
    fields = [Field(state, (i,)) for i in range(3)]
    ids, land = Field(level_id), Field(wet)
    for v in range(tiles):
        depth[v] = jnp.take_along_axis(row, ids[v], axis=1, mode="promise_in_bounds")
        live[v] = land[v].astype(F32) * held
        for i in range(3):
            fields[i][v] = Field(start, (0, i))[v] * live[v]
    for load in loads[5:]:
        load.wait()
    cor_f = Field(cor)
    s = dict(
        depth=depth, live=live, level=fields[0], east=fields[1], north=fields[2],
        tide0=Field(tide, (0,)), tide1=Field(tide, (1,)), cor=lambda v: F32(0.3) * cor_f[v],
    )
    interior_steps(s, tiles, slices, range(SENT), face)

    masks = [window(cell, f) for f in range(8)]

    def packed(v, going_east):
        items = [
            s["level"][v], s["east"][v], s["north"][v], depth[v], live[v],
            s["cor"](v), s["tide0"][v], s["tide1"][v],
        ]
        if going_east:
            shift, spare, far = -(BS - OUT), 0, -(BS - OUT - 1)
        else:
            shift, spare, far = BS, OUT - 1, BS - 1
        out = jnp.zeros((8, LANES), F32)
        for f, item in enumerate(items):
            out = jnp.where(masks[f], roll(item, OUT * f + shift), out)
        out = jnp.where(cell == 6 * OUT + spare, roll(items[0], 6 * OUT + far), out)
        if v < 2:
            at = 7 * OUT + spare + (0 if going_east else BS)
            for h in range(2):
                put = lane == (at + BS * h) % LANES
                out = jnp.where(put, face[2 * v + h].astype(F32), out)
        return out

    full = tiles * 3 // 4
    for ref, going_east in ((pe, True), (pw, False)):
        for i in range(tiles - full):
            extra = packed(full + i, going_east)
            for q in range(3):
                own = packed(3 * i + q, going_east)
                ref[3 * i + q] = jnp.where(cell < USED, own, roll(extra, USED - 16 * q))


def strip_of(tile, cell):
    return jnp.where(cell < BS // 2, roll(tile, OUT), roll(tile, -OUT))


def during_kernel(slices, state, depth_in, live_in, face, cor, tide, last, strips):
    tiles = depth_in.shape[1] // LANES
    lane, cell = lane_ids()
    fields = [Field(last, (i,)) for i in range(3)]
    for v in range(tiles):
        for i in range(3):
            fields[i][v] = Field(state, (i,))[v]
    cor_f = Field(cor)
    s = dict(
        depth=Field(depth_in), live=Field(live_in), level=fields[0], east=fields[1],
        north=fields[2], tide0=Field(tide, (0,)), tide1=Field(tide, (1,)),
        cor=lambda v: F32(0.3) * cor_f[v],
    )
    interior_steps(s, tiles, slices, range(SENT, STEPS), face)
    for v in range(tiles):
        items = [
            s["level"][v], s["east"][v], s["north"][v], s["depth"][v], s["live"][v],
            s["cor"](v), s["tide0"][v], s["tide1"][v],
        ]
        for f, item in enumerate(items):
            Field(strips, (f,))[v] = strip_of(item, cell)


def after_kernel(slices, pe, pw, strips, face, last, start, live_in, gain, defect, work):
    tiles = live_in.shape[1] // LANES
    lane, cell = lane_ids()
    lower = lane < BS
    full = tiles * 3 // 4
    odd = (cell // OUT) % 2 == 1
    even = jnp.logical_and(jnp.logical_not(odd), cell < USED)
    odd = jnp.logical_and(odd, cell < USED)
    outer = jnp.logical_or(cell < OUT, cell >= BS - OUT)

    def opened(ref, v):
        if v < full:
            return ref[v]
        out = None
        for q in range(3):
            part = roll(ref[3 * (v - full) + q], 16 * q - USED)
            out = part if out is None else jnp.where(cell >= 16 * q, part, out)
        return out

    for v in range(tiles):
        west, east = opened(pe, v), roll(opened(pw, v), -OUT)
        pair = (jnp.where(even, west, east), jnp.where(odd, west, east))
        for f in range(8):
            Field(work, (f,))[v] = jnp.where(outer, roll(pair[f % 2], -OUT * f), Field(strips, (f,))[v])

    names = ("level", "east", "north", "depth", "live", "cor", "tide0", "tide1")
    s = {name: Field(work, (f,)) for f, name in enumerate(names)}
    cor_f = s["cor"]
    s["cor"] = lambda v: cor_f[v]

    t1 = s["tide1"]
    sent = [t1[0], t1[1]]

    def entry(j):
        tile, base = sent[j // 2], BS * (j % 2)
        west = spread(tile[:, base : base + 1]).astype(jnp.int32)
        east = spread(tile[:, base + BS - 1 : base + BS]).astype(jnp.int32)
        return west, face[j], east

    west_side, east_side = cell < OUT, cell >= BS - OUT

    def row_ghost(j):
        west, own, east = entry(j)
        return ghost_index(jnp.where(west_side, west, jnp.where(east_side, east, own)))

    north, south = row_ghost(0), row_ghost(1)
    slot = lax.broadcasted_iota(jnp.int32, (8, LANES), 0)
    west_e, own_e, _ = entry(2)
    _, own_w, east_w = entry(3)
    join_e = jnp.where(cell == OUT - 1, west_e, jnp.where(cell == BS - OUT - 1, own_e, slot))
    join_w = jnp.where(cell == OUT, own_w, jnp.where(cell == BS - OUT, east_w, slot))
    (to_e, on_e), (to_w, on_w) = ghost_index(join_e), ghost_index(join_w)

    def across(x):
        return take(roll(x, -1), to_e) * on_e - take(roll(x, 1), to_w) * on_w

    depth_of = jnp.minimum(cell, BS - 1 - cell)

    def update(k):
        low = OUT - jnp.minimum(k, HALF - k)
        return jnp.logical_and(depth_of >= low, depth_of <= k + OUT - 1)

    far = s["tide0"]
    far_w, far_e = cell == 0, cell == BS - 1

    def step_of(step, carry):
        ca, sa = phase(slices, step)
        level_half(s, tiles, ca, sa, update(2 * step + 1), lower, north, south, across)
        level = s["level"]
        slope = along(lambda v: level[v], tiles, lower, north, south)
        now = update(2 * step + 2)
        for v, dy in enumerate(slope):
            x, beyond = level[v], far[v]
            e = jnp.where(far_e, beyond, roll(x, -1))
            w = jnp.where(far_w, beyond, roll(x, 1))
            dx = take(e, to_e) * on_e - take(w, to_w) * on_w
            u, n = s["east"][v], s["north"][v]
            cor, live = s["cor"](v), s["live"][v]
            new_u = (F32(0.985) * u + cor * n - F32(0.15) * dx) * live
            new_n = (F32(0.985) * n - cor * u - F32(0.15) * dy) * live
            s["east"][v] = jnp.where(now, new_u, u)
            s["north"][v] = jnp.where(now, new_n, n)
        return carry

    lax.fori_loop(0, STEPS, step_of, 0)

    head, tail = cell < HALF, cell >= BS - HALF
    for v in range(tiles):
        live = Field(live_in)[v]
        for i in range(3):
            x = Field(work, (i,))[v]
            fine = jnp.where(head, roll(x, -OUT), jnp.where(tail, roll(x, OUT), Field(last, (i,))[v]))
            Field(defect, (i,))[v] = fine - Field(gain, (i,))[v] * (Field(start, (0, i))[v] * live)


def call(kernel, out_shape, operands, spaces=None, scratch=(), flops=0):
    vmem = pl.BlockSpec(memory_space=pltpu.VMEM)
    spaces = spaces or [pltpu.VMEM] * len(operands)
    size = sum(4 * x.size for x in operands)
    return pl.pallas_call(
        kernel,
        out_shape=out_shape,
        in_specs=[pl.BlockSpec(memory_space=space) for space in spaces],
        out_specs=jax.tree.map(lambda _: vmem, out_shape),
        scratch_shapes=scratch,
        cost_estimate=pl.CostEstimate(flops=flops, bytes_accessed=2 * size, transcendentals=0),
        compiler_params=pltpu.CompilerParams(vmem_limit_bytes=VMEM_LIMIT),
    )(*operands)


def shape(*dims):
    return jax.ShapeDtypeStruct(dims, F32)


def passed_along(shard, axis, by):
    size = lax.axis_size(axis)
    return lax.ppermute(shard, axis, [(i, (i + by) % size) for i in range(size)])


def body(
    start_states, coarse_gain, depth_level, depth_table, wet, block_count, neighbour, coriolis, tide
):
    slots, cells = wet.shape
    tiles = cells // LANES
    slices = lax.axis_size("tm")
    loaded = [depth_level, depth_table, wet, neighbour.T, start_states, tide, coriolis]
    state, depth, live, face, pe, pw = call(
        functools.partial(before_kernel, slices),
        [shape(3, slots, cells), shape(slots, cells), shape(slots, cells)]
        + [jax.ShapeDtypeStruct((4, slots, LANES), jnp.int32)]
        + [shape(tiles * 3 // 4, slots, LANES)] * 2,
        [block_count] + [pltpu.with_memory_space_constraint(x, pltpu.HBM) for x in loaded],
        spaces=[pltpu.SMEM] + [pltpu.HBM] * len(loaded),
        scratch=[pltpu.VMEM(x.shape, x.dtype) for x in loaded]
        + [pltpu.SemaphoreType.DMA((len(loaded),))],
    )
    from_west = passed_along(pe, "space", 1)
    from_east = passed_along(pw, "space", -1)
    last, strips = call(
        functools.partial(during_kernel, slices),
        [shape(3, slots, cells), shape(8, slots, cells)],
        [state, depth, live, face, coriolis, tide],
    )
    defect = call(
        functools.partial(after_kernel, slices),
        shape(3, slots, cells),
        [from_west, from_east, strips, face, last, start_states, live, coarse_gain],
        scratch=[pltpu.VMEM((8, slots, cells), F32)],
    )
    total, power = passed_along(defect, "tm", 1), coarse_gain
    for _ in range(slices - 2):
        total = passed_along(defect + coarse_gain * total, "tm", 1)
        power = power * coarse_gain
    total = total + power * defect
    return (total / (1.0 - power * coarse_gain))[None]


def solution(mesh):
    return jax.shard_map(
        body,
        mesh=mesh,
        in_specs=(
            P("tm", None, "space", None),
            P(None, "space", None),
            P("space", None),
            P(),
            P("space", None),
            P("space"),
            P("space", None),
            P("space", None),
            P(None, "space", None),
        ),
        out_specs=P("tm", None, "space", None),
        check_vma=False,
    )
```

```python
import functools
import math

import jax
import jax.numpy as jnp
from jax import lax
from jax.experimental import pallas as pl
from jax.experimental.pallas import tpu as pltpu
from jax.sharding import PartitionSpec as P

BS = 64
STEPS = 6
HALF = 2 * STEPS
SENT = STEPS // 2
OUT = STEPS
LANES = 128
SUB = 8
ROWS = 4
GROUPS = BS // SUB
F32 = jnp.float32
VMEM_LIMIT = 24 * 1024 * 1024


def shifted(x, by):
    return pltpu.roll(x, by % SUB, 0)


def lanes_of(x, index):
    return jnp.take_along_axis(x, index, axis=1, mode="promise_in_bounds")


def tile_iota(dim):
    return lax.broadcasted_iota(jnp.int32, (SUB, LANES), dim)


def lane_tile(ref, v, lead=()):
    return ref[tuple(lead) + (slice(None), pl.ds(v * LANES, LANES))]


def to_columns(tiles):
    out = []
    for part in (tiles[0::2], tiles[1::2]):
        turned = jnp.concatenate(part, axis=0).T
        out += [turned[:BS], turned[BS:]]
    return out


def to_tiles(columns):
    out = {}
    for part in range(2):
        turned = jnp.concatenate(columns[2 * part : 2 * part + 2], axis=0).T
        for c in range(LANES // SUB):
            out[2 * c + part] = turned[SUB * c : SUB * c + SUB]
    return [out[v] for v in range(len(out))]


def phase(count, step):
    omega = 2.0 * math.pi / (count * STEPS)
    here = lax.axis_index("tm")
    ca, sa = F32(0), F32(0)
    for n in range(count):
        angle = (n * STEPS + step) * omega
        ca = jnp.where(here == n, F32(0.3 * math.cos(angle)), ca)
        sa = jnp.where(here == n, F32(0.3 * math.sin(angle)), sa)
    return ca, sa


def chunk_ghosts(north, south):
    lane = tile_iota(1)
    top, bottom = lane >= LANES - SUB, lane < SUB
    up = jnp.where(top, jnp.maximum(north, 0), (lane + SUB) % LANES)
    down = jnp.where(bottom, LANES - SUB + jnp.maximum(south, 0), (lane + LANES - SUB) % LANES)
    up_on = jnp.where(jnp.logical_and(top, north < 0), F32(0), F32(1))
    down_on = jnp.where(jnp.logical_and(bottom, south < 0), F32(0), F32(1))
    return up, up_on, down, down_on


def face_rows(nb):
    wide = jnp.concatenate([nb] * (LANES // SUB), axis=1)
    return [jnp.broadcast_to(wide[j : j + 1], (SUB, LANES)) for j in range(4)]


def y_slopes(t, ghosts):
    up, up_on, down, down_on = ghosts
    above = lanes_of(t[0], up) * up_on
    below = lanes_of(t[3], down) * down_on
    return [t[1] - below, t[2] - t[0], t[3] - t[1], above - t[2]]


def x_slopes(columns):
    sub = tile_iota(0)
    first, last = sub == 0, sub == SUB - 1
    get = [columns(q) for q in range(GROUPS)]
    easts = [[shifted(x, -1) for x in t] for t in get]
    wests = [[shifted(x, 1) for x in t] for t in get]
    for q in range(GROUPS):
        east, west = easts[q], wests[q]
        if q + 1 < GROUPS:
            east = [jnp.where(last, b, a) for a, b in zip(east, easts[q + 1])]
        if q > 0:
            west = [jnp.where(first, b, a) for a, b in zip(west, wests[q - 1])]
        yield [e - w for e, w in zip(east, west)]


def new_level(level, t0, t1, ca, sa, dx, dy, live):
    return (level + (t0 * ca + t1 * sa) - (dx + dy)) * live


def new_velocity(u, w, cor, dx, dy, live):
    return (
        (F32(0.985) * u + cor * w - F32(0.15) * dx) * live,
        (F32(0.985) * w - cor * u - F32(0.15) * dy) * live,
    )


NAMES = ("level", "east", "north", "depth", "live", "cor", "tide0", "tide1")


def fields_of(state, still):
    return {
        name: (state, f) if f < 3 else (still, f - 3) for f, name in enumerate(NAMES)
    }


def interior_steps(s, slices, steps, ghosts):
    sub = tile_iota(0)

    def tiles(name, q):
        ref, f = s[name]
        return [ref[f, i, pl.ds(SUB * q, SUB), :] for i in range(ROWS)]

    def put(name, q, k, new, old):
        ref, f = s[name]
        least = min(SUB * q, BS - SUB - SUB * q) + 1
        if k >= least + SUB - 1:
            return
        if k >= least:
            edge = (sub if q < GROUPS // 2 else SUB - 1 - sub) + least
            new = [jnp.where(edge > k, a, b) for a, b in zip(new, old)]
        for i in range(ROWS):
            ref[f, i, pl.ds(SUB * q, SUB), :] = new[i]

    def product(a, b):
        return [x * y for x, y in zip(a, b)]

    for step in steps:
        ca, sa = phase(slices, step)
        slope = x_slopes(lambda q: product(tiles("depth", q), tiles("east", q)))
        for q, dx in enumerate(slope):
            dy = y_slopes(product(tiles("depth", q), tiles("north", q)), ghosts)
            old = tiles("level", q)
            t0, t1, live = tiles("tide0", q), tiles("tide1", q), tiles("live", q)
            new = [
                new_level(old[i], t0[i], t1[i], ca, sa, dx[i], dy[i], live[i]) for i in range(ROWS)
            ]
            put("level", q, 2 * step + 1, new, old)
        slope = x_slopes(lambda q: tiles("level", q))
        for q, dx in enumerate(slope):
            dy = y_slopes(tiles("level", q), ghosts)
            u, w, cor, live = (tiles(n, q) for n in ("east", "north", "cor", "live"))
            new = [new_velocity(u[i], w[i], cor[i], dx[i], dy[i], live[i]) for i in range(ROWS)]
            put("east", q, 2 * step + 2, [a for a, _ in new], u)
            put("north", q, 2 * step + 2, [b for _, b in new], w)


def before_kernel(
    slices, count_ref, level_h, table_h, wet_h, nb_h, start_h, tide_h, cor_h,
    state, still, begin, face, pe, pw,
    level_id, table, wet, nb_ref, start, tide, cor, sems,
):
    loads = [
        pltpu.make_async_copy(src, dst, sems.at[i])
        for i, (src, dst) in enumerate(
            [
                (level_h, level_id), (table_h, table), (wet_h, wet), (nb_h, nb_ref),
                (start_h, start), (tide_h, tide), (cor_h, cor),
            ]
        )
    ]
    for load in loads:
        load.start()
    tiles = wet.shape[1] // LANES
    held = (tile_iota(0) < count_ref[0]).astype(F32)

    def store(ref, f, columns):
        for i in range(ROWS):
            ref[f, i] = columns[i]

    for load in loads[:4]:
        load.wait()
    row = F32(0.15) * table[...].reshape(1, table.shape[0])
    row = jnp.broadcast_to(jnp.concatenate([row] * (LANES // row.shape[1]), axis=1), (SUB, LANES))
    live = [lane_tile(wet, v).astype(F32) * held for v in range(tiles)]
    store(still, 1, to_columns(live))
    store(still, 0, to_columns([lanes_of(row, lane_tile(level_id, v)) for v in range(tiles)]))
    rows = face_rows(nb_ref[...])
    for j in range(4):
        face[j] = rows[j]
    loads[4].wait()
    for f in range(3):
        own = [lane_tile(start, v, (0, f)) * live[v] for v in range(tiles)]
        for v in range(tiles):
            begin[f, :, pl.ds(v * LANES, LANES)] = own[v]
        store(state, f, to_columns(own))
    loads[5].wait()
    for f in range(2):
        store(still, 3 + f, to_columns([lane_tile(tide, v, (f,)) for v in range(tiles)]))
    loads[6].wait()
    store(still, 2, to_columns([F32(0.3) * lane_tile(cor, v) for v in range(tiles)]))

    s = fields_of(state, still)
    interior_steps(s, slices, range(SENT), chunk_ghosts(rows[0], rows[1]))

    for f, name in enumerate(NAMES):
        ref, at = s[name]
        for i in range(ROWS):
            pe[i, pl.ds(OUT * f, OUT), :] = ref[at, i, pl.ds(BS - OUT, OUT), :]
            pw[i, pl.ds(OUT * f, OUT), :] = ref[at, i, pl.ds(0, OUT), :]
    for i in range(ROWS):
        pe[i, pl.ds(6 * OUT, 1), :] = state[0, i, pl.ds(BS - OUT - 1, 1), :]
        pw[i, pl.ds(6 * OUT + OUT - 1, 1), :] = state[0, i, pl.ds(OUT, 1), :]
        entry = rows[i][:1].astype(F32)
        pe[i, pl.ds(7 * OUT, 1), :] = entry
        pw[i, pl.ds(7 * OUT + OUT - 1, 1), :] = entry


def during_kernel(slices, state, still, face, last):
    last[...] = state[...]
    ghosts = chunk_ghosts(face[0], face[1])
    interior_steps(fields_of(last, still), slices, range(SENT, STEPS), ghosts)


def after_kernel(slices, pe, pw, last, still, face, begin, gain, defect, joined):
    tiles = begin.shape[-1] // LANES
    sub, lane = tile_iota(0), tile_iota(1)
    s = fields_of(last, still)

    for f, name in enumerate(NAMES):
        ref, at = s[name]
        for i in range(ROWS):
            joined[f, i, 0, pl.ds(0, OUT), :] = pe[i, pl.ds(OUT * f, OUT), :]
            joined[f, i, 0, pl.ds(OUT, 2), :] = ref[at, i, pl.ds(0, 2), :]
            joined[f, i, 1, pl.ds(0, 2), :] = ref[at, i, pl.ds(BS - 2, 2), :]
            joined[f, i, 1, pl.ds(2, OUT), :] = pw[i, pl.ds(OUT * f, OUT), :]

    def load(name, side, g):
        f = NAMES.index(name)
        if g == 0:
            return [joined[f, i, side] for i in range(ROWS)]
        ref, at = s[name]
        low = SUB * g - OUT
        low = low if side == 0 else BS - SUB - low
        return [ref[at, i, pl.ds(low, SUB), :] for i in range(ROWS)]

    own = [face[j] for j in range(4)]
    ghosts, joins, far = [], [], []
    for side in range(2):
        row = 0 if side == 0 else SUB - 1
        sent = [
            jnp.broadcast_to(joined[7, j, side, pl.ds(row, 1), :].astype(jnp.int32), (SUB, LANES))
            for j in range(4)
        ]
        outer = sub < OUT if side == 0 else sub >= 2
        mixed = [jnp.where(outer, sent[j], own[j]) for j in range(4)]
        here = chunk_ghosts(own[0], own[1])
        ghosts.append([chunk_ghosts(mixed[0], mixed[1]), here, here])
        to = jnp.where(outer, own[3 - side], sent[2 + side])
        joins.append((lane - lane % SUB + jnp.maximum(to, 0), (to >= 0).astype(F32)))
    inner_row = (OUT, 1)
    outer_row = (OUT - 1, 2)

    def x_side(side, t, beyond=None):
        index, on = joins[side]
        looked = [lanes_of(x, index) * on for x in t[0]]
        inner = [jnp.where(sub == inner_row[side], b, a) for a, b in zip(t[0], looked)]
        outer = [jnp.where(sub == outer_row[side], b, a) for a, b in zip(t[0], looked)]
        sign = -1 if side == 0 else 1
        end_in, end_out = (SUB - 1, 0) if side == 0 else (0, SUB - 1)
        inward = [[shifted(x, sign) for x in inner]]
        outward = [[shifted(x, -sign) for x in outer]]
        if beyond is not None:
            outward[0] = [jnp.where(sub == end_out, b, a) for a, b in zip(outward[0], beyond)]
        plain_out = [[shifted(x, -sign) for x in t[0]]]
        for g in range(1, len(t)):
            inward.append([shifted(x, sign) for x in t[g]])
            plain_out.append([shifted(x, -sign) for x in t[g]])
        for g in range(1, len(t)):
            outward.append(
                [jnp.where(sub == end_out, b, a) for a, b in zip(plain_out[g], plain_out[g - 1])]
            )
        for g in range(len(t) - 1):
            inward[g] = [
                jnp.where(sub == end_in, b, a) for a, b in zip(inward[g], inward[g + 1])
            ]
        return [
            [(a - b) if side == 0 else (b - a) for a, b in zip(inward[g], outward[g])]
            for g in range(len(t))
        ]

    def changed(side, g, k):
        place = sub if side == 0 else SUB - 1 - sub
        if g == 0:
            reach = min(k, HALF - k)
            mask = place >= OUT - reach
            return mask if k >= 2 else jnp.logical_and(mask, place <= OUT)
        least = SUB * g - OUT + 1
        if k < least:
            return False
        return None if k >= least + SUB - 1 else place + least <= k

    cells = {
        (n, side, g): load(n, side, g)
        for n in ("level", "east", "north") for side in range(2) for g in range(3)
    }

    def put(name, side, g, mask, new):
        key = (name, side, g)
        if mask is not None:
            new = [jnp.where(mask, a, b) for a, b in zip(new, cells[key])]
        cells[key] = new

    def product(a, b):
        return [x * y for x, y in zip(a, b)]

    for k in range(1, HALF + 1):
        ca, sa = phase(slices, (k - 1) // 2)
        active = [g for g in range(3) if changed(0, g, k) is not False]
        reach = min(3, len(active) + 1)
        for side in range(2):
            if k % 2 == 1:
                depth = [load("depth", side, g) for g in range(reach)]
                dx = x_side(
                    side, [product(depth[g], cells["east", side, g]) for g in range(reach)]
                )
                for g in active:
                    flux = product(depth[g], cells["north", side, g])
                    dy = y_slopes(flux, ghosts[side][g])
                    t0, t1, live = (load(n, side, g) for n in ("tide0", "tide1", "live"))
                    old = cells["level", side, g]
                    new = [
                        new_level(old[i], t0[i], t1[i], ca, sa, dx[g][i], dy[i], live[i])
                        for i in range(ROWS)
                    ]
                    put("level", side, g, changed(side, g, k), new)
            else:
                beyond = load("tide0", side, 0) if k == OUT else None
                dx = x_side(side, [cells["level", side, g] for g in range(reach)], beyond)
                for g in active:
                    dy = y_slopes(cells["level", side, g], ghosts[side][g])
                    cor, live = load("cor", side, g), load("live", side, g)
                    u, w = cells["east", side, g], cells["north", side, g]
                    new = [
                        new_velocity(u[i], w[i], cor[i], dx[g][i], dy[i], live[i])
                        for i in range(ROWS)
                    ]
                    mask = changed(side, g, k)
                    put("east", side, g, mask, [a for a, _ in new])
                    put("north", side, g, mask, [b for _, b in new])

    for f, name in enumerate(NAMES[:3]):
        fine = []
        for i in range(ROWS):
            a, b, c = (shifted(cells[name, 0, g][i], 2) for g in range(3))
            d, e, h = (shifted(cells[name, 1, g][i], -2) for g in range(3))
            q = [last[f, i, pl.ds(SUB * n, SUB), :] for n in range(GROUPS)]
            q[0] = jnp.where(sub < 2, a, b)
            q[1] = jnp.where(sub < 2, b, jnp.where(sub < 4, c, q[1]))
            q[6] = jnp.where(sub >= 6, e, jnp.where(sub >= 4, h, q[6]))
            q[7] = jnp.where(sub >= 6, d, e)
            fine.append(jnp.concatenate(q, axis=0))
        for v, x in enumerate(to_tiles(fine)):
            at = pl.ds(v * LANES, LANES)
            defect[f, :, at] = x - gain[f, :, at] * begin[f, :, at]


def call(kernel, out_shape, operands, spaces=None, scratch=()):
    vmem = pl.BlockSpec(memory_space=pltpu.VMEM)
    spaces = spaces or [pltpu.VMEM] * len(operands)
    size = sum(4 * x.size for x in operands)
    return pl.pallas_call(
        kernel,
        out_shape=out_shape,
        in_specs=[pl.BlockSpec(memory_space=space) for space in spaces],
        out_specs=jax.tree.map(lambda _: vmem, out_shape),
        scratch_shapes=scratch,
        cost_estimate=pl.CostEstimate(flops=0, bytes_accessed=2 * size, transcendentals=0),
        compiler_params=pltpu.CompilerParams(vmem_limit_bytes=VMEM_LIMIT),
    )(*operands)


def shape(*dims):
    return jax.ShapeDtypeStruct(dims, F32)


def passed_along(shard, axis, by):
    size = lax.axis_size(axis)
    return lax.ppermute(shard, axis, [(i, (i + by) % size) for i in range(size)])


def body(
    start_states, coarse_gain, depth_level, depth_table, wet, block_count, neighbour, coriolis, tide
):
    slots, cells = wet.shape
    slices = lax.axis_size("tm")
    loaded = [depth_level, depth_table, wet, neighbour.T, start_states, tide, coriolis]
    state, still, begin, face, pe, pw = call(
        functools.partial(before_kernel, slices),
        [shape(3, ROWS, BS, LANES), shape(5, ROWS, BS, LANES), shape(3, slots, cells)]
        + [jax.ShapeDtypeStruct((4, SUB, LANES), jnp.int32)]
        + [shape(ROWS, len(NAMES) * OUT, LANES)] * 2,
        [block_count] + [pltpu.with_memory_space_constraint(x, pltpu.HBM) for x in loaded],
        spaces=[pltpu.SMEM] + [pltpu.HBM] * len(loaded),
        scratch=[pltpu.VMEM(x.shape, x.dtype) for x in loaded]
        + [pltpu.SemaphoreType.DMA((len(loaded),))],
    )
    from_west = passed_along(pe, "space", 1)
    from_east = passed_along(pw, "space", -1)
    last = call(
        functools.partial(during_kernel, slices),
        shape(3, ROWS, BS, LANES),
        [state, still, face],
    )
    defect = call(
        functools.partial(after_kernel, slices),
        shape(3, slots, cells),
        [from_west, from_east, last, still, face, begin, coarse_gain],
        scratch=[pltpu.VMEM((len(NAMES), ROWS, 2, SUB, LANES), F32)],
    )
    total, power = passed_along(defect, "tm", 1), coarse_gain
    for _ in range(slices - 2):
        total = passed_along(defect + coarse_gain * total, "tm", 1)
        power = power * coarse_gain
    total = total + power * defect
    return (total / (1.0 - power * coarse_gain))[None]


def solution(mesh):
    return jax.shard_map(
        body,
        mesh=mesh,
        in_specs=(
            P("tm", None, "space", None),
            P(None, "space", None),
            P("space", None),
            P(),
            P("space", None),
            P("space"),
            P("space", None),
            P("space", None),
            P(None, "space", None),
        ),
        out_specs=P("tm", None, "space", None),
        check_vma=False,
    )
```

```python
import functools
import math

import jax
import jax.numpy as jnp
from jax import lax
from jax.experimental import pallas as pl
from jax.experimental.pallas import tpu as pltpu
from jax.sharding import PartitionSpec as P

BS = 64
STEPS = 6
HALF = 2 * STEPS
SENT = STEPS // 2
OUT = STEPS
LANES = 128
SUB = 8
ROWS = 4
GROUPS = BS // SUB
F32 = jnp.float32
VMEM_LIMIT = 24 * 1024 * 1024


def shifted(x, by):
    return pltpu.roll(x, by % SUB, 0)


def lanes_of(x, index):
    return jnp.take_along_axis(x, index, axis=1, mode="promise_in_bounds")


def tile_iota(dim):
    return lax.broadcasted_iota(jnp.int32, (SUB, LANES), dim)


def lane_tile(ref, v, lead=()):
    return ref[tuple(lead) + (slice(None), pl.ds(v * LANES, LANES))]


def to_columns(tiles):
    out = []
    for part in (tiles[0::2], tiles[1::2]):
        turned = jnp.concatenate(part, axis=0).T
        out += [turned[:BS], turned[BS:]]
    return out


def to_tiles(columns):
    out = {}
    for part in range(2):
        turned = jnp.concatenate(columns[2 * part : 2 * part + 2], axis=0).T
        for c in range(LANES // SUB):
            out[2 * c + part] = turned[SUB * c : SUB * c + SUB]
    return [out[v] for v in range(len(out))]


def phase(count, step):
    omega = 2.0 * math.pi / (count * STEPS)
    here = lax.axis_index("tm")
    ca, sa = F32(0), F32(0)
    for n in range(count):
        angle = (n * STEPS + step) * omega
        ca = jnp.where(here == n, F32(0.3 * math.cos(angle)), ca)
        sa = jnp.where(here == n, F32(0.3 * math.sin(angle)), sa)
    return ca, sa


def chunk_ghosts(north, south):
    lane = tile_iota(1)
    top, bottom = lane >= LANES - SUB, lane < SUB
    up = jnp.where(top, jnp.maximum(north, 0), (lane + SUB) % LANES)
    down = jnp.where(bottom, LANES - SUB + jnp.maximum(south, 0), (lane + LANES - SUB) % LANES)
    up_on = jnp.where(jnp.logical_and(top, north < 0), F32(0), F32(1))
    down_on = jnp.where(jnp.logical_and(bottom, south < 0), F32(0), F32(1))
    return up, up_on, down, down_on


def two_way_ghosts(ghosts):
    up, up_on, down, down_on = ghosts
    return lanes_of(down, up), lanes_of(down_on, up), lanes_of(up, down), lanes_of(up_on, down)


def face_rows(nb):
    wide = jnp.concatenate([nb] * (LANES // SUB), axis=1)
    return [jnp.broadcast_to(wide[j : j + 1], (SUB, LANES)) for j in range(4)]


def y_slopes(t, ghosts):
    up, up_on, down, down_on = ghosts
    above = lanes_of(t[0], up) * up_on
    below = lanes_of(t[3], down) * down_on
    return [t[1] - below, t[2] - t[0], t[3] - t[1], above - t[2]]


def x_slopes(columns, runs):
    sub = tile_iota(0)
    first, last = sub == 0, sub == SUB - 1
    for run in runs:
        get = [columns(q) for q in run]
        easts = [[shifted(x, -1) for x in t] for t in get]
        wests = [[shifted(x, 1) for x in t] for t in get]
        for n, q in enumerate(run):
            east, west = easts[n], wests[n]
            if n + 1 < len(run):
                east = [jnp.where(last, b, a) for a, b in zip(east, easts[n + 1])]
            if n > 0:
                west = [jnp.where(first, b, a) for a, b in zip(west, wests[n - 1])]
            yield q, [e - w for e, w in zip(east, west)]


def new_level(level, t0, t1, ca, sa, dx, dy, live):
    return (level + (t0 * ca + t1 * sa) - (dx + dy)) * live


def new_velocity(u, w, cor, dx, dy, live):
    return (
        (F32(0.985) * u + cor * w - F32(0.15) * dx) * live,
        (F32(0.985) * w - cor * u - F32(0.15) * dy) * live,
    )


NAMES = ("level", "east", "north", "depth", "live", "cor", "tide0", "tide1")


def fields_of(state, still):
    return {
        name: (state, f) if f < 3 else (still, f - 3) for f, name in enumerate(NAMES)
    }


def interior_steps(s, runs, slices, steps, ghosts, wide):
    sub = tile_iota(0)
    place = {q: SUB * n for n, q in enumerate(q for run in runs for q in run)}

    def tiles(name, q):
        ref, f = s[name]
        return [ref[f, i, pl.ds(place[q], SUB), :] for i in range(ROWS)]

    def put(name, q, k, new, old):
        ref, f = s[name]
        least = min(SUB * q, BS - SUB - SUB * q) + 1
        if k >= least + SUB - 1:
            return
        if k >= least:
            edge = (sub if q < GROUPS // 2 else SUB - 1 - sub) + least
            new = [jnp.where(edge > k, a, b) for a, b in zip(new, old)]
        for i in range(ROWS):
            ref[f, i, pl.ds(place[q], SUB), :] = new[i]

    def product(a, b):
        return [x * y for x, y in zip(a, b)]

    up, up_on, down, down_on = ghosts
    if wide:
        back_up, back_up_on, back_down, back_down_on = two_way_ghosts(ghosts)
    live_over, live_under = {}, {}
    for q in place if wide else ():
        live = tiles("live", q)
        live_over[q] = lanes_of(live[0], up) * up_on
        live_under[q] = lanes_of(live[3], down) * down_on
    for step in steps:
        ca, sa = phase(slices, step)
        slope = x_slopes(lambda q: product(tiles("depth", q), tiles("east", q)), runs)
        dys = {}
        for q, dx in slope:
            old = tiles("level", q)
            t0, t1, live = tiles("tide0", q), tiles("tide1", q), tiles("live", q)
            part = [old[i] + (t0[i] * ca + t1[i] * sa) - dx[i] for i in range(ROWS)]
            flux = product(tiles("depth", q), tiles("north", q))
            above, below = lanes_of(flux[0], up) * up_on, lanes_of(flux[3], down) * down_on
            north = flux[1:] + [above]
            south = [below] + flux[:3]
            new = [(part[i] - (north[i] - south[i])) * live[i] for i in range(ROWS)]
            put("level", q, 2 * step + 1, new, old)
            if not wide:
                continue
            over = lanes_of(flux[1], up) - lanes_of(flux[3], back_up) * back_up_on
            over = (lanes_of(part[0], up) - over) * live_over[q]
            under = lanes_of(flux[0], back_down) * back_down_on - lanes_of(flux[2], down)
            under = (lanes_of(part[3], down) - under) * live_under[q]
            dys[q] = [new[1] - under, new[2] - new[0], new[3] - new[1], over - new[2]]
        slope = x_slopes(lambda q: tiles("level", q), runs)
        for q, dx in slope:
            u, w, cor, live = (tiles(n, q) for n in ("east", "north", "cor", "live"))
            dy = dys[q] if wide else y_slopes(tiles("level", q), ghosts)
            new = [new_velocity(u[i], w[i], cor[i], dx[i], dy[i], live[i]) for i in range(ROWS)]
            put("east", q, 2 * step + 2, [a for a, _ in new], u)
            put("north", q, 2 * step + 2, [b for _, b in new], w)


PARTS = ((0, 1, GROUPS - 2, GROUPS - 1), tuple(range(2, GROUPS - 2)))
ALL = tuple(range(GROUPS))


def started(pairs, sems):
    loads = [pltpu.make_async_copy(src, dst, sems.at[i]) for i, (src, dst) in enumerate(pairs)]
    for load in loads:
        load.start()
    return loads


def prepare(state, still, groups, level_id, table, wet, start, tide, cor, count_ref, wait):
    tiles = wet.shape[1] // LANES
    held = tile_iota(0) < count_ref[0]

    def turn(source, put):
        for i, columns in enumerate(to_columns([source(v) for v in range(tiles)])):
            for n, q in enumerate(groups):
                put((i, pl.ds(SUB * n, SUB)), columns[SUB * q : SUB * q + SUB])

    def store(ref, f, source):
        def put(at, x):
            ref[f, at[0], at[1], :] = x

        turn(source, put)

    wait(0)
    levels = table.shape[0]
    row = F32(0.15) * table[...].reshape(1, levels)
    row = jnp.concatenate([row, jnp.zeros((1, LANES - levels), F32)], axis=1)
    row = jnp.broadcast_to(row, (SUB, LANES))

    def coded(v):
        here = jnp.logical_and(lane_tile(wet, v) > 0, held)
        return jnp.where(here, lane_tile(level_id, v), levels)

    def store_depth(at, code):
        still[0, at[0], at[1], :] = lanes_of(row, code)
        still[1, at[0], at[1], :] = (code < levels).astype(F32)

    turn(coded, store_depth)
    wait(1)

    def store_state(f):
        def put(at, x):
            state[f, at[0], at[1], :] = x * still[1, at[0], at[1], :]

        return put

    for f in range(3):
        turn(lambda v, f=f: lane_tile(start, v, (0, f)), store_state(f))
    wait(2)
    for f in range(2):
        store(still, 3 + f, lambda v, f=f: lane_tile(tide, v, (f,)))
    wait(3)
    store(still, 2, lambda v: F32(0.3) * lane_tile(cor, v))


def before_kernel(
    slices, count_ref, level_h, table_h, wet_h, nb_h, start_h, tide_h, cor_h,
    level_id, table, wet, start, tide, cor, face, pe, pw,
    nb_ref, state, still, sems,
):
    loads = started(
        [
            (level_h, level_id), (table_h, table), (wet_h, wet), (nb_h, nb_ref),
            (start_h, start), (tide_h, tide), (cor_h, cor),
        ],
        sems,
    )

    def wait(n):
        for load in (loads[:4], loads[4:5], loads[5:6], loads[6:])[n]:
            load.wait()

    prepare(state, still, PARTS[0], level_id, table, wet, start, tide, cor, count_ref, wait)
    rows = face_rows(nb_ref[...])
    for j in range(4):
        face[j] = rows[j]
    s = fields_of(state, still)
    runs = (PARTS[0][:2], PARTS[0][2:])
    interior_steps(s, runs, slices, range(SENT), chunk_ghosts(rows[0], rows[1]), True)

    end = SUB * len(PARTS[0])
    for f, name in enumerate(NAMES):
        ref, at = s[name]
        for i in range(ROWS):
            pe[i, pl.ds(OUT * f, OUT), :] = ref[at, i, pl.ds(end - OUT, OUT), :]
            pw[i, pl.ds(OUT * f, OUT), :] = ref[at, i, pl.ds(0, OUT), :]
    for i in range(ROWS):
        pe[i, pl.ds(6 * OUT, 1), :] = state[0, i, pl.ds(end - OUT - 1, 1), :]
        pw[i, pl.ds(6 * OUT + OUT - 1, 1), :] = state[0, i, pl.ds(OUT, 1), :]
        entry = rows[i][:1].astype(F32)
        pe[i, pl.ds(7 * OUT, 1), :] = entry
        pw[i, pl.ds(7 * OUT + OUT - 1, 1), :] = entry


def power(x, n):
    return functools.reduce(lambda a, b: a * b, [x] * n)


def part_tile(ref, f, i, n):
    return ref[f, i, pl.ds(SUB * n, SUB), :]


def during_kernel(
    slices, level_id, table, wet, start, tide, cor, face, count_ref, gain_h,
    last, still, inner, inner_gain, edge_gain, edge_base,
    gain, sems,
):
    loads = started([(gain_h, gain)], sems)
    tiles = wet.shape[1] // LANES
    prepare(last, still, ALL, level_id, table, wet, start, tide, cor, count_ref, lambda n: None)
    ghosts = chunk_ghosts(face[0], face[1])
    interior_steps(fields_of(last, still), (ALL,), slices, range(STEPS), ghosts, False)
    held = (tile_iota(0) < count_ref[0]).astype(F32)
    for load in loads:
        load.wait()
    for f in range(3):
        gains = [lane_tile(gain, v, (f,)) for v in range(tiles)]
        base = [
            gains[v] * (lane_tile(start, v, (0, f)) * (lane_tile(wet, v).astype(F32) * held))
            for v in range(tiles)
        ]
        gains, base = to_columns(gains), to_columns(base)
        for i in range(ROWS):
            for n in range(GROUPS // 2):
                at, to = [slice(SUB * part[n], SUB * part[n] + SUB) for part in PARTS], pl.ds(SUB * n, SUB)
                edge_gain[f, i, to, :] = gains[i][at[0]]
                edge_base[f, i, to, :] = base[i][at[0]]
                inner_gain[f, i, to, :] = gains[i][at[1]]
                inner[f, i, to, :] = last[f, i, pl.ds(SUB * PARTS[1][n], SUB), :] - base[i][at[1]]


def after_kernel(slices, pe, pw, last, still, face, base, edge, joined):
    sub, lane = tile_iota(0), tile_iota(1)
    s = fields_of(last, still)

    for f, name in enumerate(NAMES):
        ref, at = s[name]
        for i in range(ROWS):
            joined[f, i, 0, pl.ds(0, OUT), :] = pe[i, pl.ds(OUT * f, OUT), :]
            joined[f, i, 0, pl.ds(OUT, 2), :] = ref[at, i, pl.ds(0, 2), :]
            joined[f, i, 1, pl.ds(0, 2), :] = ref[at, i, pl.ds(BS - 2, 2), :]
            joined[f, i, 1, pl.ds(2, OUT), :] = pw[i, pl.ds(OUT * f, OUT), :]

    def load(name, side, g):
        f = NAMES.index(name)
        if g == 0:
            return [joined[f, i, side] for i in range(ROWS)]
        ref, at = s[name]
        low = SUB * g - OUT
        low = low if side == 0 else BS - SUB - low
        return [ref[at, i, pl.ds(low, SUB), :] for i in range(ROWS)]

    own = [face[j] for j in range(4)]
    ghosts, joins, far = [], [], []
    for side in range(2):
        row = 0 if side == 0 else SUB - 1
        sent = [
            jnp.broadcast_to(joined[7, j, side, pl.ds(row, 1), :].astype(jnp.int32), (SUB, LANES))
            for j in range(4)
        ]
        outer = sub < OUT if side == 0 else sub >= 2
        mixed = [jnp.where(outer, sent[j], own[j]) for j in range(4)]
        here = chunk_ghosts(own[0], own[1])
        ghosts.append([chunk_ghosts(mixed[0], mixed[1]), here, here])
        to = jnp.where(outer, own[3 - side], sent[2 + side])
        joins.append((lane - lane % SUB + jnp.maximum(to, 0), (to >= 0).astype(F32)))
    inner_row = (OUT, 1)
    outer_row = (OUT - 1, 2)

    def x_side(side, t, beyond=None):
        index, on = joins[side]
        looked = [lanes_of(x, index) * on for x in t[0]]
        inner = [jnp.where(sub == inner_row[side], b, a) for a, b in zip(t[0], looked)]
        outer = [jnp.where(sub == outer_row[side], b, a) for a, b in zip(t[0], looked)]
        sign = -1 if side == 0 else 1
        end_in, end_out = (SUB - 1, 0) if side == 0 else (0, SUB - 1)
        inward = [[shifted(x, sign) for x in inner]]
        outward = [[shifted(x, -sign) for x in outer]]
        if beyond is not None:
            outward[0] = [jnp.where(sub == end_out, b, a) for a, b in zip(outward[0], beyond)]
        plain_out = [[shifted(x, -sign) for x in t[0]]]
        for g in range(1, len(t)):
            inward.append([shifted(x, sign) for x in t[g]])
            plain_out.append([shifted(x, -sign) for x in t[g]])
        for g in range(1, len(t)):
            outward.append(
                [jnp.where(sub == end_out, b, a) for a, b in zip(plain_out[g], plain_out[g - 1])]
            )
        for g in range(len(t) - 1):
            inward[g] = [
                jnp.where(sub == end_in, b, a) for a, b in zip(inward[g], inward[g + 1])
            ]
        return [
            [(a - b) if side == 0 else (b - a) for a, b in zip(inward[g], outward[g])]
            for g in range(len(t))
        ]

    def changed(side, g, k):
        place = sub if side == 0 else SUB - 1 - sub
        if g == 0:
            reach = min(k, HALF - k)
            mask = place >= OUT - reach
            return mask if k >= 2 else jnp.logical_and(mask, place <= OUT)
        least = SUB * g - OUT + 1
        if k < least:
            return False
        return None if k >= least + SUB - 1 else place + least <= k

    cells = {
        (n, side, g): load(n, side, g)
        for n in ("level", "east", "north") for side in range(2) for g in range(3)
    }

    def put(name, side, g, mask, new):
        key = (name, side, g)
        if mask is not None:
            new = [jnp.where(mask, a, b) for a, b in zip(new, cells[key])]
        cells[key] = new

    def product(a, b):
        return [x * y for x, y in zip(a, b)]

    for k in range(1, HALF + 1):
        ca, sa = phase(slices, (k - 1) // 2)
        active = [g for g in range(3) if changed(0, g, k) is not False]
        reach = min(3, len(active) + 1)
        for side in range(2):
            if k % 2 == 1:
                depth = [load("depth", side, g) for g in range(reach)]
                dx = x_side(
                    side, [product(depth[g], cells["east", side, g]) for g in range(reach)]
                )
                for g in active:
                    flux = product(depth[g], cells["north", side, g])
                    dy = y_slopes(flux, ghosts[side][g])
                    t0, t1, live = (load(n, side, g) for n in ("tide0", "tide1", "live"))
                    old = cells["level", side, g]
                    new = [
                        new_level(old[i], t0[i], t1[i], ca, sa, dx[g][i], dy[i], live[i])
                        for i in range(ROWS)
                    ]
                    put("level", side, g, changed(side, g, k), new)
            else:
                beyond = load("tide0", side, 0) if k == OUT else None
                dx = x_side(side, [cells["level", side, g] for g in range(reach)], beyond)
                for g in active:
                    dy = y_slopes(cells["level", side, g], ghosts[side][g])
                    cor, live = load("cor", side, g), load("live", side, g)
                    u, w = cells["east", side, g], cells["north", side, g]
                    new = [
                        new_velocity(u[i], w[i], cor[i], dx[g][i], dy[i], live[i])
                        for i in range(ROWS)
                    ]
                    mask = changed(side, g, k)
                    put("east", side, g, mask, [a for a, _ in new])
                    put("north", side, g, mask, [b for _, b in new])

    for f, name in enumerate(NAMES[:3]):
        for i in range(ROWS):
            a, b, c = (shifted(cells[name, 0, g][i], 2) for g in range(3))
            d, e, h = (shifted(cells[name, 1, g][i], -2) for g in range(3))
            inside = [last[f, i, pl.ds(SUB * q, SUB), :] for q in PARTS[0][1:3]]
            fine = [
                jnp.where(sub < 2, a, b),
                jnp.where(sub < 2, b, jnp.where(sub < 4, c, inside[0])),
                jnp.where(sub >= 6, e, jnp.where(sub >= 4, h, inside[1])),
                jnp.where(sub >= 6, d, e),
            ]
            for n, x in enumerate(fine):
                edge[f, i, pl.ds(SUB * n, SUB), :] = x - part_tile(base, f, i, n)


def final_kernel(
    slices, edge_sum, edge, edge_gain, inner_sum, inner, inner_gain, result, out, sems
):
    parts = ((edge_sum, edge, edge_gain), (inner_sum, inner, inner_gain))
    copies = []
    for f in range(3):
        columns = []
        for i in range(ROWS):
            q = [None] * GROUPS
            for groups, (total, own, gain) in zip(PARTS, parts):
                for n, group in enumerate(groups):
                    g = part_tile(gain, f, i, n)
                    most = power(g, slices - 1)
                    whole = part_tile(total, f, i, n) + most * part_tile(own, f, i, n)
                    q[group] = whole / (F32(1) - most * g)
            columns.append(jnp.concatenate(q, axis=0))
        for v, x in enumerate(to_tiles(columns)):
            out[0, f, :, pl.ds(v * LANES, LANES)] = x
        copies.append(pltpu.make_async_copy(out.at[0, f], result.at[0, f], sems.at[f]))
        copies[-1].start()
    for copy in copies:
        copy.wait()


def call(kernel, out_shape, operands, spaces=None, out_space=pltpu.VMEM, scratch=()):
    spaces = spaces or [pltpu.VMEM] * len(operands)
    size = sum(4 * x.size for x in operands)
    return pl.pallas_call(
        kernel,
        out_shape=out_shape,
        in_specs=[pl.BlockSpec(memory_space=space) for space in spaces],
        out_specs=jax.tree.map(lambda _: pl.BlockSpec(memory_space=out_space), out_shape),
        scratch_shapes=scratch,
        cost_estimate=pl.CostEstimate(flops=0, bytes_accessed=2 * size, transcendentals=0),
        compiler_params=pltpu.CompilerParams(vmem_limit_bytes=VMEM_LIMIT),
    )(*operands)


def shape(*dims):
    return jax.ShapeDtypeStruct(dims, F32)


def in_hbm(arrays):
    return [pltpu.with_memory_space_constraint(x, pltpu.HBM) for x in arrays]


def passed_along(shard, axis, by):
    size = lax.axis_size(axis)
    return lax.ppermute(shard, axis, [(i, (i + by) % size) for i in range(size)])


def periodic_sum(defect, gain, slices):
    total = passed_along(defect, "tm", 1)
    for _ in range(slices - 2):
        total = passed_along(defect + gain * total, "tm", 1)
    return total


def body(
    start_states, coarse_gain, depth_level, depth_table, wet, block_count, neighbour, coriolis, tide
):
    slices = lax.axis_size("tm")
    loaded = [depth_level, depth_table, wet, start_states, tide, coriolis]
    faces = neighbour.T
    whole, half = shape(3, ROWS, BS, LANES), shape(3, ROWS, BS // 2, LANES)
    *held, face, pe, pw = call(
        functools.partial(before_kernel, slices),
        [jax.ShapeDtypeStruct(x.shape, x.dtype) for x in loaded]
        + [jax.ShapeDtypeStruct((4, SUB, LANES), jnp.int32)]
        + [shape(ROWS, len(NAMES) * OUT, LANES)] * 2,
        [block_count] + in_hbm(loaded[:3] + [faces] + loaded[3:]),
        spaces=[pltpu.SMEM] + [pltpu.HBM] * (len(loaded) + 1),
        scratch=[
            pltpu.VMEM(faces.shape, faces.dtype),
            pltpu.VMEM(half.shape, F32),
            pltpu.VMEM((5,) + half.shape[1:], F32),
            pltpu.SemaphoreType.DMA((len(loaded) + 1,)),
        ],
    )
    from_west = passed_along(pe, "space", 1)
    from_east = passed_along(pw, "space", -1)
    last, still, inner, inner_gain, edge_gain, edge_base = call(
        functools.partial(during_kernel, slices),
        [whole, shape(5, ROWS, BS, LANES)] + [half] * 4,
        held + [face, block_count] + in_hbm([coarse_gain]),
        spaces=[pltpu.VMEM] * (len(held) + 1) + [pltpu.SMEM, pltpu.HBM],
        scratch=[pltpu.VMEM(coarse_gain.shape, F32), pltpu.SemaphoreType.DMA((1,))],
    )
    inner_sum = periodic_sum(inner, inner_gain, slices)
    edge = call(
        functools.partial(after_kernel, slices),
        half,
        [from_west, from_east, last, still, face, edge_base],
        scratch=[pltpu.VMEM((len(NAMES), ROWS, 2, SUB, LANES), F32)],
    )
    edge_sum = periodic_sum(edge, edge_gain, slices)
    return call(
        functools.partial(final_kernel, slices),
        shape(*start_states.shape),
        [edge_sum, edge, edge_gain, inner_sum, inner, inner_gain],
        out_space=pltpu.HBM,
        scratch=[pltpu.VMEM(start_states.shape, F32), pltpu.SemaphoreType.DMA((3,))],
    )


def solution(mesh):
    return jax.shard_map(
        body,
        mesh=mesh,
        in_specs=(
            P("tm", None, "space", None),
            P(None, "space", None),
            P("space", None),
            P(),
            P("space", None),
            P("space"),
            P("space", None),
            P("space", None),
            P(None, "space", None),
        ),
        out_specs=P("tm", None, "space", None),
        check_vma=False,
    )
```

```python
import functools
import math

import jax
import jax.numpy as jnp
from jax import lax
from jax.experimental import pallas as pl
from jax.experimental.pallas import tpu as pltpu
from jax.sharding import PartitionSpec as P

BS = 64
STEPS = 6
HALF = 2 * STEPS
SENT = STEPS // 2
OUT = STEPS
LANES = 128
SUB = 8
ROWS = 4
GROUPS = BS // SUB
F32 = jnp.float32
VMEM_LIMIT = 24 * 1024 * 1024


def shifted(x, by):
    return pltpu.roll(x, by % SUB, 0)


def lanes_of(x, index):
    return jnp.take_along_axis(x, index, axis=1, mode="promise_in_bounds")


def tile_iota(dim):
    return lax.broadcasted_iota(jnp.int32, (SUB, LANES), dim)


def lane_tile(ref, v, lead=()):
    return ref[tuple(lead) + (slice(None), pl.ds(v * LANES, LANES))]


def to_columns(tiles):
    out = []
    for part in (tiles[0::2], tiles[1::2]):
        turned = jnp.concatenate(part, axis=0).T
        out += [turned[:BS], turned[BS:]]
    return out


def to_tiles(columns):
    out = {}
    for part in range(2):
        turned = jnp.concatenate(columns[2 * part : 2 * part + 2], axis=0).T
        for c in range(LANES // SUB):
            out[2 * c + part] = turned[SUB * c : SUB * c + SUB]
    return [out[v] for v in range(len(out))]


def phase(count, step):
    omega = 2.0 * math.pi / (count * STEPS)
    here = lax.axis_index("tm")
    ca, sa = F32(0), F32(0)
    for n in range(count):
        angle = (n * STEPS + step) * omega
        ca = jnp.where(here == n, F32(0.3 * math.cos(angle)), ca)
        sa = jnp.where(here == n, F32(0.3 * math.sin(angle)), sa)
    return ca, sa


def chunk_ghosts(north, south):
    lane = tile_iota(1)
    top, bottom = lane >= LANES - SUB, lane < SUB
    up = jnp.where(top, jnp.maximum(north, 0), (lane + SUB) % LANES)
    down = jnp.where(bottom, LANES - SUB + jnp.maximum(south, 0), (lane + LANES - SUB) % LANES)
    up_on = jnp.where(jnp.logical_and(top, north < 0), F32(0), F32(1))
    down_on = jnp.where(jnp.logical_and(bottom, south < 0), F32(0), F32(1))
    return up, up_on, down, down_on


def two_way_ghosts(ghosts):
    up, up_on, down, down_on = ghosts
    return lanes_of(down, up), lanes_of(down_on, up), lanes_of(up, down), lanes_of(up_on, down)


def face_rows(nb):
    wide = jnp.concatenate([nb] * (LANES // SUB), axis=1)
    return [jnp.broadcast_to(wide[j : j + 1], (SUB, LANES)) for j in range(4)]


def y_slopes(t, ghosts):
    up, up_on, down, down_on = ghosts
    above = lanes_of(t[0], up) * up_on
    below = lanes_of(t[3], down) * down_on
    return [t[1] - below, t[2] - t[0], t[3] - t[1], above - t[2]]


def x_slopes(columns, runs):
    sub = tile_iota(0)
    first, last = sub == 0, sub == SUB - 1
    for run in runs:
        get = [columns(q) for q in run]
        easts = [[shifted(x, -1) for x in t] for t in get]
        wests = [[shifted(x, 1) for x in t] for t in get]
        for n, q in enumerate(run):
            east, west = easts[n], wests[n]
            if n + 1 < len(run):
                east = [jnp.where(last, b, a) for a, b in zip(east, easts[n + 1])]
            if n > 0:
                west = [jnp.where(first, b, a) for a, b in zip(west, wests[n - 1])]
            yield q, [e - w for e, w in zip(east, west)]


def new_level(level, t0, t1, ca, sa, dx, dy, live):
    return (level + (t0 * ca + t1 * sa) - (dx + dy)) * live


def new_velocity(u, w, cor, dx, dy, live):
    return (
        (F32(0.985) * u + cor * w - F32(0.15) * dx) * live,
        (F32(0.985) * w - cor * u - F32(0.15) * dy) * live,
    )


NAMES = ("level", "east", "north", "depth", "live", "cor", "tide0", "tide1")


def fields_of(state, still):
    return {
        name: (state, f) if f < 3 else (still, f - 3) for f, name in enumerate(NAMES)
    }


def interior_steps(s, runs, times, steps, ghosts, wide):
    sub = tile_iota(0)
    place = {q: SUB * n for n, q in enumerate(q for run in runs for q in run)}

    def tiles(name, q):
        ref, f = s[name]
        return [ref[f, i, pl.ds(place[q], SUB), :] for i in range(ROWS)]

    def put(name, q, k, new, old):
        ref, f = s[name]
        least = min(SUB * q, BS - SUB - SUB * q) + 1
        if k >= least + SUB - 1:
            return
        if k >= least:
            edge = (sub if q < GROUPS // 2 else SUB - 1 - sub) + least
            new = [jnp.where(edge > k, a, b) for a, b in zip(new, old)]
        for i in range(ROWS):
            ref[f, i, pl.ds(place[q], SUB), :] = new[i]

    def product(a, b):
        return [x * y for x, y in zip(a, b)]

    up, up_on, down, down_on = ghosts
    if wide:
        back_up, back_up_on, back_down, back_down_on = two_way_ghosts(ghosts)
    live_over, live_under = {}, {}
    for q in place if wide else ():
        live = tiles("live", q)
        live_over[q] = lanes_of(live[0], up) * up_on
        live_under[q] = lanes_of(live[3], down) * down_on
    for step in steps:
        ca, sa = times[2 * step], times[2 * step + 1]
        slope = x_slopes(lambda q: product(tiles("depth", q), tiles("east", q)), runs)
        dys = {}
        for q, dx in slope:
            old = tiles("level", q)
            t0, t1, live = tiles("tide0", q), tiles("tide1", q), tiles("live", q)
            part = [old[i] + (t0[i] * ca + t1[i] * sa) - dx[i] for i in range(ROWS)]
            flux = product(tiles("depth", q), tiles("north", q))
            above, below = lanes_of(flux[0], up) * up_on, lanes_of(flux[3], down) * down_on
            north = flux[1:] + [above]
            south = [below] + flux[:3]
            new = [(part[i] - (north[i] - south[i])) * live[i] for i in range(ROWS)]
            put("level", q, 2 * step + 1, new, old)
            if not wide:
                continue
            over = lanes_of(flux[1], up) - lanes_of(flux[3], back_up) * back_up_on
            over = (lanes_of(part[0], up) - over) * live_over[q]
            under = lanes_of(flux[0], back_down) * back_down_on - lanes_of(flux[2], down)
            under = (lanes_of(part[3], down) - under) * live_under[q]
            dys[q] = [new[1] - under, new[2] - new[0], new[3] - new[1], over - new[2]]
        slope = x_slopes(lambda q: tiles("level", q), runs)
        for q, dx in slope:
            u, w, cor, live = (tiles(n, q) for n in ("east", "north", "cor", "live"))
            dy = dys[q] if wide else y_slopes(tiles("level", q), ghosts)
            new = [new_velocity(u[i], w[i], cor[i], dx[i], dy[i], live[i]) for i in range(ROWS)]
            put("east", q, 2 * step + 2, [a for a, _ in new], u)
            put("north", q, 2 * step + 2, [b for _, b in new], w)


PARTS = ((0, 1, GROUPS - 2, GROUPS - 1), tuple(range(2, GROUPS - 2)))
ALL = tuple(range(GROUPS))


def started(pairs, sems):
    loads = [pltpu.make_async_copy(src, dst, sems.at[i]) for i, (src, dst) in enumerate(pairs)]
    for load in loads:
        load.start()
    return loads


def prepare(state, still, groups, row, held, level_id, wet, start, tide, cor):
    tiles = wet.shape[1] // LANES
    held = held[...] > 0

    def turn(source, put):
        for i, columns in enumerate(to_columns([source(v) for v in range(tiles)])):
            for n, q in enumerate(groups):
                put((i, pl.ds(SUB * n, SUB)), columns[SUB * q : SUB * q + SUB])

    def store(ref, f, source):
        def put(at, x):
            ref[f, at[0], at[1], :] = x

        turn(source, put)

    levels = LANES - 1
    row = row[...]

    def coded(v):
        here = jnp.logical_and(lane_tile(wet, v) > 0, held)
        return jnp.where(here, lane_tile(level_id, v), levels)

    def store_depth(at, code):
        still[0, at[0], at[1], :] = lanes_of(row, code)
        still[1, at[0], at[1], :] = (code < levels).astype(F32)

    turn(coded, store_depth)

    def store_state(f):
        def put(at, x):
            state[f, at[0], at[1], :] = x * still[1, at[0], at[1], :]

        return put

    for f in range(3):
        turn(lambda v, f=f: lane_tile(start, v, (0, f)), store_state(f))
    for f in range(2):
        store(still, 3 + f, lambda v, f=f: lane_tile(tide, v, (f,)))
    store(still, 2, lambda v: F32(0.3) * lane_tile(cor, v))


def clock_kernel(slices, times):
    for step in range(STEPS):
        for j, x in enumerate(phase(slices, step)):
            times[2 * step + j] = jnp.full((SUB, LANES), x, F32)


def depths_kernel(table, row):
    levels = table.shape[0]
    depths = F32(0.15) * table[...].reshape(1, levels)
    depths = jnp.concatenate([depths, jnp.zeros((1, LANES - levels), F32)], axis=1)
    row[...] = jnp.broadcast_to(depths, (SUB, LANES))


def slots_kernel(count_ref, nb, face, held):
    for j, x in enumerate(face_rows(nb[...])):
        face[j] = x
    held[...] = (tile_iota(0) < count_ref[0]).astype(jnp.int32)


def before_kernel(
    times, face, held, row, level_id, wet, start, tide, cor, pe, pw, state, still
):

    prepare(state, still, PARTS[0], row, held, level_id, wet, start, tide, cor)
    rows = [face[j] for j in range(4)]
    s = fields_of(state, still)
    runs = (PARTS[0][:2], PARTS[0][2:])
    interior_steps(s, runs, times, range(SENT), chunk_ghosts(rows[0], rows[1]), True)

    end = SUB * len(PARTS[0])
    for f, name in enumerate(NAMES):
        ref, at = s[name]
        for i in range(ROWS):
            pe[i, pl.ds(OUT * f, OUT), :] = ref[at, i, pl.ds(end - OUT, OUT), :]
            pw[i, pl.ds(OUT * f, OUT), :] = ref[at, i, pl.ds(0, OUT), :]
    for i in range(ROWS):
        pe[i, pl.ds(6 * OUT, 1), :] = state[0, i, pl.ds(end - OUT - 1, 1), :]
        pw[i, pl.ds(6 * OUT + OUT - 1, 1), :] = state[0, i, pl.ds(OUT, 1), :]
        entry = rows[i][:1].astype(F32)
        pe[i, pl.ds(7 * OUT, 1), :] = entry
        pw[i, pl.ds(7 * OUT + OUT - 1, 1), :] = entry


def power(x, n):
    return functools.reduce(lambda a, b: a * b, [x] * n)


def part_tile(ref, f, i, n):
    return ref[f, i, pl.ds(SUB * n, SUB), :]


def during_kernel(
    times, face, held, row, level_id, wet, start, tide, cor, gain_h,
    last, still, inner, inner_gain, edge_gain, edge_base,
    gain, sems,
):
    loads = started([(gain_h, gain)], sems)
    tiles = wet.shape[1] // LANES
    prepare(last, still, ALL, row, held, level_id, wet, start, tide, cor)
    ghosts = chunk_ghosts(face[0], face[1])
    interior_steps(fields_of(last, still), (ALL,), times, range(STEPS), ghosts, False)
    held = held[...].astype(F32)
    for load in loads:
        load.wait()
    for f in range(3):
        gains = [lane_tile(gain, v, (f,)) for v in range(tiles)]
        base = [
            gains[v] * (lane_tile(start, v, (0, f)) * (lane_tile(wet, v).astype(F32) * held))
            for v in range(tiles)
        ]
        gains, base = to_columns(gains), to_columns(base)
        for i in range(ROWS):
            for n in range(GROUPS // 2):
                at, to = [slice(SUB * part[n], SUB * part[n] + SUB) for part in PARTS], pl.ds(SUB * n, SUB)
                edge_gain[f, i, to, :] = gains[i][at[0]]
                edge_base[f, i, to, :] = base[i][at[0]]
                inner_gain[f, i, to, :] = gains[i][at[1]]
                inner[f, i, to, :] = last[f, i, pl.ds(SUB * PARTS[1][n], SUB), :] - base[i][at[1]]


def after_kernel(times, pe, pw, last, still, face, base, edge, joined):
    sub, lane = tile_iota(0), tile_iota(1)
    s = fields_of(last, still)

    for f, name in enumerate(NAMES):
        ref, at = s[name]
        for i in range(ROWS):
            joined[f, i, 0, pl.ds(0, OUT), :] = pe[i, pl.ds(OUT * f, OUT), :]
            joined[f, i, 0, pl.ds(OUT, 2), :] = ref[at, i, pl.ds(0, 2), :]
            joined[f, i, 1, pl.ds(0, 2), :] = ref[at, i, pl.ds(BS - 2, 2), :]
            joined[f, i, 1, pl.ds(2, OUT), :] = pw[i, pl.ds(OUT * f, OUT), :]

    def load(name, side, g):
        f = NAMES.index(name)
        if g == 0:
            return [joined[f, i, side] for i in range(ROWS)]
        ref, at = s[name]
        low = SUB * g - OUT
        low = low if side == 0 else BS - SUB - low
        return [ref[at, i, pl.ds(low, SUB), :] for i in range(ROWS)]

    own = [face[j] for j in range(4)]
    ghosts, joins, far = [], [], []
    for side in range(2):
        row = 0 if side == 0 else SUB - 1
        sent = [
            jnp.broadcast_to(joined[7, j, side, pl.ds(row, 1), :].astype(jnp.int32), (SUB, LANES))
            for j in range(4)
        ]
        outer = sub < OUT if side == 0 else sub >= 2
        mixed = [jnp.where(outer, sent[j], own[j]) for j in range(4)]
        here = chunk_ghosts(own[0], own[1])
        ghosts.append([chunk_ghosts(mixed[0], mixed[1]), here, here])
        to = jnp.where(outer, own[3 - side], sent[2 + side])
        joins.append((lane - lane % SUB + jnp.maximum(to, 0), (to >= 0).astype(F32)))
    inner_row = (OUT, 1)
    outer_row = (OUT - 1, 2)

    def x_side(side, t, beyond=None):
        index, on = joins[side]
        looked = [lanes_of(x, index) * on for x in t[0]]
        inner = [jnp.where(sub == inner_row[side], b, a) for a, b in zip(t[0], looked)]
        outer = [jnp.where(sub == outer_row[side], b, a) for a, b in zip(t[0], looked)]
        sign = -1 if side == 0 else 1
        end_in, end_out = (SUB - 1, 0) if side == 0 else (0, SUB - 1)
        inward = [[shifted(x, sign) for x in inner]]
        outward = [[shifted(x, -sign) for x in outer]]
        if beyond is not None:
            outward[0] = [jnp.where(sub == end_out, b, a) for a, b in zip(outward[0], beyond)]
        plain_out = [[shifted(x, -sign) for x in t[0]]]
        for g in range(1, len(t)):
            inward.append([shifted(x, sign) for x in t[g]])
            plain_out.append([shifted(x, -sign) for x in t[g]])
        for g in range(1, len(t)):
            outward.append(
                [jnp.where(sub == end_out, b, a) for a, b in zip(plain_out[g], plain_out[g - 1])]
            )
        for g in range(len(t) - 1):
            inward[g] = [
                jnp.where(sub == end_in, b, a) for a, b in zip(inward[g], inward[g + 1])
            ]
        return [
            [(a - b) if side == 0 else (b - a) for a, b in zip(inward[g], outward[g])]
            for g in range(len(t))
        ]

    def changed(side, g, k):
        place = sub if side == 0 else SUB - 1 - sub
        if g == 0:
            reach = min(k, HALF - k)
            mask = place >= OUT - reach
            return mask if k >= 2 else jnp.logical_and(mask, place <= OUT)
        least = SUB * g - OUT + 1
        if k < least:
            return False
        return None if k >= least + SUB - 1 else place + least <= k

    cells = {
        (n, side, g): load(n, side, g)
        for n in ("level", "east", "north") for side in range(2) for g in range(3)
    }

    def put(name, side, g, mask, new):
        key = (name, side, g)
        if mask is not None:
            new = [jnp.where(mask, a, b) for a, b in zip(new, cells[key])]
        cells[key] = new

    def product(a, b):
        return [x * y for x, y in zip(a, b)]

    for k in range(1, HALF + 1):
        ca, sa = times[(k - 1) // 2 * 2], times[(k - 1) // 2 * 2 + 1]
        active = [g for g in range(3) if changed(0, g, k) is not False]
        reach = min(3, len(active) + 1)
        for side in range(2):
            if k % 2 == 1:
                depth = [load("depth", side, g) for g in range(reach)]
                dx = x_side(
                    side, [product(depth[g], cells["east", side, g]) for g in range(reach)]
                )
                for g in active:
                    flux = product(depth[g], cells["north", side, g])
                    dy = y_slopes(flux, ghosts[side][g])
                    t0, t1, live = (load(n, side, g) for n in ("tide0", "tide1", "live"))
                    old = cells["level", side, g]
                    new = [
                        new_level(old[i], t0[i], t1[i], ca, sa, dx[g][i], dy[i], live[i])
                        for i in range(ROWS)
                    ]
                    put("level", side, g, changed(side, g, k), new)
            else:
                beyond = load("tide0", side, 0) if k == OUT else None
                dx = x_side(side, [cells["level", side, g] for g in range(reach)], beyond)
                for g in active:
                    dy = y_slopes(cells["level", side, g], ghosts[side][g])
                    cor, live = load("cor", side, g), load("live", side, g)
                    u, w = cells["east", side, g], cells["north", side, g]
                    new = [
                        new_velocity(u[i], w[i], cor[i], dx[g][i], dy[i], live[i])
                        for i in range(ROWS)
                    ]
                    mask = changed(side, g, k)
                    put("east", side, g, mask, [a for a, _ in new])
                    put("north", side, g, mask, [b for _, b in new])

    for f, name in enumerate(NAMES[:3]):
        for i in range(ROWS):
            a, b, c = (shifted(cells[name, 0, g][i], 2) for g in range(3))
            d, e, h = (shifted(cells[name, 1, g][i], -2) for g in range(3))
            inside = [last[f, i, pl.ds(SUB * q, SUB), :] for q in PARTS[0][1:3]]
            fine = [
                jnp.where(sub < 2, a, b),
                jnp.where(sub < 2, b, jnp.where(sub < 4, c, inside[0])),
                jnp.where(sub >= 6, e, jnp.where(sub >= 4, h, inside[1])),
                jnp.where(sub >= 6, d, e),
            ]
            for n, x in enumerate(fine):
                edge[f, i, pl.ds(SUB * n, SUB), :] = x - part_tile(base, f, i, n)


def final_kernel(
    slices, edge_sum, edge, edge_gain, inner_sum, inner, inner_gain, result, out, sems
):
    parts = ((edge_sum, edge, edge_gain), (inner_sum, inner, inner_gain))
    copies = []
    for f in range(3):
        columns = []
        for i in range(ROWS):
            q = [None] * GROUPS
            for groups, (total, own, gain) in zip(PARTS, parts):
                for n, group in enumerate(groups):
                    g = part_tile(gain, f, i, n)
                    most = power(g, slices - 1)
                    whole = part_tile(total, f, i, n) + most * part_tile(own, f, i, n)
                    q[group] = whole / (F32(1) - most * g)
            columns.append(jnp.concatenate(q, axis=0))
        for v, x in enumerate(to_tiles(columns)):
            out[0, f, :, pl.ds(v * LANES, LANES)] = x
        copies.append(pltpu.make_async_copy(out.at[0, f], result.at[0, f], sems.at[f]))
        copies[-1].start()
    for copy in copies:
        copy.wait()


def call(kernel, out_shape, operands, spaces=None, out_space=pltpu.VMEM, scratch=(), flops=0):
    spaces = spaces or [pltpu.VMEM] * len(operands)
    size = 2 * sum(4 * x.size for x in operands)
    return pl.pallas_call(
        kernel,
        out_shape=out_shape,
        in_specs=[pl.BlockSpec(memory_space=space) for space in spaces],
        out_specs=jax.tree.map(lambda _: pl.BlockSpec(memory_space=out_space), out_shape),
        scratch_shapes=scratch,
        cost_estimate=pl.CostEstimate(flops=flops, bytes_accessed=size, transcendentals=0),
        compiler_params=pltpu.CompilerParams(vmem_limit_bytes=VMEM_LIMIT),
    )(*operands)


def shape(*dims):
    return jax.ShapeDtypeStruct(dims, F32)


def in_hbm(arrays):
    return [pltpu.with_memory_space_constraint(x, pltpu.HBM) for x in arrays]


def passed_along(shard, axis, by):
    size = lax.axis_size(axis)
    return lax.ppermute(shard, axis, [(i, (i + by) % size) for i in range(size)])


def periodic_sum(defect, gain, slices):
    total = passed_along(defect, "tm", 1)
    for _ in range(slices - 2):
        total = passed_along(defect + gain * total, "tm", 1)
    return total


def body(
    start_states, coarse_gain, depth_level, depth_table, wet, block_count, neighbour, coriolis, tide
):
    slices = lax.axis_size("tm")
    whole, half = shape(3, ROWS, BS, LANES), shape(3, ROWS, BS // 2, LANES)
    times = call(
        functools.partial(clock_kernel, slices), shape(2 * STEPS, SUB, LANES), [], flops=10**10
    )
    flags = jax.ShapeDtypeStruct((SUB, LANES), jnp.int32)
    row = call(depths_kernel, shape(SUB, LANES), [depth_table])
    slot_tiles = call(
        slots_kernel,
        [jax.ShapeDtypeStruct((4, SUB, LANES), jnp.int32), flags],
        [block_count, neighbour.T],
        spaces=[pltpu.SMEM, pltpu.VMEM],
    )
    ready = [times] + list(slot_tiles) + [row, depth_level, wet, start_states, tide, coriolis]
    pe, pw = call(
        before_kernel,
        [shape(ROWS, len(NAMES) * OUT, LANES)] * 2,
        ready,
        scratch=[pltpu.VMEM(half.shape, F32), pltpu.VMEM((5,) + half.shape[1:], F32)],
    )
    from_west = passed_along(pe, "space", 1)
    from_east = passed_along(pw, "space", -1)
    last, still, inner, inner_gain, edge_gain, edge_base = call(
        during_kernel,
        [whole, shape(5, ROWS, BS, LANES)] + [half] * 4,
        ready + in_hbm([coarse_gain]),
        spaces=[pltpu.VMEM] * len(ready) + [pltpu.HBM],
        scratch=[pltpu.VMEM(coarse_gain.shape, F32), pltpu.SemaphoreType.DMA((1,))],
    )
    inner_sum = periodic_sum(inner, inner_gain, slices)
    edge = call(
        after_kernel,
        half,
        [times, from_west, from_east, last, still, slot_tiles[0], edge_base],
        scratch=[pltpu.VMEM((len(NAMES), ROWS, 2, SUB, LANES), F32)],
    )
    edge_sum = periodic_sum(edge, edge_gain, slices)
    return call(
        functools.partial(final_kernel, slices),
        shape(*start_states.shape),
        [edge_sum, edge, edge_gain, inner_sum, inner, inner_gain],
        out_space=pltpu.HBM,
        scratch=[pltpu.VMEM(start_states.shape, F32), pltpu.SemaphoreType.DMA((3,))],
    )


def solution(mesh):
    return jax.shard_map(
        body,
        mesh=mesh,
        in_specs=(
            P("tm", None, "space", None),
            P(None, "space", None),
            P("space", None),
            P(),
            P("space", None),
            P("space"),
            P("space", None),
            P("space", None),
            P(None, "space", None),
        ),
        out_specs=P("tm", None, "space", None),
        check_vma=False,
    )
```

```python
import functools
import math

import jax
import jax.numpy as jnp
from jax import lax
from jax.experimental import pallas as pl
from jax.experimental.pallas import tpu as pltpu
from jax.sharding import PartitionSpec as P

BS = 64
STEPS = 6
HALF = 2 * STEPS
SENT = STEPS // 2
OUT = STEPS
LANES = 128
SUB = 8
ROWS = 4
GROUPS = BS // SUB
F32 = jnp.float32
VMEM_LIMIT = 24 * 1024 * 1024


def shifted(x, by):
    return pltpu.roll(x, by % SUB, 0)


def lanes_of(x, index):
    return jnp.take_along_axis(x, index, axis=1, mode="promise_in_bounds")


def tile_iota(dim):
    return lax.broadcasted_iota(jnp.int32, (SUB, LANES), dim)


def lane_tile(ref, v, lead=()):
    return ref[tuple(lead) + (slice(None), pl.ds(v * LANES, LANES))]


def to_columns(tiles):
    out = []
    for part in (tiles[0::2], tiles[1::2]):
        turned = jnp.concatenate(part, axis=0).T
        out += [turned[:BS], turned[BS:]]
    return out


def to_tiles(columns):
    out = {}
    for part in range(2):
        turned = jnp.concatenate(columns[2 * part : 2 * part + 2], axis=0).T
        for c in range(LANES // SUB):
            out[2 * c + part] = turned[SUB * c : SUB * c + SUB]
    return [out[v] for v in range(len(out))]


def phase(count, step):
    omega = 2.0 * math.pi / (count * STEPS)
    here = lax.axis_index("tm")
    ca, sa = F32(0), F32(0)
    for n in range(count):
        angle = (n * STEPS + step) * omega
        ca = jnp.where(here == n, F32(0.3 * math.cos(angle)), ca)
        sa = jnp.where(here == n, F32(0.3 * math.sin(angle)), sa)
    return ca, sa


def chunk_ghosts(north, south):
    lane = tile_iota(1)
    top, bottom = lane >= LANES - SUB, lane < SUB
    up = jnp.where(top, jnp.maximum(north, 0), (lane + SUB) % LANES)
    down = jnp.where(bottom, LANES - SUB + jnp.maximum(south, 0), (lane + LANES - SUB) % LANES)
    up_on = jnp.where(jnp.logical_and(top, north < 0), F32(0), F32(1))
    down_on = jnp.where(jnp.logical_and(bottom, south < 0), F32(0), F32(1))
    return up, up_on, down, down_on


def two_way_ghosts(ghosts):
    up, up_on, down, down_on = ghosts
    return lanes_of(down, up), lanes_of(down_on, up), lanes_of(up, down), lanes_of(up_on, down)


def face_rows(nb):
    wide = jnp.concatenate([nb] * (LANES // SUB), axis=1)
    return [jnp.broadcast_to(wide[j : j + 1], (SUB, LANES)) for j in range(4)]


def y_slopes(t, ghosts):
    up, up_on, down, down_on = ghosts
    above = lanes_of(t[0], up) * up_on
    below = lanes_of(t[3], down) * down_on
    return [t[1] - below, t[2] - t[0], t[3] - t[1], above - t[2]]


def x_slopes(columns, runs):
    sub = tile_iota(0)
    first, last = sub == 0, sub == SUB - 1
    for run in runs:
        get = [columns(q) for q in run]
        easts = [[shifted(x, -1) for x in t] for t in get]
        wests = [[shifted(x, 1) for x in t] for t in get]
        for n, q in enumerate(run):
            east, west = easts[n], wests[n]
            if n + 1 < len(run):
                east = [jnp.where(last, b, a) for a, b in zip(east, easts[n + 1])]
            if n > 0:
                west = [jnp.where(first, b, a) for a, b in zip(west, wests[n - 1])]
            yield q, [e - w for e, w in zip(east, west)]


def new_level(level, t0, t1, ca, sa, dx, dy, live):
    return (level + (t0 * ca + t1 * sa) - (dx + dy)) * live


def new_velocity(u, w, cor, dx, dy, live):
    return (
        (F32(0.985) * u + cor * w - F32(0.15) * dx) * live,
        (F32(0.985) * w - cor * u - F32(0.15) * dy) * live,
    )


NAMES = ("level", "east", "north", "depth", "live", "cor", "tide0", "tide1")


def fields_of(state, land, rest):
    refs = [(state, 0), (state, 1), (state, 2), (land, 0), (land, 1)]
    return dict(zip(NAMES, refs + [(rest, f) for f in range(3)]))


def interior_steps(s, runs, times, steps, ghosts, wide):
    sub = tile_iota(0)
    place = {q: SUB * n for n, q in enumerate(q for run in runs for q in run)}

    def tiles(name, q):
        ref, f = s[name]
        return [ref[f, i, pl.ds(place[q], SUB), :] for i in range(ROWS)]

    def put(name, q, k, new, old):
        ref, f = s[name]
        least = min(SUB * q, BS - SUB - SUB * q) + 1
        if k >= least + SUB - 1:
            return
        if k >= least:
            edge = (sub if q < GROUPS // 2 else SUB - 1 - sub) + least
            new = [jnp.where(edge > k, a, b) for a, b in zip(new, old)]
        for i in range(ROWS):
            ref[f, i, pl.ds(place[q], SUB), :] = new[i]

    def product(a, b):
        return [x * y for x, y in zip(a, b)]

    def unneeded(q, k):
        return wide and min(SUB * q, BS - SUB - SUB * q) > OUT + 2 * SENT - k

    up, up_on, down, down_on = ghosts
    if wide:
        back_up, back_up_on, back_down, back_down_on = two_way_ghosts(ghosts)
    live_over, live_under = {}, {}
    for q in place if wide else ():
        live = tiles("live", q)
        live_over[q] = lanes_of(live[0], up) * up_on
        live_under[q] = lanes_of(live[3], down) * down_on
    for step in steps:
        ca, sa = times[2 * step], times[2 * step + 1]
        slope = x_slopes(lambda q: product(tiles("depth", q), tiles("east", q)), runs)
        dys = {}
        for q, dx in slope:
            if unneeded(q, 2 * step + 1):
                continue
            old = tiles("level", q)
            t0, t1, live = tiles("tide0", q), tiles("tide1", q), tiles("live", q)
            part = [old[i] + (t0[i] * ca + t1[i] * sa) - dx[i] for i in range(ROWS)]
            flux = product(tiles("depth", q), tiles("north", q))
            above, below = lanes_of(flux[0], up) * up_on, lanes_of(flux[3], down) * down_on
            north = flux[1:] + [above]
            south = [below] + flux[:3]
            new = [(part[i] - (north[i] - south[i])) * live[i] for i in range(ROWS)]
            put("level", q, 2 * step + 1, new, old)
            if not wide:
                continue
            over = lanes_of(flux[1], up) - lanes_of(flux[3], back_up) * back_up_on
            over = (lanes_of(part[0], up) - over) * live_over[q]
            under = lanes_of(flux[0], back_down) * back_down_on - lanes_of(flux[2], down)
            under = (lanes_of(part[3], down) - under) * live_under[q]
            dys[q] = [new[1] - under, new[2] - new[0], new[3] - new[1], over - new[2]]
        slope = x_slopes(lambda q: tiles("level", q), runs)
        for q, dx in slope:
            if unneeded(q, 2 * step + 2):
                continue
            u, w, cor, live = (tiles(n, q) for n in ("east", "north", "cor", "live"))
            dy = dys[q] if wide else y_slopes(tiles("level", q), ghosts)
            new = [new_velocity(u[i], w[i], cor[i], dx[i], dy[i], live[i]) for i in range(ROWS)]
            put("east", q, 2 * step + 2, [a for a, _ in new], u)
            put("north", q, 2 * step + 2, [b for _, b in new], w)


ALL = tuple(range(GROUPS))
SIDES = (ALL[:2], ALL[-2:])
NEAR = SIDES[0] + SIDES[1]
EDGE, INNER = 2 * HALF, BS - 2 * HALF


def parted(q):
    low = tile_iota(0) < HALF - SUB
    edge = [q[0], jnp.where(low, q[1], q[-2]), q[-1]]
    return edge, list(q[2:-2]) + [jnp.where(low, q[-2], q[1])]


def joint(edge, inner):
    low = tile_iota(0) < HALF - SUB
    second, last_but_one = jnp.where(low, edge[1], inner[-1]), jnp.where(low, inner[-1], edge[1])
    return [edge[0], second] + inner[:-1] + [last_but_one, edge[2]]


def started(pairs, sems):
    loads = [pltpu.make_async_copy(src, dst, sems.at[i]) for i, (src, dst) in enumerate(pairs)]
    for load in loads:
        load.start()
    return loads


def turn(groups, source, put):
    tiles = BS * BS // LANES
    for i, columns in enumerate(to_columns([source(v) for v in range(tiles)])):
        for n, q in enumerate(groups):
            put((i, pl.ds(SUB * n, SUB)), columns[SUB * q : SUB * q + SUB])


def storing(ref, f):
    def put(at, x):
        ref[f, at[0], at[1], :] = x

    return put


def turn_rest(groups, tide, cor, rest):
    for f in range(2):
        turn(groups, lambda v, f=f: lane_tile(tide, v, (f,)), storing(rest, 1 + f))
    turn(groups, lambda v: F32(0.3) * lane_tile(cor, v), storing(rest, 0))


def turn_land(groups, held, row, level_id, wet, land):
    none = LANES - 1
    held, row = held[...] > 0, row[...]

    def coded(v):
        here = jnp.logical_and(lane_tile(wet, v) > 0, held)
        return jnp.where(here, lane_tile(level_id, v), none)

    def put(at, code):
        land[0, at[0], at[1], :] = lanes_of(row, code)
        land[1, at[0], at[1], :] = (code < none).astype(F32)

    turn(groups, coded, put)


def turn_state(groups, start, land, state):
    def storing_live(f):
        def put(at, x):
            state[f, at[0], at[1], :] = x * land[1, at[0], at[1], :]

        return put

    for f in range(3):
        turn(groups, lambda v, f=f: lane_tile(start, v, (0, f)), storing_live(f))


def clock_kernel(slices, times):
    for step in range(STEPS):
        for j, x in enumerate(phase(slices, step)):
            times[2 * step + j] = jnp.full((SUB, LANES), x, F32)


def depths_kernel(table, row):
    levels = table.shape[0]
    depths = F32(0.15) * table[...].reshape(1, levels)
    depths = jnp.concatenate([depths, jnp.zeros((1, LANES - levels), F32)], axis=1)
    row[...] = jnp.broadcast_to(depths, (SUB, LANES))


def slots_kernel(count_ref, nb, face, held):
    for j, x in enumerate(face_rows(nb[...])):
        face[j] = x
    held[...] = (tile_iota(0) < count_ref[0]).astype(jnp.int32)


def still_kernel(held, row, level_id, wet, tide, cor, land, rest):
    turn_rest(NEAR, tide, cor, rest)
    turn_land(NEAR, held, row, level_id, wet, land)


def before_kernel(times, face, start, land, rest, pe, pw, state):
    turn_state(NEAR, start, land, state)
    rows = [face[j] for j in range(4)]
    s = fields_of(state, land, rest)
    interior_steps(s, SIDES, times, range(SENT), chunk_ghosts(rows[0], rows[1]), True)

    end = SUB * len(NEAR)
    for f, name in enumerate(NAMES):
        ref, at = s[name]
        for i in range(ROWS):
            pe[i, pl.ds(OUT * f, OUT), :] = ref[at, i, pl.ds(end - OUT, OUT), :]
            pw[i, pl.ds(OUT * f, OUT), :] = ref[at, i, pl.ds(0, OUT), :]
    for i in range(ROWS):
        pe[i, pl.ds(6 * OUT, 1), :] = state[0, i, pl.ds(end - OUT - 1, 1), :]
        pw[i, pl.ds(6 * OUT + OUT - 1, 1), :] = state[0, i, pl.ds(OUT, 1), :]
        entry = rows[i][:1].astype(F32)
        pe[i, pl.ds(7 * OUT, 1), :] = entry
        pw[i, pl.ds(7 * OUT + OUT - 1, 1), :] = entry


def power(x, n):
    return functools.reduce(lambda a, b: a * b, [x] * n)


def part_tile(ref, f, i, n):
    return ref[f, i, pl.ds(SUB * n, SUB), :]


def during_kernel(
    times, face, held, row, level_id, wet, start, tide, cor, gain_h,
    last, land, rest, inner, inner_gain, edge_gain, edge_base,
    gain, sems,
):
    loads = started([(gain_h, gain)], sems)
    tiles = wet.shape[1] // LANES
    turn_land(ALL, held, row, level_id, wet, land)
    turn_state(ALL, start, land, last)
    turn_rest(ALL, tide, cor, rest)
    ghosts = chunk_ghosts(face[0], face[1])
    interior_steps(fields_of(last, land, rest), (ALL,), times, range(STEPS), ghosts, False)
    held = held[...].astype(F32)
    for load in loads:
        load.wait()

    def store(ref, f, i, parts):
        for n, x in enumerate(parts):
            ref[f, i, pl.ds(SUB * n, SUB), :] = x

    for f in range(3):
        gains = [lane_tile(gain, v, (f,)) for v in range(tiles)]
        base = [
            gains[v] * (lane_tile(start, v, (0, f)) * (lane_tile(wet, v).astype(F32) * held))
            for v in range(tiles)
        ]
        gains, base = to_columns(gains), to_columns(base)
        for i in range(ROWS):
            gain_parts, base_parts, last_parts = (
                parted([x[SUB * q : SUB * q + SUB] for q in ALL])
                for x in (gains[i], base[i], last[f, i])
            )
            store(edge_gain, f, i, gain_parts[0])
            store(inner_gain, f, i, gain_parts[1])
            store(edge_base, f, i, base_parts[0])
            store(inner, f, i, [x - y for x, y in zip(last_parts[1], base_parts[1])])


def after_kernel(times, pe, pw, last, land, rest, face, base, edge, joined):
    sub, lane = tile_iota(0), tile_iota(1)
    s = fields_of(last, land, rest)

    for f, name in enumerate(NAMES):
        ref, at = s[name]
        for i in range(ROWS):
            joined[f, i, 0, pl.ds(0, OUT), :] = pe[i, pl.ds(OUT * f, OUT), :]
            joined[f, i, 0, pl.ds(OUT, 2), :] = ref[at, i, pl.ds(0, 2), :]
            joined[f, i, 1, pl.ds(0, 2), :] = ref[at, i, pl.ds(BS - 2, 2), :]
            joined[f, i, 1, pl.ds(2, OUT), :] = pw[i, pl.ds(OUT * f, OUT), :]

    def load(name, side, g):
        f = NAMES.index(name)
        if g == 0:
            return [joined[f, i, side] for i in range(ROWS)]
        ref, at = s[name]
        low = SUB * g - OUT
        low = low if side == 0 else BS - SUB - low
        return [ref[at, i, pl.ds(low, SUB), :] for i in range(ROWS)]

    own = [face[j] for j in range(4)]
    ghosts, joins, far = [], [], []
    for side in range(2):
        row = 0 if side == 0 else SUB - 1
        sent = [
            jnp.broadcast_to(joined[7, j, side, pl.ds(row, 1), :].astype(jnp.int32), (SUB, LANES))
            for j in range(4)
        ]
        outer = sub < OUT if side == 0 else sub >= 2
        mixed = [jnp.where(outer, sent[j], own[j]) for j in range(4)]
        here = chunk_ghosts(own[0], own[1])
        ghosts.append([chunk_ghosts(mixed[0], mixed[1]), here, here])
        to = jnp.where(outer, own[3 - side], sent[2 + side])
        joins.append((lane - lane % SUB + jnp.maximum(to, 0), (to >= 0).astype(F32)))
    inner_row = (OUT, 1)
    outer_row = (OUT - 1, 2)

    def x_side(side, t, beyond=None):
        index, on = joins[side]
        looked = [lanes_of(x, index) * on for x in t[0]]
        inner = [jnp.where(sub == inner_row[side], b, a) for a, b in zip(t[0], looked)]
        outer = [jnp.where(sub == outer_row[side], b, a) for a, b in zip(t[0], looked)]
        sign = -1 if side == 0 else 1
        end_in, end_out = (SUB - 1, 0) if side == 0 else (0, SUB - 1)
        inward = [[shifted(x, sign) for x in inner]]
        outward = [[shifted(x, -sign) for x in outer]]
        if beyond is not None:
            outward[0] = [jnp.where(sub == end_out, b, a) for a, b in zip(outward[0], beyond)]
        plain_out = [[shifted(x, -sign) for x in t[0]]]
        for g in range(1, len(t)):
            inward.append([shifted(x, sign) for x in t[g]])
            plain_out.append([shifted(x, -sign) for x in t[g]])
        for g in range(1, len(t)):
            outward.append(
                [jnp.where(sub == end_out, b, a) for a, b in zip(plain_out[g], plain_out[g - 1])]
            )
        for g in range(len(t) - 1):
            inward[g] = [
                jnp.where(sub == end_in, b, a) for a, b in zip(inward[g], inward[g + 1])
            ]
        return [
            [(a - b) if side == 0 else (b - a) for a, b in zip(inward[g], outward[g])]
            for g in range(len(t))
        ]

    def changed(side, g, k):
        place = sub if side == 0 else SUB - 1 - sub
        if g == 0:
            reach = min(k, HALF - k)
            mask = place >= OUT - reach
            return mask if k >= 2 else jnp.logical_and(mask, place <= OUT)
        least = SUB * g - OUT + 1
        if k < least:
            return False
        return None if k >= least + SUB - 1 else place + least <= k

    cells = {
        (n, side, g): load(n, side, g)
        for n in ("level", "east", "north") for side in range(2) for g in range(3)
    }

    def put(name, side, g, mask, new):
        key = (name, side, g)
        if mask is not None:
            new = [jnp.where(mask, a, b) for a, b in zip(new, cells[key])]
        cells[key] = new

    def product(a, b):
        return [x * y for x, y in zip(a, b)]

    for k in range(1, HALF + 1):
        ca, sa = times[(k - 1) // 2 * 2], times[(k - 1) // 2 * 2 + 1]
        active = [g for g in range(3) if changed(0, g, k) is not False]
        reach = min(3, len(active) + 1)
        for side in range(2):
            if k % 2 == 1:
                depth = [load("depth", side, g) for g in range(reach)]
                dx = x_side(
                    side, [product(depth[g], cells["east", side, g]) for g in range(reach)]
                )
                for g in active:
                    flux = product(depth[g], cells["north", side, g])
                    dy = y_slopes(flux, ghosts[side][g])
                    t0, t1, live = (load(n, side, g) for n in ("tide0", "tide1", "live"))
                    old = cells["level", side, g]
                    new = [
                        new_level(old[i], t0[i], t1[i], ca, sa, dx[g][i], dy[i], live[i])
                        for i in range(ROWS)
                    ]
                    put("level", side, g, changed(side, g, k), new)
            else:
                beyond = load("tide0", side, 0) if k == OUT else None
                dx = x_side(side, [cells["level", side, g] for g in range(reach)], beyond)
                for g in active:
                    dy = y_slopes(cells["level", side, g], ghosts[side][g])
                    cor, live = load("cor", side, g), load("live", side, g)
                    u, w = cells["east", side, g], cells["north", side, g]
                    new = [
                        new_velocity(u[i], w[i], cor[i], dx[g][i], dy[i], live[i])
                        for i in range(ROWS)
                    ]
                    mask = changed(side, g, k)
                    put("east", side, g, mask, [a for a, _ in new])
                    put("north", side, g, mask, [b for _, b in new])

    for f, name in enumerate(NAMES[:3]):
        for i in range(ROWS):
            a, b, c = (shifted(cells[name, 0, g][i], 2) for g in range(3))
            d, e, h = (shifted(cells[name, 1, g][i], -2) for g in range(3))
            second, last_but_one = jnp.where(sub < 2, b, c), jnp.where(sub >= 6, e, h)
            fine = [
                jnp.where(sub < 2, a, b),
                jnp.where(sub < HALF - SUB, second, last_but_one),
                jnp.where(sub >= 6, d, e),
            ]
            for n, x in enumerate(fine):
                edge[f, i, pl.ds(SUB * n, SUB), :] = x - part_tile(base, f, i, n)


def final_kernel(
    slices, edge_sum, edge, edge_gain, inner_sum, inner, inner_gain, result, out, sems
):
    parts = ((edge_sum, edge, edge_gain), (inner_sum, inner, inner_gain))
    copies = []
    for f in range(3):
        columns = []
        for i in range(ROWS):
            done = []
            for total, own, gain in parts:
                done.append([])
                for n in range(gain.shape[2] // SUB):
                    g = part_tile(gain, f, i, n)
                    most = power(g, slices - 1)
                    whole = part_tile(total, f, i, n) + most * part_tile(own, f, i, n)
                    done[-1].append(whole / (F32(1) - most * g))
            q = joint(*done)
            columns.append(jnp.concatenate(q, axis=0))
        for v, x in enumerate(to_tiles(columns)):
            out[0, f, :, pl.ds(v * LANES, LANES)] = x
        copies.append(pltpu.make_async_copy(out.at[0, f], result.at[0, f], sems.at[f]))
        copies[-1].start()
    for copy in copies:
        copy.wait()


def call(kernel, out_shape, operands, spaces=None, out_space=pltpu.VMEM, scratch=(), flops=0):
    spaces = spaces or [pltpu.VMEM] * len(operands)
    size = 2 * sum(4 * x.size for x in operands)
    return pl.pallas_call(
        kernel,
        out_shape=out_shape,
        in_specs=[pl.BlockSpec(memory_space=space) for space in spaces],
        out_specs=jax.tree.map(lambda _: pl.BlockSpec(memory_space=out_space), out_shape),
        scratch_shapes=scratch,
        cost_estimate=pl.CostEstimate(flops=flops, bytes_accessed=size, transcendentals=0),
        compiler_params=pltpu.CompilerParams(vmem_limit_bytes=VMEM_LIMIT),
    )(*operands)


def shape(*dims):
    return jax.ShapeDtypeStruct(dims, F32)


def in_hbm(arrays):
    return [pltpu.with_memory_space_constraint(x, pltpu.HBM) for x in arrays]


def passed_along(shard, axis, by):
    size = lax.axis_size(axis)
    return lax.ppermute(shard, axis, [(i, (i + by) % size) for i in range(size)])


def periodic_sum(defect, gain, slices):
    total = passed_along(defect, "tm", 1)
    for _ in range(slices - 2):
        total = passed_along(defect + gain * total, "tm", 1)
    return total


def body(
    start_states, coarse_gain, depth_level, depth_table, wet, block_count, neighbour, coriolis, tide
):
    slices = lax.axis_size("tm")

    def columns(fields, size):
        return shape(fields, ROWS, size, LANES)

    times = call(
        functools.partial(clock_kernel, slices), shape(2 * STEPS, SUB, LANES), [], flops=10**10
    )
    flags = jax.ShapeDtypeStruct((SUB, LANES), jnp.int32)
    row = call(depths_kernel, shape(SUB, LANES), [depth_table])
    slot_tiles = call(
        slots_kernel,
        [jax.ShapeDtypeStruct((4, SUB, LANES), jnp.int32), flags],
        [block_count, neighbour.T],
        spaces=[pltpu.SMEM, pltpu.VMEM],
    )
    face, held = slot_tiles
    ready = [times, face, held, row, depth_level, wet, start_states, tide, coriolis]
    near = SUB * len(NEAR)
    land, rest = call(
        still_kernel,
        [columns(2, near), columns(3, near)],
        [held, row, depth_level, wet, tide, coriolis],
    )
    pe, pw = call(
        before_kernel,
        [shape(ROWS, len(NAMES) * OUT, LANES)] * 2,
        [times, face, start_states, land, rest],
        scratch=[pltpu.VMEM(columns(3, near).shape, F32)],
    )
    from_west = passed_along(pe, "space", 1)
    from_east = passed_along(pw, "space", -1)
    last, land, rest, inner, inner_gain, edge_gain, edge_base = call(
        during_kernel,
        [columns(3, BS), columns(2, BS), columns(3, BS)]
        + [columns(3, INNER)] * 2
        + [columns(3, EDGE)] * 2,
        ready + in_hbm([coarse_gain]),
        spaces=[pltpu.VMEM] * len(ready) + [pltpu.HBM],
        scratch=[pltpu.VMEM(coarse_gain.shape, F32), pltpu.SemaphoreType.DMA((1,))],
    )
    inner_sum = periodic_sum(inner, inner_gain, slices)
    edge = call(
        after_kernel,
        columns(3, EDGE),
        [times, from_west, from_east, last, land, rest, face, edge_base],
        scratch=[pltpu.VMEM((len(NAMES), ROWS, 2, SUB, LANES), F32)],
    )
    edge_sum = periodic_sum(edge, edge_gain, slices)
    return call(
        functools.partial(final_kernel, slices),
        shape(*start_states.shape),
        [edge_sum, edge, edge_gain, inner_sum, inner, inner_gain],
        out_space=pltpu.HBM,
        scratch=[pltpu.VMEM(start_states.shape, F32), pltpu.SemaphoreType.DMA((3,))],
    )


def solution(mesh):
    return jax.shard_map(
        body,
        mesh=mesh,
        in_specs=(
            P("tm", None, "space", None),
            P(None, "space", None),
            P("space", None),
            P(),
            P("space", None),
            P("space"),
            P("space", None),
            P("space", None),
            P(None, "space", None),
        ),
        out_specs=P("tm", None, "space", None),
        check_vma=False,
    )
```

```python
import functools
import math

import jax
import jax.numpy as jnp
from jax import lax
from jax.experimental import pallas as pl
from jax.experimental.pallas import tpu as pltpu
from jax.sharding import PartitionSpec as P

BS = 64
STEPS = 6
HALF = 2 * STEPS
SENT = STEPS // 2
OUT = STEPS
LANES = 128
SUB = 8
ROWS = 4
GROUPS = BS // SUB
F32 = jnp.float32
VMEM_LIMIT = 24 * 1024 * 1024


def shifted(x, by):
    return pltpu.roll(x, by % SUB, 0)


def lanes_of(x, index):
    return jnp.take_along_axis(x, index, axis=1, mode="promise_in_bounds")


def tile_iota(dim):
    return lax.broadcasted_iota(jnp.int32, (SUB, LANES), dim)


def lane_tile(ref, v, lead=()):
    return ref[tuple(lead) + (slice(None), pl.ds(v * LANES, LANES))]


def to_columns(tiles):
    out = []
    for part in (tiles[0::2], tiles[1::2]):
        turned = jnp.concatenate(part, axis=0).T
        out += [turned[:BS], turned[BS:]]
    return out


def to_tiles(columns):
    out = {}
    for part in range(2):
        turned = jnp.concatenate(columns[2 * part : 2 * part + 2], axis=0).T
        for c in range(LANES // SUB):
            out[2 * c + part] = turned[SUB * c : SUB * c + SUB]
    return [out[v] for v in range(len(out))]


def phase(count, step):
    omega = 2.0 * math.pi / (count * STEPS)
    here = lax.axis_index("tm")
    ca, sa = F32(0), F32(0)
    for n in range(count):
        angle = (n * STEPS + step) * omega
        ca = jnp.where(here == n, F32(0.3 * math.cos(angle)), ca)
        sa = jnp.where(here == n, F32(0.3 * math.sin(angle)), sa)
    return ca, sa


def chunk_ghosts(north, south):
    lane = tile_iota(1)
    top, bottom = lane >= LANES - SUB, lane < SUB
    up = jnp.where(top, jnp.maximum(north, 0), (lane + SUB) % LANES)
    down = jnp.where(bottom, LANES - SUB + jnp.maximum(south, 0), (lane + LANES - SUB) % LANES)
    up_on = jnp.where(jnp.logical_and(top, north < 0), F32(0), F32(1))
    down_on = jnp.where(jnp.logical_and(bottom, south < 0), F32(0), F32(1))
    return up, up_on, down, down_on


def two_way_ghosts(ghosts):
    up, up_on, down, down_on = ghosts
    return lanes_of(down, up), lanes_of(down_on, up), lanes_of(up, down), lanes_of(up_on, down)


def face_rows(nb):
    wide = jnp.concatenate([nb] * (LANES // SUB), axis=1)
    return [jnp.broadcast_to(wide[j : j + 1], (SUB, LANES)) for j in range(4)]


def y_slopes(t, ghosts):
    up, up_on, down, down_on = ghosts
    above = lanes_of(t[0], up) * up_on
    below = lanes_of(t[3], down) * down_on
    return [t[1] - below, t[2] - t[0], t[3] - t[1], above - t[2]]


def x_slopes(columns, runs):
    sub = tile_iota(0)
    first, last = sub == 0, sub == SUB - 1
    for run in runs:
        get = [columns(q) for q in run]
        easts = [[shifted(x, -1) for x in t] for t in get]
        wests = [[shifted(x, 1) for x in t] for t in get]
        for n, q in enumerate(run):
            east, west = easts[n], wests[n]
            if n + 1 < len(run):
                east = [jnp.where(last, b, a) for a, b in zip(east, easts[n + 1])]
            if n > 0:
                west = [jnp.where(first, b, a) for a, b in zip(west, wests[n - 1])]
            yield q, [e - w for e, w in zip(east, west)]


def new_level(level, t0, t1, ca, sa, dx, dy, live):
    return (level + (t0 * ca + t1 * sa) - (dx + dy)) * live


def new_velocity(u, w, cor, dx, dy, live):
    return (
        (F32(0.985) * u + cor * w - F32(0.15) * dx) * live,
        (F32(0.985) * w - cor * u - F32(0.15) * dy) * live,
    )


NAMES = ("level", "east", "north", "depth", "live", "cor", "tide0", "tide1")


def fields_of(state, land, rest):
    refs = [(state, 0), (state, 1), (state, 2), (land, 0), (land, 1)]
    return dict(zip(NAMES, refs + [(rest, f) for f in range(3)]))


def interior_steps(s, runs, times, steps, ghosts, wide):
    sub = tile_iota(0)
    place = {q: SUB * n for n, q in enumerate(q for run in runs for q in run)}

    def tiles(name, q):
        ref, f = s[name]
        return [ref[f, i, pl.ds(place[q], SUB), :] for i in range(ROWS)]

    def put(name, q, k, new, old):
        ref, f = s[name]
        least = min(SUB * q, BS - SUB - SUB * q) + 1
        if k >= least + SUB - 1:
            return
        if k >= least:
            edge = (sub if q < GROUPS // 2 else SUB - 1 - sub) + least
            new = [jnp.where(edge > k, a, b) for a, b in zip(new, old)]
        for i in range(ROWS):
            ref[f, i, pl.ds(place[q], SUB), :] = new[i]

    def product(a, b):
        return [x * y for x, y in zip(a, b)]

    def unneeded(q, k):
        return wide and min(SUB * q, BS - SUB - SUB * q) > OUT + 2 * SENT - k

    up, up_on, down, down_on = ghosts
    if wide:
        back_up, back_up_on, back_down, back_down_on = two_way_ghosts(ghosts)
    live_over, live_under = {}, {}
    for q in place if wide else ():
        live = tiles("live", q)
        live_over[q] = lanes_of(live[0], up) * up_on
        live_under[q] = lanes_of(live[3], down) * down_on
    for step in steps:
        ca, sa = times[2 * step], times[2 * step + 1]
        slope = x_slopes(lambda q: product(tiles("depth", q), tiles("east", q)), runs)
        dys = {}
        for q, dx in slope:
            if unneeded(q, 2 * step + 1):
                continue
            old = tiles("level", q)
            t0, t1, live = tiles("tide0", q), tiles("tide1", q), tiles("live", q)
            part = [old[i] + (t0[i] * ca + t1[i] * sa) - dx[i] for i in range(ROWS)]
            flux = product(tiles("depth", q), tiles("north", q))
            above, below = lanes_of(flux[0], up) * up_on, lanes_of(flux[3], down) * down_on
            north = flux[1:] + [above]
            south = [below] + flux[:3]
            new = [(part[i] - (north[i] - south[i])) * live[i] for i in range(ROWS)]
            put("level", q, 2 * step + 1, new, old)
            if not wide:
                continue
            over = lanes_of(flux[1], up) - lanes_of(flux[3], back_up) * back_up_on
            over = (lanes_of(part[0], up) - over) * live_over[q]
            under = lanes_of(flux[0], back_down) * back_down_on - lanes_of(flux[2], down)
            under = (lanes_of(part[3], down) - under) * live_under[q]
            dys[q] = [new[1] - under, new[2] - new[0], new[3] - new[1], over - new[2]]
        slope = x_slopes(lambda q: tiles("level", q), runs)
        for q, dx in slope:
            if unneeded(q, 2 * step + 2):
                continue
            u, w, cor, live = (tiles(n, q) for n in ("east", "north", "cor", "live"))
            dy = dys[q] if wide else y_slopes(tiles("level", q), ghosts)
            new = [new_velocity(u[i], w[i], cor[i], dx[i], dy[i], live[i]) for i in range(ROWS)]
            put("east", q, 2 * step + 2, [a for a, _ in new], u)
            put("north", q, 2 * step + 2, [b for _, b in new], w)


ALL = tuple(range(GROUPS))
SIDES = (ALL[:2], ALL[-2:])
NEAR = SIDES[0] + SIDES[1]
EDGE, INNER = 2 * HALF, BS - 2 * HALF


def parted(q):
    low = tile_iota(0) < HALF - SUB
    edge = [q[0], jnp.where(low, q[1], q[-2]), q[-1]]
    return edge, list(q[2:-2]) + [jnp.where(low, q[-2], q[1])]


def joint(edge, inner):
    low = tile_iota(0) < HALF - SUB
    second, last_but_one = jnp.where(low, edge[1], inner[-1]), jnp.where(low, inner[-1], edge[1])
    return [edge[0], second] + inner[:-1] + [last_but_one, edge[2]]


def started(pairs, sems):
    loads = [pltpu.make_async_copy(src, dst, sems.at[i]) for i, (src, dst) in enumerate(pairs)]
    for load in loads:
        load.start()
    return loads


def turn(groups, source, put):
    tiles = BS * BS // LANES
    for i, columns in enumerate(to_columns([source(v) for v in range(tiles)])):
        for n, q in enumerate(groups):
            put((i, pl.ds(SUB * n, SUB)), columns[SUB * q : SUB * q + SUB])


def storing(ref, f):
    def put(at, x):
        ref[f, at[0], at[1], :] = x

    return put


def turn_tide(groups, tide, tides):
    for f in range(2):
        turn(groups, lambda v, f=f: lane_tile(tide, v, (f,)), storing(tides, f))


def turn_cor(groups, cor, out):
    turn(groups, lambda v: F32(0.3) * lane_tile(cor, v), storing(out, 0))


def turn_rest(groups, tide, cor, rest):
    turn_tide(groups, tide, rest.at[pl.ds(1, 2)])
    turn_cor(groups, cor, rest.at[pl.ds(0, 1)])


def turn_land(groups, held, row, level_id, wet, land):
    none = LANES - 1
    held, row = held[...] > 0, row[...]

    def coded(v):
        here = jnp.logical_and(lane_tile(wet, v) > 0, held)
        return jnp.where(here, lane_tile(level_id, v), none)

    def put(at, code):
        land[0, at[0], at[1], :] = lanes_of(row, code)
        land[1, at[0], at[1], :] = (code < none).astype(F32)

    turn(groups, coded, put)


def turn_state(groups, start, land, state):
    def storing_live(f):
        def put(at, x):
            state[f, at[0], at[1], :] = x * land[1, at[0], at[1], :]

        return put

    for f in range(3):
        turn(groups, lambda v, f=f: lane_tile(start, v, (0, f)), storing_live(f))


def clock_kernel(slices, times):
    for step in range(STEPS):
        for j, x in enumerate(phase(slices, step)):
            times[2 * step + j] = jnp.full((SUB, LANES), x, F32)


def depths_kernel(table, row):
    levels = table.shape[0]
    depths = F32(0.15) * table[...].reshape(1, levels)
    depths = jnp.concatenate([depths, jnp.zeros((1, LANES - levels), F32)], axis=1)
    row[...] = jnp.broadcast_to(depths, (SUB, LANES))


def slots_kernel(count_ref, nb, face, held):
    for j, x in enumerate(face_rows(nb[...])):
        face[j] = x
    held[...] = (tile_iota(0) < count_ref[0]).astype(jnp.int32)


def still_kernel(held, row, level_id, wet, cor, land, turned):
    turn_land(NEAR, held, row, level_id, wet, land)
    turn_cor(NEAR, cor, turned)


def before_kernel(times, face, start, tide, land, cor, pe, pw, state, tides):
    turn_state(NEAR, start, land, state)
    turn_tide(NEAR, tide, tides)
    rows = [face[j] for j in range(4)]
    s = fields_of(state, land, tides)
    s.update(cor=(cor, 0), tide0=(tides, 0), tide1=(tides, 1))
    interior_steps(s, SIDES, times, range(SENT), chunk_ghosts(rows[0], rows[1]), True)

    end = SUB * len(NEAR)
    for f, name in enumerate(NAMES):
        ref, at = s[name]
        for i in range(ROWS):
            pe[i, pl.ds(OUT * f, OUT), :] = ref[at, i, pl.ds(end - OUT, OUT), :]
            pw[i, pl.ds(OUT * f, OUT), :] = ref[at, i, pl.ds(0, OUT), :]
    for i in range(ROWS):
        pe[i, pl.ds(6 * OUT, 1), :] = state[0, i, pl.ds(end - OUT - 1, 1), :]
        pw[i, pl.ds(6 * OUT + OUT - 1, 1), :] = state[0, i, pl.ds(OUT, 1), :]
        entry = rows[i][:1].astype(F32)
        pe[i, pl.ds(7 * OUT, 1), :] = entry
        pw[i, pl.ds(7 * OUT + OUT - 1, 1), :] = entry


def power(x, n):
    return functools.reduce(lambda a, b: a * b, [x] * n)


def part_tile(ref, f, i, n):
    return ref[f, i, pl.ds(SUB * n, SUB), :]


def during_kernel(
    times, face, held, row, level_id, wet, start, tide, cor, gain_h,
    last, land, rest, inner, inner_gain, edge_gain, edge_base,
    gain, sems,
):
    loads = started([(gain_h, gain)], sems)
    tiles = wet.shape[1] // LANES
    turn_land(ALL, held, row, level_id, wet, land)
    turn_state(ALL, start, land, last)
    turn_rest(ALL, tide, cor, rest)
    ghosts = chunk_ghosts(face[0], face[1])
    interior_steps(fields_of(last, land, rest), (ALL,), times, range(STEPS), ghosts, False)
    held = held[...].astype(F32)
    for load in loads:
        load.wait()

    def store(ref, f, i, parts):
        for n, x in enumerate(parts):
            ref[f, i, pl.ds(SUB * n, SUB), :] = x

    for f in range(3):
        gains = [lane_tile(gain, v, (f,)) for v in range(tiles)]
        base = [
            gains[v] * (lane_tile(start, v, (0, f)) * (lane_tile(wet, v).astype(F32) * held))
            for v in range(tiles)
        ]
        gains, base = to_columns(gains), to_columns(base)
        for i in range(ROWS):
            gain_parts, base_parts, last_parts = (
                parted([x[SUB * q : SUB * q + SUB] for q in ALL])
                for x in (gains[i], base[i], last[f, i])
            )
            store(edge_gain, f, i, gain_parts[0])
            store(inner_gain, f, i, gain_parts[1])
            store(edge_base, f, i, base_parts[0])
            store(inner, f, i, [x - y for x, y in zip(last_parts[1], base_parts[1])])


def after_kernel(times, pe, pw, last, land, rest, face, base, edge, joined):
    sub, lane = tile_iota(0), tile_iota(1)
    s = fields_of(last, land, rest)

    for f, name in enumerate(NAMES):
        ref, at = s[name]
        for i in range(ROWS):
            joined[f, i, 0, pl.ds(0, OUT), :] = pe[i, pl.ds(OUT * f, OUT), :]
            joined[f, i, 0, pl.ds(OUT, 2), :] = ref[at, i, pl.ds(0, 2), :]
            joined[f, i, 1, pl.ds(0, 2), :] = ref[at, i, pl.ds(BS - 2, 2), :]
            joined[f, i, 1, pl.ds(2, OUT), :] = pw[i, pl.ds(OUT * f, OUT), :]

    def load(name, side, g):
        f = NAMES.index(name)
        if g == 0:
            return [joined[f, i, side] for i in range(ROWS)]
        ref, at = s[name]
        low = SUB * g - OUT
        low = low if side == 0 else BS - SUB - low
        return [ref[at, i, pl.ds(low, SUB), :] for i in range(ROWS)]

    own = [face[j] for j in range(4)]
    ghosts, joins, far = [], [], []
    for side in range(2):
        row = 0 if side == 0 else SUB - 1
        sent = [
            jnp.broadcast_to(joined[7, j, side, pl.ds(row, 1), :].astype(jnp.int32), (SUB, LANES))
            for j in range(4)
        ]
        outer = sub < OUT if side == 0 else sub >= 2
        mixed = [jnp.where(outer, sent[j], own[j]) for j in range(4)]
        here = chunk_ghosts(own[0], own[1])
        ghosts.append([chunk_ghosts(mixed[0], mixed[1]), here, here])
        to = jnp.where(outer, own[3 - side], sent[2 + side])
        joins.append((lane - lane % SUB + jnp.maximum(to, 0), (to >= 0).astype(F32)))
    inner_row = (OUT, 1)
    outer_row = (OUT - 1, 2)

    def x_side(side, t, beyond=None):
        index, on = joins[side]
        looked = [lanes_of(x, index) * on for x in t[0]]
        inner = [jnp.where(sub == inner_row[side], b, a) for a, b in zip(t[0], looked)]
        outer = [jnp.where(sub == outer_row[side], b, a) for a, b in zip(t[0], looked)]
        sign = -1 if side == 0 else 1
        end_in, end_out = (SUB - 1, 0) if side == 0 else (0, SUB - 1)
        inward = [[shifted(x, sign) for x in inner]]
        outward = [[shifted(x, -sign) for x in outer]]
        if beyond is not None:
            outward[0] = [jnp.where(sub == end_out, b, a) for a, b in zip(outward[0], beyond)]
        plain_out = [[shifted(x, -sign) for x in t[0]]]
        for g in range(1, len(t)):
            inward.append([shifted(x, sign) for x in t[g]])
            plain_out.append([shifted(x, -sign) for x in t[g]])
        for g in range(1, len(t)):
            outward.append(
                [jnp.where(sub == end_out, b, a) for a, b in zip(plain_out[g], plain_out[g - 1])]
            )
        for g in range(len(t) - 1):
            inward[g] = [
                jnp.where(sub == end_in, b, a) for a, b in zip(inward[g], inward[g + 1])
            ]
        return [
            [(a - b) if side == 0 else (b - a) for a, b in zip(inward[g], outward[g])]
            for g in range(len(t))
        ]

    def changed(side, g, k):
        place = sub if side == 0 else SUB - 1 - sub
        if g == 0:
            reach = min(k, HALF - k)
            mask = place >= OUT - reach
            return mask if k >= 2 else jnp.logical_and(mask, place <= OUT)
        least = SUB * g - OUT + 1
        if k < least:
            return False
        return None if k >= least + SUB - 1 else place + least <= k

    cells = {
        (n, side, g): load(n, side, g)
        for n in ("level", "east", "north") for side in range(2) for g in range(3)
    }

    def put(name, side, g, mask, new):
        key = (name, side, g)
        if mask is not None:
            new = [jnp.where(mask, a, b) for a, b in zip(new, cells[key])]
        cells[key] = new

    def product(a, b):
        return [x * y for x, y in zip(a, b)]

    for k in range(1, HALF + 1):
        ca, sa = times[(k - 1) // 2 * 2], times[(k - 1) // 2 * 2 + 1]
        active = [g for g in range(3) if changed(0, g, k) is not False]
        reach = min(3, len(active) + 1)
        for side in range(2):
            if k % 2 == 1:
                depth = [load("depth", side, g) for g in range(reach)]
                dx = x_side(
                    side, [product(depth[g], cells["east", side, g]) for g in range(reach)]
                )
                for g in active:
                    flux = product(depth[g], cells["north", side, g])
                    dy = y_slopes(flux, ghosts[side][g])
                    t0, t1, live = (load(n, side, g) for n in ("tide0", "tide1", "live"))
                    old = cells["level", side, g]
                    new = [
                        new_level(old[i], t0[i], t1[i], ca, sa, dx[g][i], dy[i], live[i])
                        for i in range(ROWS)
                    ]
                    put("level", side, g, changed(side, g, k), new)
            else:
                beyond = load("tide0", side, 0) if k == OUT else None
                dx = x_side(side, [cells["level", side, g] for g in range(reach)], beyond)
                for g in active:
                    dy = y_slopes(cells["level", side, g], ghosts[side][g])
                    cor, live = load("cor", side, g), load("live", side, g)
                    u, w = cells["east", side, g], cells["north", side, g]
                    new = [
                        new_velocity(u[i], w[i], cor[i], dx[g][i], dy[i], live[i])
                        for i in range(ROWS)
                    ]
                    mask = changed(side, g, k)
                    put("east", side, g, mask, [a for a, _ in new])
                    put("north", side, g, mask, [b for _, b in new])

    for f, name in enumerate(NAMES[:3]):
        for i in range(ROWS):
            a, b, c = (shifted(cells[name, 0, g][i], 2) for g in range(3))
            d, e, h = (shifted(cells[name, 1, g][i], -2) for g in range(3))
            second, last_but_one = jnp.where(sub < 2, b, c), jnp.where(sub >= 6, e, h)
            fine = [
                jnp.where(sub < 2, a, b),
                jnp.where(sub < HALF - SUB, second, last_but_one),
                jnp.where(sub >= 6, d, e),
            ]
            for n, x in enumerate(fine):
                edge[f, i, pl.ds(SUB * n, SUB), :] = x - part_tile(base, f, i, n)


def final_kernel(
    slices, edge_sum, edge, edge_gain, inner_sum, inner, inner_gain, result, out, sems
):
    parts = ((edge_sum, edge, edge_gain), (inner_sum, inner, inner_gain))
    copies = []
    for f in range(3):
        columns = []
        for i in range(ROWS):
            done = []
            for total, own, gain in parts:
                done.append([])
                for n in range(gain.shape[2] // SUB):
                    g = part_tile(gain, f, i, n)
                    most = power(g, slices - 1)
                    whole = part_tile(total, f, i, n) + most * part_tile(own, f, i, n)
                    done[-1].append(whole / (F32(1) - most * g))
            q = joint(*done)
            columns.append(jnp.concatenate(q, axis=0))
        for v, x in enumerate(to_tiles(columns)):
            out[0, f, :, pl.ds(v * LANES, LANES)] = x
        copies.append(pltpu.make_async_copy(out.at[0, f], result.at[0, f], sems.at[f]))
        copies[-1].start()
    for copy in copies:
        copy.wait()


def call(kernel, out_shape, operands, spaces=None, out_space=pltpu.VMEM, scratch=(), flops=0):
    spaces = spaces or [pltpu.VMEM] * len(operands)
    size = 2 * sum(4 * x.size for x in operands)
    return pl.pallas_call(
        kernel,
        out_shape=out_shape,
        in_specs=[pl.BlockSpec(memory_space=space) for space in spaces],
        out_specs=jax.tree.map(lambda _: pl.BlockSpec(memory_space=out_space), out_shape),
        scratch_shapes=scratch,
        cost_estimate=pl.CostEstimate(flops=flops, bytes_accessed=size, transcendentals=0),
        compiler_params=pltpu.CompilerParams(vmem_limit_bytes=VMEM_LIMIT),
    )(*operands)


def shape(*dims):
    return jax.ShapeDtypeStruct(dims, F32)


def in_hbm(arrays):
    return [pltpu.with_memory_space_constraint(x, pltpu.HBM) for x in arrays]


def passed_along(shard, axis, by):
    size = lax.axis_size(axis)
    return lax.ppermute(shard, axis, [(i, (i + by) % size) for i in range(size)])


def periodic_sum(defect, gain, slices):
    total = passed_along(defect, "tm", 1)
    for _ in range(slices - 2):
        total = passed_along(defect + gain * total, "tm", 1)
    return total


def body(
    start_states, coarse_gain, depth_level, depth_table, wet, block_count, neighbour, coriolis, tide
):
    slices = lax.axis_size("tm")

    def columns(fields, size):
        return shape(fields, ROWS, size, LANES)

    times = call(
        functools.partial(clock_kernel, slices), shape(2 * STEPS, SUB, LANES), [], flops=10**10
    )
    flags = jax.ShapeDtypeStruct((SUB, LANES), jnp.int32)
    row = call(depths_kernel, shape(SUB, LANES), [depth_table])
    slot_tiles = call(
        slots_kernel,
        [jax.ShapeDtypeStruct((4, SUB, LANES), jnp.int32), flags],
        [block_count, neighbour.T],
        spaces=[pltpu.SMEM, pltpu.VMEM],
    )
    face, held = slot_tiles
    ready = [times, face, held, row, depth_level, wet, start_states, tide, coriolis]
    near = SUB * len(NEAR)
    land, cor = call(
        still_kernel,
        [columns(2, near), columns(1, near)],
        [held, row, depth_level, wet, coriolis],
    )
    pe, pw = call(
        before_kernel,
        [shape(ROWS, len(NAMES) * OUT, LANES)] * 2,
        [times, face, start_states, tide, land, cor],
        scratch=[pltpu.VMEM(columns(n, near).shape, F32) for n in (3, 2)],
    )
    from_west = passed_along(pe, "space", 1)
    from_east = passed_along(pw, "space", -1)
    last, land, rest, inner, inner_gain, edge_gain, edge_base = call(
        during_kernel,
        [columns(3, BS), columns(2, BS), columns(3, BS)]
        + [columns(3, INNER)] * 2
        + [columns(3, EDGE)] * 2,
        ready + in_hbm([coarse_gain]),
        spaces=[pltpu.VMEM] * len(ready) + [pltpu.HBM],
        scratch=[pltpu.VMEM(coarse_gain.shape, F32), pltpu.SemaphoreType.DMA((1,))],
    )
    inner_sum = periodic_sum(inner, inner_gain, slices)
    edge = call(
        after_kernel,
        columns(3, EDGE),
        [times, from_west, from_east, last, land, rest, face, edge_base],
        scratch=[pltpu.VMEM((len(NAMES), ROWS, 2, SUB, LANES), F32)],
    )
    edge_sum = periodic_sum(edge, edge_gain, slices)
    return call(
        functools.partial(final_kernel, slices),
        shape(*start_states.shape),
        [edge_sum, edge, edge_gain, inner_sum, inner, inner_gain],
        out_space=pltpu.HBM,
        scratch=[pltpu.VMEM(start_states.shape, F32), pltpu.SemaphoreType.DMA((3,))],
    )


def solution(mesh):
    return jax.shard_map(
        body,
        mesh=mesh,
        in_specs=(
            P("tm", None, "space", None),
            P(None, "space", None),
            P("space", None),
            P(),
            P("space", None),
            P("space"),
            P("space", None),
            P("space", None),
            P(None, "space", None),
        ),
        out_specs=P("tm", None, "space", None),
        check_vma=False,
    )
```

```python
import functools
import math

import jax
import jax.numpy as jnp
from jax import lax
from jax.experimental import pallas as pl
from jax.experimental.pallas import tpu as pltpu
from jax.sharding import PartitionSpec as P

BS = 64
STEPS = 6
HALF = 2 * STEPS
SENT = STEPS // 2
OUT = STEPS
LANES = 128
SUB = 8
ROWS = 4
GROUPS = BS // SUB
F32 = jnp.float32
VMEM_LIMIT = 24 * 1024 * 1024


def shifted(x, by):
    return pltpu.roll(x, by % SUB, 0)


def lanes_of(x, index):
    return jnp.take_along_axis(x, index, axis=1, mode="promise_in_bounds")


def tile_iota(dim):
    return lax.broadcasted_iota(jnp.int32, (SUB, LANES), dim)


def lane_tile(ref, v, lead=()):
    return ref[tuple(lead) + (slice(None), pl.ds(v * LANES, LANES))]


def to_columns(tiles):
    out = []
    for part in (tiles[0::2], tiles[1::2]):
        turned = jnp.concatenate(part, axis=0).T
        out += [turned[:BS], turned[BS:]]
    return out


def to_tiles(columns):
    out = {}
    for part in range(2):
        turned = jnp.concatenate(columns[2 * part : 2 * part + 2], axis=0).T
        for c in range(LANES // SUB):
            out[2 * c + part] = turned[SUB * c : SUB * c + SUB]
    return [out[v] for v in range(len(out))]


def phase(count, step):
    omega = 2.0 * math.pi / (count * STEPS)
    here = lax.axis_index("tm")
    ca, sa = F32(0), F32(0)
    for n in range(count):
        angle = (n * STEPS + step) * omega
        ca = jnp.where(here == n, F32(0.3 * math.cos(angle)), ca)
        sa = jnp.where(here == n, F32(0.3 * math.sin(angle)), sa)
    return ca, sa


def chunk_ghosts(north, south):
    lane = tile_iota(1)
    top, bottom = lane >= LANES - SUB, lane < SUB
    up = jnp.where(top, jnp.maximum(north, 0), (lane + SUB) % LANES)
    down = jnp.where(bottom, LANES - SUB + jnp.maximum(south, 0), (lane + LANES - SUB) % LANES)
    up_on = jnp.where(jnp.logical_and(top, north < 0), F32(0), F32(1))
    down_on = jnp.where(jnp.logical_and(bottom, south < 0), F32(0), F32(1))
    return up, up_on, down, down_on


def two_way_ghosts(ghosts):
    up, up_on, down, down_on = ghosts
    return lanes_of(down, up), lanes_of(down_on, up), lanes_of(up, down), lanes_of(up_on, down)


def face_rows(nb):
    wide = jnp.concatenate([nb] * (LANES // SUB), axis=1)
    return [jnp.broadcast_to(wide[j : j + 1], (SUB, LANES)) for j in range(4)]


def y_slopes(t, ghosts):
    up, up_on, down, down_on = ghosts
    above = lanes_of(t[0], up) * up_on
    below = lanes_of(t[3], down) * down_on
    return [t[1] - below, t[2] - t[0], t[3] - t[1], above - t[2]]


def x_slopes(columns, runs):
    sub = tile_iota(0)
    first, last = sub == 0, sub == SUB - 1
    for run in runs:
        get = [columns(q) for q in run]
        easts = [[shifted(x, -1) for x in t] for t in get]
        wests = [[shifted(x, 1) for x in t] for t in get]
        for n, q in enumerate(run):
            east, west = easts[n], wests[n]
            if n + 1 < len(run):
                east = [jnp.where(last, b, a) for a, b in zip(east, easts[n + 1])]
            if n > 0:
                west = [jnp.where(first, b, a) for a, b in zip(west, wests[n - 1])]
            yield q, [e - w for e, w in zip(east, west)]


def new_level(level, t0, t1, ca, sa, dx, dy, live):
    return (level + (t0 * ca + t1 * sa) - (dx + dy)) * live


def new_velocity(u, w, cor, dx, dy, live):
    push = F32(0.15) * live
    return (F32(0.985) * u + cor * w) - push * dx, (F32(0.985) * w - cor * u) - push * dy


NAMES = ("level", "east", "north", "depth", "live", "cor", "tide0", "tide1")


def fields_of(state, land, rest):
    refs = [(state, 0), (state, 1), (state, 2), (land, 0), (land, 1)]
    return dict(zip(NAMES, refs + [(rest, f) for f in range(3)]))


def interior_steps(s, runs, times, steps, ghosts, wide):
    sub = tile_iota(0)
    place = {q: SUB * n for n, q in enumerate(q for run in runs for q in run)}

    def tiles(name, q):
        ref, f = s[name]
        return [ref[f, i, pl.ds(place[q], SUB), :] for i in range(ROWS)]

    def put(name, q, k, new, old):
        ref, f = s[name]
        least = min(SUB * q, BS - SUB - SUB * q) + 1
        if k >= least + SUB - 1:
            return
        if k >= least:
            edge = (sub if q < GROUPS // 2 else SUB - 1 - sub) + least
            new = [jnp.where(edge > k, a, b) for a, b in zip(new, old)]
        for i in range(ROWS):
            ref[f, i, pl.ds(place[q], SUB), :] = new[i]

    def product(a, b):
        return [x * y for x, y in zip(a, b)]

    def unneeded(q, k):
        return wide and min(SUB * q, BS - SUB - SUB * q) > OUT + 2 * SENT - k

    up, up_on, down, down_on = ghosts
    if wide:
        back_up, back_up_on, back_down, back_down_on = two_way_ghosts(ghosts)
    live_over, live_under = {}, {}
    for q in place if wide else ():
        live = tiles("live", q)
        live_over[q] = lanes_of(live[0], up) * up_on
        live_under[q] = lanes_of(live[3], down) * down_on
    for step in steps:
        ca, sa = times[2 * step], times[2 * step + 1]
        slope = x_slopes(lambda q: product(tiles("depth", q), tiles("east", q)), runs)
        dys = {}
        for q, dx in slope:
            if unneeded(q, 2 * step + 1):
                continue
            old = tiles("level", q)
            t0, t1, live = tiles("tide0", q), tiles("tide1", q), tiles("live", q)
            part = [old[i] + (t0[i] * ca + t1[i] * sa) - dx[i] for i in range(ROWS)]
            flux = product(tiles("depth", q), tiles("north", q))
            above, below = lanes_of(flux[0], up) * up_on, lanes_of(flux[3], down) * down_on
            north = flux[1:] + [above]
            south = [below] + flux[:3]
            new = [(part[i] - (north[i] - south[i])) * live[i] for i in range(ROWS)]
            put("level", q, 2 * step + 1, new, old)
            if not wide:
                continue
            over = lanes_of(flux[1], up) - lanes_of(flux[3], back_up) * back_up_on
            over = (lanes_of(part[0], up) - over) * live_over[q]
            under = lanes_of(flux[0], back_down) * back_down_on - lanes_of(flux[2], down)
            under = (lanes_of(part[3], down) - under) * live_under[q]
            dys[q] = [new[1] - under, new[2] - new[0], new[3] - new[1], over - new[2]]
        slope = x_slopes(lambda q: tiles("level", q), runs)
        for q, dx in slope:
            if unneeded(q, 2 * step + 2):
                continue
            u, w, cor, live = (tiles(n, q) for n in ("east", "north", "cor", "live"))
            dy = dys[q] if wide else y_slopes(tiles("level", q), ghosts)
            new = [new_velocity(u[i], w[i], cor[i], dx[i], dy[i], live[i]) for i in range(ROWS)]
            put("east", q, 2 * step + 2, [a for a, _ in new], u)
            put("north", q, 2 * step + 2, [b for _, b in new], w)


ALL = tuple(range(GROUPS))
SIDES = (ALL[:2], ALL[-2:])
NEAR = SIDES[0] + SIDES[1]
EDGE, INNER = 2 * HALF, BS - 2 * HALF


def parted(q):
    low = tile_iota(0) < HALF - SUB
    edge = [q[0], jnp.where(low, q[1], q[-2]), q[-1]]
    return edge, list(q[2:-2]) + [jnp.where(low, q[-2], q[1])]


def joint(edge, inner):
    low = tile_iota(0) < HALF - SUB
    second, last_but_one = jnp.where(low, edge[1], inner[-1]), jnp.where(low, inner[-1], edge[1])
    return [edge[0], second] + inner[:-1] + [last_but_one, edge[2]]


def started(pairs, sems):
    loads = [pltpu.make_async_copy(src, dst, sems.at[i]) for i, (src, dst) in enumerate(pairs)]
    for load in loads:
        load.start()
    return loads


def turn(groups, source, put):
    tiles = BS * BS // LANES
    for i, columns in enumerate(to_columns([source(v) for v in range(tiles)])):
        for n, q in enumerate(groups):
            put((i, pl.ds(SUB * n, SUB)), columns[SUB * q : SUB * q + SUB])


def storing(ref, f):
    def put(at, x):
        ref[f, at[0], at[1], :] = x

    return put


def turn_tide(groups, tide, tides):
    for f in range(2):
        turn(groups, lambda v, f=f: lane_tile(tide, v, (f,)), storing(tides, f))


def turn_cor(groups, cor, out):
    turn(groups, lambda v: F32(0.3) * lane_tile(cor, v), storing(out, 0))


def turn_rest(groups, tide, cor, rest):
    turn_tide(groups, tide, rest.at[pl.ds(1, 2)])
    turn_cor(groups, cor, rest.at[pl.ds(0, 1)])


def turn_land(groups, held, row, level_id, wet, land):
    none = LANES - 1
    held, row = held[...] > 0, row[...]

    def coded(v):
        here = jnp.logical_and(lane_tile(wet, v) > 0, held)
        return jnp.where(here, lane_tile(level_id, v), none)

    def put(at, code):
        land[0, at[0], at[1], :] = lanes_of(row, code)
        land[1, at[0], at[1], :] = (code < none).astype(F32)

    turn(groups, coded, put)


def turn_state(groups, start, land, state):
    def storing_live(f):
        def put(at, x):
            state[f, at[0], at[1], :] = x * land[1, at[0], at[1], :]

        return put

    for f in range(3):
        turn(groups, lambda v, f=f: lane_tile(start, v, (0, f)), storing_live(f))


def clock_kernel(slices, times):
    for step in range(STEPS):
        for j, x in enumerate(phase(slices, step)):
            times[2 * step + j] = jnp.full((SUB, LANES), x, F32)


def depths_kernel(table, row):
    levels = table.shape[0]
    depths = F32(0.15) * table[...].reshape(1, levels)
    depths = jnp.concatenate([depths, jnp.zeros((1, LANES - levels), F32)], axis=1)
    row[...] = jnp.broadcast_to(depths, (SUB, LANES))


def slots_kernel(count_ref, nb, face, held):
    for j, x in enumerate(face_rows(nb[...])):
        face[j] = x
    held[...] = (tile_iota(0) < count_ref[0]).astype(jnp.int32)


def still_kernel(held, row, level_id, wet, cor, land, turned):
    turn_land(NEAR, held, row, level_id, wet, land)
    turn_cor(NEAR, cor, turned)


def before_kernel(times, face, start, tide, land, cor, pe, pw, state, tides):
    turn_state(NEAR, start, land, state)
    turn_tide(NEAR, tide, tides)
    rows = [face[j] for j in range(4)]
    s = fields_of(state, land, tides)
    s.update(cor=(cor, 0), tide0=(tides, 0), tide1=(tides, 1))
    interior_steps(s, SIDES, times, range(SENT), chunk_ghosts(rows[0], rows[1]), True)

    end = SUB * len(NEAR)
    for f, name in enumerate(NAMES):
        ref, at = s[name]
        for i in range(ROWS):
            pe[i, pl.ds(OUT * f, OUT), :] = ref[at, i, pl.ds(end - OUT, OUT), :]
            pw[i, pl.ds(OUT * f, OUT), :] = ref[at, i, pl.ds(0, OUT), :]
    for i in range(ROWS):
        pe[i, pl.ds(6 * OUT, 1), :] = state[0, i, pl.ds(end - OUT - 1, 1), :]
        pw[i, pl.ds(6 * OUT + OUT - 1, 1), :] = state[0, i, pl.ds(OUT, 1), :]
        entry = rows[i][:1].astype(F32)
        pe[i, pl.ds(7 * OUT, 1), :] = entry
        pw[i, pl.ds(7 * OUT + OUT - 1, 1), :] = entry


def power(x, n):
    return functools.reduce(lambda a, b: a * b, [x] * n)


def part_tile(ref, f, i, n):
    return ref[f, i, pl.ds(SUB * n, SUB), :]


def during_kernel(
    times, face, held, row, level_id, wet, start, tide, cor, gain_h,
    last, land, rest, inner, inner_gain, edge_gain, edge_base,
    gain, sems,
):
    loads = started([(gain_h, gain)], sems)
    tiles = wet.shape[1] // LANES
    turn_land(ALL, held, row, level_id, wet, land)
    turn_state(ALL, start, land, last)
    turn_rest(ALL, tide, cor, rest)
    ghosts = chunk_ghosts(face[0], face[1])
    interior_steps(fields_of(last, land, rest), (ALL,), times, range(STEPS), ghosts, False)
    held = held[...].astype(F32)
    for load in loads:
        load.wait()

    def store(ref, f, i, parts):
        for n, x in enumerate(parts):
            ref[f, i, pl.ds(SUB * n, SUB), :] = x

    for f in range(3):
        gains = [lane_tile(gain, v, (f,)) for v in range(tiles)]
        base = [
            gains[v] * (lane_tile(start, v, (0, f)) * (lane_tile(wet, v).astype(F32) * held))
            for v in range(tiles)
        ]
        gains, base = to_columns(gains), to_columns(base)
        for i in range(ROWS):
            gain_parts, base_parts, last_parts = (
                parted([x[SUB * q : SUB * q + SUB] for q in ALL])
                for x in (gains[i], base[i], last[f, i])
            )
            store(edge_gain, f, i, gain_parts[0])
            store(inner_gain, f, i, gain_parts[1])
            store(edge_base, f, i, base_parts[0])
            store(inner, f, i, [x - y for x, y in zip(last_parts[1], base_parts[1])])


def after_kernel(times, pe, pw, last, land, rest, face, base, edge, joined):
    sub, lane = tile_iota(0), tile_iota(1)
    s = fields_of(last, land, rest)

    for f, name in enumerate(NAMES):
        ref, at = s[name]
        for i in range(ROWS):
            joined[f, i, 0, pl.ds(0, OUT), :] = pe[i, pl.ds(OUT * f, OUT), :]
            joined[f, i, 0, pl.ds(OUT, 2), :] = ref[at, i, pl.ds(0, 2), :]
            joined[f, i, 1, pl.ds(0, 2), :] = ref[at, i, pl.ds(BS - 2, 2), :]
            joined[f, i, 1, pl.ds(2, OUT), :] = pw[i, pl.ds(OUT * f, OUT), :]

    def load(name, side, g):
        f = NAMES.index(name)
        if g == 0:
            return [joined[f, i, side] for i in range(ROWS)]
        ref, at = s[name]
        low = SUB * g - OUT
        low = low if side == 0 else BS - SUB - low
        return [ref[at, i, pl.ds(low, SUB), :] for i in range(ROWS)]

    own = [face[j] for j in range(4)]
    ghosts, joins, far = [], [], []
    for side in range(2):
        row = 0 if side == 0 else SUB - 1
        sent = [
            jnp.broadcast_to(joined[7, j, side, pl.ds(row, 1), :].astype(jnp.int32), (SUB, LANES))
            for j in range(4)
        ]
        outer = sub < OUT if side == 0 else sub >= 2
        mixed = [jnp.where(outer, sent[j], own[j]) for j in range(4)]
        here = chunk_ghosts(own[0], own[1])
        ghosts.append([chunk_ghosts(mixed[0], mixed[1]), here, here])
        to = jnp.where(outer, own[3 - side], sent[2 + side])
        joins.append((lane - lane % SUB + jnp.maximum(to, 0), (to >= 0).astype(F32)))
    inner_row = (OUT, 1)
    outer_row = (OUT - 1, 2)

    def x_side(side, t, beyond=None):
        index, on = joins[side]
        looked = [lanes_of(x, index) * on for x in t[0]]
        inner = [jnp.where(sub == inner_row[side], b, a) for a, b in zip(t[0], looked)]
        outer = [jnp.where(sub == outer_row[side], b, a) for a, b in zip(t[0], looked)]
        sign = -1 if side == 0 else 1
        end_in, end_out = (SUB - 1, 0) if side == 0 else (0, SUB - 1)
        inward = [[shifted(x, sign) for x in inner]]
        outward = [[shifted(x, -sign) for x in outer]]
        if beyond is not None:
            outward[0] = [jnp.where(sub == end_out, b, a) for a, b in zip(outward[0], beyond)]
        plain_out = [[shifted(x, -sign) for x in t[0]]]
        for g in range(1, len(t)):
            inward.append([shifted(x, sign) for x in t[g]])
            plain_out.append([shifted(x, -sign) for x in t[g]])
        for g in range(1, len(t)):
            outward.append(
                [jnp.where(sub == end_out, b, a) for a, b in zip(plain_out[g], plain_out[g - 1])]
            )
        for g in range(len(t) - 1):
            inward[g] = [
                jnp.where(sub == end_in, b, a) for a, b in zip(inward[g], inward[g + 1])
            ]
        return [
            [(a - b) if side == 0 else (b - a) for a, b in zip(inward[g], outward[g])]
            for g in range(len(t))
        ]

    def changed(side, g, k):
        place = sub if side == 0 else SUB - 1 - sub
        if g == 0:
            reach = min(k, HALF - k)
            mask = place >= OUT - reach
            return mask if k >= 2 else jnp.logical_and(mask, place <= OUT)
        least = SUB * g - OUT + 1
        if k < least:
            return False
        return None if k >= least + SUB - 1 else place + least <= k

    cells = {
        (n, side, g): load(n, side, g)
        for n in ("level", "east", "north") for side in range(2) for g in range(3)
    }

    def put(name, side, g, mask, new):
        key = (name, side, g)
        if mask is not None:
            new = [jnp.where(mask, a, b) for a, b in zip(new, cells[key])]
        cells[key] = new

    def product(a, b):
        return [x * y for x, y in zip(a, b)]

    for k in range(1, HALF + 1):
        ca, sa = times[(k - 1) // 2 * 2], times[(k - 1) // 2 * 2 + 1]
        active = [g for g in range(3) if changed(0, g, k) is not False]
        reach = min(3, len(active) + 1)
        for side in range(2):
            if k % 2 == 1:
                depth = [load("depth", side, g) for g in range(reach)]
                dx = x_side(
                    side, [product(depth[g], cells["east", side, g]) for g in range(reach)]
                )
                for g in active:
                    flux = product(depth[g], cells["north", side, g])
                    dy = y_slopes(flux, ghosts[side][g])
                    t0, t1, live = (load(n, side, g) for n in ("tide0", "tide1", "live"))
                    old = cells["level", side, g]
                    new = [
                        new_level(old[i], t0[i], t1[i], ca, sa, dx[g][i], dy[i], live[i])
                        for i in range(ROWS)
                    ]
                    put("level", side, g, changed(side, g, k), new)
            else:
                beyond = load("tide0", side, 0) if k == OUT else None
                dx = x_side(side, [cells["level", side, g] for g in range(reach)], beyond)
                for g in active:
                    dy = y_slopes(cells["level", side, g], ghosts[side][g])
                    cor, live = load("cor", side, g), load("live", side, g)
                    u, w = cells["east", side, g], cells["north", side, g]
                    new = [
                        new_velocity(u[i], w[i], cor[i], dx[g][i], dy[i], live[i])
                        for i in range(ROWS)
                    ]
                    mask = changed(side, g, k)
                    put("east", side, g, mask, [a for a, _ in new])
                    put("north", side, g, mask, [b for _, b in new])

    for f, name in enumerate(NAMES[:3]):
        for i in range(ROWS):
            a, b, c = (shifted(cells[name, 0, g][i], 2) for g in range(3))
            d, e, h = (shifted(cells[name, 1, g][i], -2) for g in range(3))
            second, last_but_one = jnp.where(sub < 2, b, c), jnp.where(sub >= 6, e, h)
            fine = [
                jnp.where(sub < 2, a, b),
                jnp.where(sub < HALF - SUB, second, last_but_one),
                jnp.where(sub >= 6, d, e),
            ]
            for n, x in enumerate(fine):
                edge[f, i, pl.ds(SUB * n, SUB), :] = x - part_tile(base, f, i, n)


def final_kernel(
    slices, edge_sum, edge, edge_gain, inner_sum, inner, inner_gain, result, out, sems
):
    parts = ((edge_sum, edge, edge_gain), (inner_sum, inner, inner_gain))
    copies = []
    for f in range(3):
        columns = []
        for i in range(ROWS):
            done = []
            for total, own, gain in parts:
                done.append([])
                for n in range(gain.shape[2] // SUB):
                    g = part_tile(gain, f, i, n)
                    most = power(g, slices - 1)
                    whole = part_tile(total, f, i, n) + most * part_tile(own, f, i, n)
                    done[-1].append(whole / (F32(1) - most * g))
            q = joint(*done)
            columns.append(jnp.concatenate(q, axis=0))
        for v, x in enumerate(to_tiles(columns)):
            out[0, f, :, pl.ds(v * LANES, LANES)] = x
        copies.append(pltpu.make_async_copy(out.at[0, f], result.at[0, f], sems.at[f]))
        copies[-1].start()
    for copy in copies:
        copy.wait()


def call(kernel, out_shape, operands, spaces=None, out_space=pltpu.VMEM, scratch=(), flops=0):
    spaces = spaces or [pltpu.VMEM] * len(operands)
    size = 2 * sum(4 * x.size for x in operands)
    return pl.pallas_call(
        kernel,
        out_shape=out_shape,
        in_specs=[pl.BlockSpec(memory_space=space) for space in spaces],
        out_specs=jax.tree.map(lambda _: pl.BlockSpec(memory_space=out_space), out_shape),
        scratch_shapes=scratch,
        cost_estimate=pl.CostEstimate(flops=flops, bytes_accessed=size, transcendentals=0),
        compiler_params=pltpu.CompilerParams(vmem_limit_bytes=VMEM_LIMIT),
    )(*operands)


def shape(*dims):
    return jax.ShapeDtypeStruct(dims, F32)


def in_hbm(arrays):
    return [pltpu.with_memory_space_constraint(x, pltpu.HBM) for x in arrays]


def passed_along(shard, axis, by):
    size = lax.axis_size(axis)
    return lax.ppermute(shard, axis, [(i, (i + by) % size) for i in range(size)])


def periodic_sum(defect, gain, slices):
    total = passed_along(defect, "tm", 1)
    for _ in range(slices - 2):
        total = passed_along(defect + gain * total, "tm", 1)
    return total


def body(
    start_states, coarse_gain, depth_level, depth_table, wet, block_count, neighbour, coriolis, tide
):
    slices = lax.axis_size("tm")

    def columns(fields, size):
        return shape(fields, ROWS, size, LANES)

    times = call(
        functools.partial(clock_kernel, slices), shape(2 * STEPS, SUB, LANES), [], flops=10**10
    )
    flags = jax.ShapeDtypeStruct((SUB, LANES), jnp.int32)
    row = call(depths_kernel, shape(SUB, LANES), [depth_table])
    slot_tiles = call(
        slots_kernel,
        [jax.ShapeDtypeStruct((4, SUB, LANES), jnp.int32), flags],
        [block_count, neighbour.T],
        spaces=[pltpu.SMEM, pltpu.VMEM],
    )
    face, held = slot_tiles
    ready = [times, face, held, row, depth_level, wet, start_states, tide, coriolis]
    near = SUB * len(NEAR)
    land, cor = call(
        still_kernel,
        [columns(2, near), columns(1, near)],
        [held, row, depth_level, wet, coriolis],
    )
    pe, pw = call(
        before_kernel,
        [shape(ROWS, len(NAMES) * OUT, LANES)] * 2,
        [times, face, start_states, tide, land, cor],
        scratch=[pltpu.VMEM(columns(n, near).shape, F32) for n in (3, 2)],
    )
    from_west = passed_along(pe, "space", 1)
    from_east = passed_along(pw, "space", -1)
    last, land, rest, inner, inner_gain, edge_gain, edge_base = call(
        during_kernel,
        [columns(3, BS), columns(2, BS), columns(3, BS)]
        + [columns(3, INNER)] * 2
        + [columns(3, EDGE)] * 2,
        ready + in_hbm([coarse_gain]),
        spaces=[pltpu.VMEM] * len(ready) + [pltpu.HBM],
        scratch=[pltpu.VMEM(coarse_gain.shape, F32), pltpu.SemaphoreType.DMA((1,))],
    )
    inner_sum = periodic_sum(inner, inner_gain, slices)
    edge = call(
        after_kernel,
        columns(3, EDGE),
        [times, from_west, from_east, last, land, rest, face, edge_base],
        scratch=[pltpu.VMEM((len(NAMES), ROWS, 2, SUB, LANES), F32)],
    )
    edge_sum = periodic_sum(edge, edge_gain, slices)
    return call(
        functools.partial(final_kernel, slices),
        shape(*start_states.shape),
        [edge_sum, edge, edge_gain, inner_sum, inner, inner_gain],
        out_space=pltpu.HBM,
        scratch=[pltpu.VMEM(start_states.shape, F32), pltpu.SemaphoreType.DMA((3,))],
    )


def solution(mesh):
    return jax.shard_map(
        body,
        mesh=mesh,
        in_specs=(
            P("tm", None, "space", None),
            P(None, "space", None),
            P("space", None),
            P(),
            P("space", None),
            P("space"),
            P("space", None),
            P("space", None),
            P(None, "space", None),
        ),
        out_specs=P("tm", None, "space", None),
        check_vma=False,
    )
```

```python
import functools
import math

import jax
import jax.numpy as jnp
from jax import lax
from jax.experimental import pallas as pl
from jax.experimental.pallas import tpu as pltpu
from jax.sharding import PartitionSpec as P

BS = 64
STEPS = 6
HALF = 2 * STEPS
SENT = STEPS // 2
OUT = STEPS
LANES = 128
SUB = 8
ROWS = 4
GROUPS = BS // SUB
F32 = jnp.float32
VMEM_LIMIT = 24 * 1024 * 1024


def shifted(x, by):
    return pltpu.roll(x, by % SUB, 0)


def lanes_of(x, index):
    return jnp.take_along_axis(x, index, axis=1, mode="promise_in_bounds")


def tile_iota(dim):
    return lax.broadcasted_iota(jnp.int32, (SUB, LANES), dim)


def lane_tile(ref, v, lead=()):
    return ref[tuple(lead) + (slice(None), pl.ds(v * LANES, LANES))]


def to_columns(tiles):
    out = []
    for part in (tiles[0::2], tiles[1::2]):
        turned = jnp.concatenate(part, axis=0).T
        out += [turned[:BS], turned[BS:]]
    return out


def to_tiles(columns):
    out = {}
    for part in range(2):
        turned = jnp.concatenate(columns[2 * part : 2 * part + 2], axis=0).T
        for c in range(LANES // SUB):
            out[2 * c + part] = turned[SUB * c : SUB * c + SUB]
    return [out[v] for v in range(len(out))]


def phase(count, step):
    omega = 2.0 * math.pi / (count * STEPS)
    here = lax.axis_index("tm")
    ca, sa = F32(0), F32(0)
    for n in range(count):
        angle = (n * STEPS + step) * omega
        ca = jnp.where(here == n, F32(0.3 * math.cos(angle)), ca)
        sa = jnp.where(here == n, F32(0.3 * math.sin(angle)), sa)
    return ca, sa


def chunk_ghosts(north, south):
    lane = tile_iota(1)
    top, bottom = lane >= LANES - SUB, lane < SUB
    up = jnp.where(top, jnp.maximum(north, 0), (lane + SUB) % LANES)
    down = jnp.where(bottom, LANES - SUB + jnp.maximum(south, 0), (lane + LANES - SUB) % LANES)
    up_on = jnp.where(jnp.logical_and(top, north < 0), F32(0), F32(1))
    down_on = jnp.where(jnp.logical_and(bottom, south < 0), F32(0), F32(1))
    return up, up_on, down, down_on


def two_way_ghosts(ghosts):
    up, up_on, down, down_on = ghosts
    return lanes_of(down, up), lanes_of(down_on, up), lanes_of(up, down), lanes_of(up_on, down)


def face_rows(nb):
    wide = jnp.concatenate([nb] * (LANES // SUB), axis=1)
    return [jnp.broadcast_to(wide[j : j + 1], (SUB, LANES)) for j in range(4)]


def y_slopes(t, ghosts):
    up, up_on, down, down_on = ghosts
    above = lanes_of(t[0], up) * up_on
    below = lanes_of(t[3], down) * down_on
    return [t[1] - below, t[2] - t[0], t[3] - t[1], above - t[2]]


def x_slopes(columns, runs):
    sub = tile_iota(0)
    first, last = sub == 0, sub == SUB - 1
    for run in runs:
        get = [columns(q) for q in run]
        easts = [[shifted(x, -1) for x in t] for t in get]
        wests = [[shifted(x, 1) for x in t] for t in get]
        for n, q in enumerate(run):
            east, west = easts[n], wests[n]
            if n + 1 < len(run):
                east = [jnp.where(last, b, a) for a, b in zip(east, easts[n + 1])]
            if n > 0:
                west = [jnp.where(first, b, a) for a, b in zip(west, wests[n - 1])]
            yield q, [e - w for e, w in zip(east, west)]


def new_level(level, t0, t1, ca, sa, dx, dy, live):
    return (level + (t0 * ca + t1 * sa) - (dx + dy)) * live


def new_velocity(u, w, cor, dx, dy, live):
    return (
        (F32(0.985) * u + cor * w - F32(0.15) * dx) * live,
        (F32(0.985) * w - cor * u - F32(0.15) * dy) * live,
    )


NAMES = ("level", "east", "north", "depth", "live", "cor", "tide0", "tide1")


def fields_of(state, land, rest):
    refs = [(state, 0), (state, 1), (state, 2), (land, 0), (land, 1)]
    return dict(zip(NAMES, refs + [(rest, f) for f in range(3)]))


def interior_steps(s, runs, times, steps, ghosts, wide):
    sub = tile_iota(0)
    place = {q: SUB * n for n, q in enumerate(q for run in runs for q in run)}

    def tiles(name, q):
        ref, f = s[name]
        return [ref[f, i, pl.ds(place[q], SUB), :] for i in range(ROWS)]

    def put(name, q, k, new, old):
        ref, f = s[name]
        least = min(SUB * q, BS - SUB - SUB * q) + 1
        if k >= least + SUB - 1:
            return
        if k >= least:
            edge = (sub if q < GROUPS // 2 else SUB - 1 - sub) + least
            new = [jnp.where(edge > k, a, b) for a, b in zip(new, old)]
        for i in range(ROWS):
            ref[f, i, pl.ds(place[q], SUB), :] = new[i]

    def product(a, b):
        return [x * y for x, y in zip(a, b)]

    def unneeded(q, k):
        return wide and min(SUB * q, BS - SUB - SUB * q) > OUT + 2 * SENT - k

    up, up_on, down, down_on = ghosts
    if wide:
        back_up, back_up_on, back_down, back_down_on = two_way_ghosts(ghosts)
    live_over, live_under = {}, {}
    for q in place if wide else ():
        live = tiles("live", q)
        live_over[q] = lanes_of(live[0], up) * up_on
        live_under[q] = lanes_of(live[3], down) * down_on
    for step in steps:
        ca, sa = times[2 * step], times[2 * step + 1]
        slope = x_slopes(lambda q: product(tiles("depth", q), tiles("east", q)), runs)
        dys = {}
        for q, dx in slope:
            if unneeded(q, 2 * step + 1):
                continue
            old = tiles("level", q)
            t0, t1, live = tiles("tide0", q), tiles("tide1", q), tiles("live", q)
            part = [old[i] + (t0[i] * ca + t1[i] * sa) - dx[i] for i in range(ROWS)]
            flux = product(tiles("depth", q), tiles("north", q))
            above, below = lanes_of(flux[0], up) * up_on, lanes_of(flux[3], down) * down_on
            north = flux[1:] + [above]
            south = [below] + flux[:3]
            new = [(part[i] - (north[i] - south[i])) * live[i] for i in range(ROWS)]
            put("level", q, 2 * step + 1, new, old)
            if not wide:
                continue
            over = lanes_of(flux[1], up) - lanes_of(flux[3], back_up) * back_up_on
            over = (lanes_of(part[0], up) - over) * live_over[q]
            under = lanes_of(flux[0], back_down) * back_down_on - lanes_of(flux[2], down)
            under = (lanes_of(part[3], down) - under) * live_under[q]
            dys[q] = [new[1] - under, new[2] - new[0], new[3] - new[1], over - new[2]]
        slope = x_slopes(lambda q: tiles("level", q), runs)
        for q, dx in slope:
            if unneeded(q, 2 * step + 2):
                continue
            u, w, cor, live = (tiles(n, q) for n in ("east", "north", "cor", "live"))
            dy = dys[q] if wide else y_slopes(tiles("level", q), ghosts)
            new = [new_velocity(u[i], w[i], cor[i], dx[i], dy[i], live[i]) for i in range(ROWS)]
            put("east", q, 2 * step + 2, [a for a, _ in new], u)
            put("north", q, 2 * step + 2, [b for _, b in new], w)


ALL = tuple(range(GROUPS))
SIDES = (ALL[:2], ALL[-2:])
NEAR = SIDES[0] + SIDES[1]
EDGE, INNER = 2 * HALF, BS - 2 * HALF


def parted(q):
    low = tile_iota(0) < HALF - SUB
    edge = [q[0], jnp.where(low, q[1], q[-2]), q[-1]]
    return edge, list(q[2:-2]) + [jnp.where(low, q[-2], q[1])]


def joint(edge, inner):
    low = tile_iota(0) < HALF - SUB
    second, last_but_one = jnp.where(low, edge[1], inner[-1]), jnp.where(low, inner[-1], edge[1])
    return [edge[0], second] + inner[:-1] + [last_but_one, edge[2]]


def started(pairs, sems):
    loads = [pltpu.make_async_copy(src, dst, sems.at[i]) for i, (src, dst) in enumerate(pairs)]
    for load in loads:
        load.start()
    return loads


def turn(groups, source, put):
    tiles = BS * BS // LANES
    for i, columns in enumerate(to_columns([source(v) for v in range(tiles)])):
        for n, q in enumerate(groups):
            put((i, pl.ds(SUB * n, SUB)), columns[SUB * q : SUB * q + SUB])


def storing(ref, f):
    def put(at, x):
        ref[f, at[0], at[1], :] = x

    return put


def turn_tide(groups, tide, tides):
    for f in range(2):
        turn(groups, lambda v, f=f: lane_tile(tide, v, (f,)), storing(tides, f))


def turn_cor(groups, cor, out):
    turn(groups, lambda v: F32(0.3) * lane_tile(cor, v), storing(out, 0))


def turn_rest(groups, tide, cor, rest):
    turn_tide(groups, tide, rest.at[pl.ds(1, 2)])
    turn_cor(groups, cor, rest.at[pl.ds(0, 1)])


def turn_land(groups, held, row, level_id, wet, land):
    none = LANES - 1
    held, row = held[...] > 0, row[...]

    def coded(v):
        here = jnp.logical_and(lane_tile(wet, v) > 0, held)
        return jnp.where(here, lane_tile(level_id, v), none)

    def put(at, code):
        land[0, at[0], at[1], :] = lanes_of(row, code)
        land[1, at[0], at[1], :] = (code < none).astype(F32)

    turn(groups, coded, put)


def turn_state(groups, start, land, state):
    def storing_live(f):
        def put(at, x):
            state[f, at[0], at[1], :] = x * land[1, at[0], at[1], :]

        return put

    for f in range(3):
        turn(groups, lambda v, f=f: lane_tile(start, v, (0, f)), storing_live(f))


def clock_kernel(slices, times):
    for step in range(STEPS):
        for j, x in enumerate(phase(slices, step)):
            times[2 * step + j] = jnp.full((SUB, LANES), x, F32)


def depths_kernel(table, row):
    levels = table.shape[0]
    depths = F32(0.15) * table[...].reshape(1, levels)
    depths = jnp.concatenate([depths, jnp.zeros((1, LANES - levels), F32)], axis=1)
    row[...] = jnp.broadcast_to(depths, (SUB, LANES))


def slots_kernel(count_ref, nb, face, held):
    for j, x in enumerate(face_rows(nb[...])):
        face[j] = x
    held[...] = (tile_iota(0) < count_ref[0]).astype(jnp.int32)


def still_kernel(held, row, level_id, wet, cor, land, turned):
    turn_land(NEAR, held, row, level_id, wet, land)
    turn_cor(NEAR, cor, turned)


def before_kernel(times, face, start, tide, land, cor, pe, pw, state, tides):
    turn_state(NEAR, start, land, state)
    turn_tide(NEAR, tide, tides)
    rows = [face[j] for j in range(4)]
    s = fields_of(state, land, tides)
    s.update(cor=(cor, 0), tide0=(tides, 0), tide1=(tides, 1))
    interior_steps(s, SIDES, times, range(SENT), chunk_ghosts(rows[0], rows[1]), True)

    end = SUB * len(NEAR)
    for f, name in enumerate(NAMES):
        ref, at = s[name]
        for i in range(ROWS):
            pe[i, pl.ds(OUT * f, OUT), :] = ref[at, i, pl.ds(end - OUT, OUT), :]
            pw[i, pl.ds(OUT * f, OUT), :] = ref[at, i, pl.ds(0, OUT), :]
    for i in range(ROWS):
        pe[i, pl.ds(6 * OUT, 1), :] = state[0, i, pl.ds(end - OUT - 1, 1), :]
        pw[i, pl.ds(6 * OUT + OUT - 1, 1), :] = state[0, i, pl.ds(OUT, 1), :]
        entry = rows[i][:1].astype(F32)
        pe[i, pl.ds(7 * OUT, 1), :] = entry
        pw[i, pl.ds(7 * OUT + OUT - 1, 1), :] = entry


def power(x, n):
    return functools.reduce(lambda a, b: a * b, [x] * n)


def part_tile(ref, f, i, n):
    return ref[f, i, pl.ds(SUB * n, SUB), :]


def during_kernel(
    times, face, held, row, level_id, wet, start, tide, cor, gain_h,
    last, land, rest, inner, inner_gain, edge_gain, edge_base,
    gain, sems,
):
    loads = started([(gain_h, gain)], sems)
    tiles = wet.shape[1] // LANES
    turn_land(ALL, held, row, level_id, wet, land)
    turn_state(ALL, start, land, last)
    turn_rest(ALL, tide, cor, rest)
    ghosts = chunk_ghosts(face[0], face[1])
    interior_steps(fields_of(last, land, rest), (ALL,), times, range(STEPS), ghosts, False)
    held = held[...].astype(F32)
    for load in loads:
        load.wait()

    def store(ref, f, i, parts):
        for n, x in enumerate(parts):
            ref[f, i, pl.ds(SUB * n, SUB), :] = x

    for f in range(3):
        gains = [lane_tile(gain, v, (f,)) for v in range(tiles)]
        base = [
            gains[v] * (lane_tile(start, v, (0, f)) * (lane_tile(wet, v).astype(F32) * held))
            for v in range(tiles)
        ]
        gains, base = to_columns(gains), to_columns(base)
        for i in range(ROWS):
            gain_parts, base_parts, last_parts = (
                parted([x[SUB * q : SUB * q + SUB] for q in ALL])
                for x in (gains[i], base[i], last[f, i])
            )
            store(edge_gain, f, i, gain_parts[0])
            store(inner_gain, f, i, gain_parts[1])
            store(edge_base, f, i, base_parts[0])
            store(inner, f, i, [x - y for x, y in zip(last_parts[1], base_parts[1])])


def after_kernel(times, pe, pw, last, land, rest, face, base, edge, joined):
    sub, lane = tile_iota(0), tile_iota(1)
    s = fields_of(last, land, rest)

    for f, name in enumerate(NAMES):
        ref, at = s[name]
        for i in range(ROWS):
            joined[f, i, 0, pl.ds(0, OUT), :] = pe[i, pl.ds(OUT * f, OUT), :]
            joined[f, i, 0, pl.ds(OUT, 2), :] = ref[at, i, pl.ds(0, 2), :]
            joined[f, i, 1, pl.ds(0, 2), :] = ref[at, i, pl.ds(BS - 2, 2), :]
            joined[f, i, 1, pl.ds(2, OUT), :] = pw[i, pl.ds(OUT * f, OUT), :]

    def load(name, side, g):
        f = NAMES.index(name)
        if g == 0:
            return [joined[f, i, side] for i in range(ROWS)]
        ref, at = s[name]
        low = SUB * g - OUT
        low = low if side == 0 else BS - SUB - low
        return [ref[at, i, pl.ds(low, SUB), :] for i in range(ROWS)]

    own = [face[j] for j in range(4)]
    ghosts, joins, far = [], [], []
    for side in range(2):
        row = 0 if side == 0 else SUB - 1
        sent = [
            jnp.broadcast_to(joined[7, j, side, pl.ds(row, 1), :].astype(jnp.int32), (SUB, LANES))
            for j in range(4)
        ]
        outer = sub < OUT if side == 0 else sub >= 2
        mixed = [jnp.where(outer, sent[j], own[j]) for j in range(4)]
        here = chunk_ghosts(own[0], own[1])
        ghosts.append([chunk_ghosts(mixed[0], mixed[1]), here, here])
        to = jnp.where(outer, own[3 - side], sent[2 + side])
        joins.append((lane - lane % SUB + jnp.maximum(to, 0), (to >= 0).astype(F32)))
    inner_row = (OUT, 1)
    outer_row = (OUT - 1, 2)

    def x_side(side, t, beyond=None):
        index, on = joins[side]
        looked = [lanes_of(x, index) * on for x in t[0]]
        inner = [jnp.where(sub == inner_row[side], b, a) for a, b in zip(t[0], looked)]
        outer = [jnp.where(sub == outer_row[side], b, a) for a, b in zip(t[0], looked)]
        sign = -1 if side == 0 else 1
        end_in, end_out = (SUB - 1, 0) if side == 0 else (0, SUB - 1)
        inward = [[shifted(x, sign) for x in inner]]
        outward = [[shifted(x, -sign) for x in outer]]
        if beyond is not None:
            outward[0] = [jnp.where(sub == end_out, b, a) for a, b in zip(outward[0], beyond)]
        plain_out = [[shifted(x, -sign) for x in t[0]]]
        for g in range(1, len(t)):
            inward.append([shifted(x, sign) for x in t[g]])
            plain_out.append([shifted(x, -sign) for x in t[g]])
        for g in range(1, len(t)):
            outward.append(
                [jnp.where(sub == end_out, b, a) for a, b in zip(plain_out[g], plain_out[g - 1])]
            )
        for g in range(len(t) - 1):
            inward[g] = [
                jnp.where(sub == end_in, b, a) for a, b in zip(inward[g], inward[g + 1])
            ]
        return [
            [(a - b) if side == 0 else (b - a) for a, b in zip(inward[g], outward[g])]
            for g in range(len(t))
        ]

    def changed(side, g, k):
        place = sub if side == 0 else SUB - 1 - sub
        if g == 0:
            reach = min(k, HALF - k)
            mask = place >= OUT - reach
            return mask if k >= 2 else jnp.logical_and(mask, place <= OUT)
        least = SUB * g - OUT + 1
        if k < least:
            return False
        return None if k >= least + SUB - 1 else place + least <= k

    cells = {
        (n, side, g): load(n, side, g)
        for n in ("level", "east", "north") for side in range(2) for g in range(3)
    }

    def put(name, side, g, mask, new):
        key = (name, side, g)
        if mask is not None:
            new = [jnp.where(mask, a, b) for a, b in zip(new, cells[key])]
        cells[key] = new

    def product(a, b):
        return [x * y for x, y in zip(a, b)]

    for k in range(1, HALF + 1):
        ca, sa = times[(k - 1) // 2 * 2], times[(k - 1) // 2 * 2 + 1]
        active = [g for g in range(3) if changed(0, g, k) is not False]
        reach = min(3, len(active) + 1)
        for side in range(2):
            if k % 2 == 1:
                depth = [load("depth", side, g) for g in range(reach)]
                dx = x_side(
                    side, [product(depth[g], cells["east", side, g]) for g in range(reach)]
                )
                for g in active:
                    flux = product(depth[g], cells["north", side, g])
                    dy = y_slopes(flux, ghosts[side][g])
                    t0, t1, live = (load(n, side, g) for n in ("tide0", "tide1", "live"))
                    old = cells["level", side, g]
                    new = [
                        new_level(old[i], t0[i], t1[i], ca, sa, dx[g][i], dy[i], live[i])
                        for i in range(ROWS)
                    ]
                    put("level", side, g, changed(side, g, k), new)
            else:
                beyond = load("tide0", side, 0) if k == OUT else None
                dx = x_side(side, [cells["level", side, g] for g in range(reach)], beyond)
                for g in active:
                    dy = y_slopes(cells["level", side, g], ghosts[side][g])
                    cor, live = load("cor", side, g), load("live", side, g)
                    u, w = cells["east", side, g], cells["north", side, g]
                    new = [
                        new_velocity(u[i], w[i], cor[i], dx[g][i], dy[i], live[i])
                        for i in range(ROWS)
                    ]
                    mask = changed(side, g, k)
                    put("east", side, g, mask, [a for a, _ in new])
                    put("north", side, g, mask, [b for _, b in new])

    for f, name in enumerate(NAMES[:3]):
        for i in range(ROWS):
            a, b, c = (shifted(cells[name, 0, g][i], 2) for g in range(3))
            d, e, h = (shifted(cells[name, 1, g][i], -2) for g in range(3))
            second, last_but_one = jnp.where(sub < 2, b, c), jnp.where(sub >= 6, e, h)
            fine = [
                jnp.where(sub < 2, a, b),
                jnp.where(sub < HALF - SUB, second, last_but_one),
                jnp.where(sub >= 6, d, e),
            ]
            for n, x in enumerate(fine):
                edge[f, i, pl.ds(SUB * n, SUB), :] = x - part_tile(base, f, i, n)


def final_kernel(
    slices, edge_sum, edge, edge_gain, inner_sum, inner, inner_gain, result, out, sems
):
    parts = ((edge_sum, edge, edge_gain), (inner_sum, inner, inner_gain))
    copies = []
    for f in range(3):
        columns = []
        for i in range(ROWS):
            done = []
            for total, own, gain in parts:
                done.append([])
                for n in range(gain.shape[2] // SUB):
                    g = part_tile(gain, f, i, n)
                    most = power(g, slices - 1)
                    whole = part_tile(total, f, i, n) + most * part_tile(own, f, i, n)
                    done[-1].append(whole / (F32(1) - most * g))
            q = joint(*done)
            columns.append(jnp.concatenate(q, axis=0))
        tiles = to_tiles(columns)
        half = len(tiles) // 2
        for n in range(2):
            for v in range(half * n, half * n + half):
                out[0, f, :, pl.ds(v * LANES, LANES)] = tiles[v]
            at = (0, f, slice(None), pl.ds(half * n * LANES, half * LANES))
            copies.append(pltpu.make_async_copy(out.at[at], result.at[at], sems.at[2 * f + n]))
            copies[-1].start()
    for copy in copies:
        copy.wait()


def call(kernel, out_shape, operands, spaces=None, out_space=pltpu.VMEM, scratch=(), flops=0):
    spaces = spaces or [pltpu.VMEM] * len(operands)
    size = 2 * sum(4 * x.size for x in operands)
    return pl.pallas_call(
        kernel,
        out_shape=out_shape,
        in_specs=[pl.BlockSpec(memory_space=space) for space in spaces],
        out_specs=jax.tree.map(lambda _: pl.BlockSpec(memory_space=out_space), out_shape),
        scratch_shapes=scratch,
        cost_estimate=pl.CostEstimate(flops=flops, bytes_accessed=size, transcendentals=0),
        compiler_params=pltpu.CompilerParams(vmem_limit_bytes=VMEM_LIMIT),
    )(*operands)


def shape(*dims):
    return jax.ShapeDtypeStruct(dims, F32)


def in_hbm(arrays):
    return [pltpu.with_memory_space_constraint(x, pltpu.HBM) for x in arrays]


def passed_along(shard, axis, by):
    size = lax.axis_size(axis)
    return lax.ppermute(shard, axis, [(i, (i + by) % size) for i in range(size)])


def periodic_sum(defect, gain, slices):
    total = passed_along(defect, "tm", 1)
    for _ in range(slices - 2):
        total = passed_along(defect + gain * total, "tm", 1)
    return total


def body(
    start_states, coarse_gain, depth_level, depth_table, wet, block_count, neighbour, coriolis, tide
):
    slices = lax.axis_size("tm")

    def columns(fields, size):
        return shape(fields, ROWS, size, LANES)

    times = call(
        functools.partial(clock_kernel, slices), shape(2 * STEPS, SUB, LANES), [], flops=10**10
    )
    flags = jax.ShapeDtypeStruct((SUB, LANES), jnp.int32)
    row = call(depths_kernel, shape(SUB, LANES), [depth_table])
    slot_tiles = call(
        slots_kernel,
        [jax.ShapeDtypeStruct((4, SUB, LANES), jnp.int32), flags],
        [block_count, neighbour.T],
        spaces=[pltpu.SMEM, pltpu.VMEM],
    )
    face, held = slot_tiles
    ready = [times, face, held, row, depth_level, wet, start_states, tide, coriolis]
    near = SUB * len(NEAR)
    land, cor = call(
        still_kernel,
        [columns(2, near), columns(1, near)],
        [held, row, depth_level, wet, coriolis],
    )
    pe, pw = call(
        before_kernel,
        [shape(ROWS, len(NAMES) * OUT, LANES)] * 2,
        [times, face, start_states, tide, land, cor],
        scratch=[pltpu.VMEM(columns(n, near).shape, F32) for n in (3, 2)],
    )
    from_west = passed_along(pe, "space", 1)
    from_east = passed_along(pw, "space", -1)
    last, land, rest, inner, inner_gain, edge_gain, edge_base = call(
        during_kernel,
        [columns(3, BS), columns(2, BS), columns(3, BS)]
        + [columns(3, INNER)] * 2
        + [columns(3, EDGE)] * 2,
        ready + in_hbm([coarse_gain]),
        spaces=[pltpu.VMEM] * len(ready) + [pltpu.HBM],
        scratch=[pltpu.VMEM(coarse_gain.shape, F32), pltpu.SemaphoreType.DMA((1,))],
    )
    inner_sum = periodic_sum(inner, inner_gain, slices)
    edge = call(
        after_kernel,
        columns(3, EDGE),
        [times, from_west, from_east, last, land, rest, face, edge_base],
        scratch=[pltpu.VMEM((len(NAMES), ROWS, 2, SUB, LANES), F32)],
    )
    edge_sum = periodic_sum(edge, edge_gain, slices)
    return call(
        functools.partial(final_kernel, slices),
        shape(*start_states.shape),
        [edge_sum, edge, edge_gain, inner_sum, inner, inner_gain],
        out_space=pltpu.HBM,
        scratch=[pltpu.VMEM(start_states.shape, F32), pltpu.SemaphoreType.DMA((6,))],
    )


def solution(mesh):
    return jax.shard_map(
        body,
        mesh=mesh,
        in_specs=(
            P("tm", None, "space", None),
            P(None, "space", None),
            P("space", None),
            P(),
            P("space", None),
            P("space"),
            P("space", None),
            P("space", None),
            P(None, "space", None),
        ),
        out_specs=P("tm", None, "space", None),
        check_vma=False,
    )
```
